512 devices in a mesh: grp: 16 (over z_hi, x), dev: 32 (over y, z_lo, core).
Axes of the slice: x: 4, y: 4, z: 16 (z_hi: 4, z_lo: 4; z = z_hi * 4 + z_lo), core: 2. Of those that a mesh axis runs over, the one named last changes fastest.
Arguments:
- embeddings: float32 [114688, 1024], P(('grp', 'dev')), may hold values from -120 to 120
- partner: int32 [114688], P(('grp', 'dev')), may hold values from 0 to 114687, as said below
Outputs:
- loss: float32 [], replicated
- grad: float32 [114688, 1024], P(('grp', 'dev'))
The draws below stay inside these ranges and needn't reach their ends.
Inputs may be any that keep to these rules, and one draw needn't show every extreme that they name: partner[partner[i]] == i and partner[i] != i for every i, and partner[i] lies in the same aligned block of 448 rows as i.
All inputs are finite; a program needn't handle non-finite values.
Results may differ from the reference program's by a relative error of at most 0.00145.
The reference program's roundings to bfloat16 on the way (of `unit` and `weight`) count: a program that leaves them out, or rounds other values in their place, can miss the bound.
Values may be sent and summed in bfloat16 or wider, within the bound.
No kernel may reach another device: no remote copies, remote signals or barrier semaphores. Data moves between devices by JAX's collectives and lax.ppermute only.
A program may use at most 64 MiB of HBM per device.

```python
import jax
import jax.numpy as jnp
from jax import lax

EMBED_WIDTH = 1024
ROUNDS = 6
ROWS_DEV = 224
EMBED_COUNT = 114688
N_GRP = 16
N_DEV = 32


def pairing(key):
    span = 2 * ROWS_DEV
    blocks = EMBED_COUNT // span
    keys = jax.random.split(key, blocks)
    perms = jax.vmap(lambda one: jax.random.permutation(one, span))(keys).astype(jnp.int32)
    order = (perms + (jnp.arange(blocks, dtype=jnp.int32) * span)[:, None]).reshape(-1)
    paired = order.reshape(-1, 2)[:, ::-1].reshape(-1)
    partner = jnp.zeros((EMBED_COUNT,), jnp.int32).at[order].set(paired)
    pair_id = jnp.zeros((EMBED_COUNT,), jnp.int32).at[order].set(jnp.arange(EMBED_COUNT, dtype=jnp.int32) // 2)
    return (partner, pair_id)


def draw_partner(key, part):
    partner, pair_id = pairing(key)
    return partner


def draw_embeddings(key, part):
    partner, pair_id = pairing(key)
    key = jax.random.fold_in(key, 11)
    keys = jax.random.split(key, 6)
    centers = jnp.clip(jax.random.normal(keys[0], (64, EMBED_WIDTH), jnp.float32), -5.0, 5.0)
    labels = jax.random.randint(keys[1], (EMBED_COUNT // 2,), 0, 64)
    strength = jnp.exp(jax.random.uniform(keys[2], (EMBED_COUNT // 2, 1), jnp.float32, -1.0, 1.5))
    pair_noise = jnp.clip(jax.random.normal(keys[3], (EMBED_COUNT // 2, EMBED_WIDTH), jnp.float32), -5.0, 5.0)
    view_noise = jnp.clip(jax.random.normal(keys[4], (EMBED_COUNT, EMBED_WIDTH), jnp.float32), -5.0, 5.0)
    pair_base = centers[labels] * strength + pair_noise
    scale = jnp.exp(jax.random.uniform(keys[5], (EMBED_COUNT, 1), jnp.float32, -1.2, 1.1))
    return (pair_base[pair_id] + 0.7 * view_noise) * scale


def setup_inputs(seed: int = 0) -> dict:
    key_of = jax.random.split(jax.random.key(seed), 3)
    return {
        "embeddings": draw_embeddings(jax.random.fold_in(key_of[2], 71), 0),
        "partner": draw_partner(jax.random.fold_in(key_of[2], 71), 0),
    }


SOFTMAX_TEMPER = 0.1

def reference(embeddings, partner):
    norm = jnp.sqrt(lax.optimization_barrier(jnp.sum(embeddings * embeddings, axis=1, keepdims=True)) + 1e-06)
    unit32 = embeddings / norm
    unit = unit32.astype(jnp.bfloat16)
    devices = N_GRP * N_DEV
    local = jnp.arange(ROWS_DEV, dtype=jnp.int32)
    offsets = jnp.arange(-ROUNDS, ROUNDS + 1, dtype=jnp.int32)
    owner_blocks = jnp.arange(devices, dtype=jnp.int32)

    def scores(owner):
        start = owner * ROWS_DEV
        row_block = lax.dynamic_slice_in_dim(unit, start, ROWS_DEV, 0)
        sources = (owner + offsets) % devices
        column_index = (sources[:, None] * ROWS_DEV + local[None, :]).reshape(-1).astype(jnp.int32)
        column_block = unit[column_index]
        similarity_logits = jnp.dot(row_block, column_block.T, preferred_element_type=jnp.float32) / SOFTMAX_TEMPER
        self_mask = start + local
        exponential_scores = jnp.where(self_mask[:, None] == column_index[None, :], jnp.float32(0.0), jnp.exp(similarity_logits - 1.0 / SOFTMAX_TEMPER))
        partner_rows = lax.dynamic_slice_in_dim(partner, start, ROWS_DEV, 0)
        match = partner_rows[:, None] == column_index[None, :]
        return (similarity_logits, exponential_scores, match, column_block, column_index)

    def forward(owner):
        similarity_logits, exponential_scores, match, column_block, column_index = scores(owner)
        return (lax.optimization_barrier(jnp.sum(exponential_scores, axis=1)), lax.optimization_barrier(jnp.sum(jnp.where(match, similarity_logits, jnp.float32(0.0)), axis=1)))
    softmax_denominator, positive_score = lax.map(forward, owner_blocks)
    softmax_denominator = softmax_denominator.reshape(-1)
    positive_score = positive_score.reshape(-1)
    loss = jnp.mean(jnp.log(softmax_denominator) + 1.0 / SOFTMAX_TEMPER - positive_score)

    def loss_gradient_pass(owner):
        similarity_logits, exponential_scores, match, column_block, column_index = scores(owner)
        denom_rows = lax.dynamic_slice_in_dim(softmax_denominator, owner * ROWS_DEV, ROWS_DEV, 0)
        denom_cols = softmax_denominator[column_index]
        weight = (exponential_scores / denom_rows[:, None] + exponential_scores / denom_cols[None, :] - 2.0 * match.astype(jnp.float32)).astype(jnp.bfloat16)
        return jnp.dot(weight, column_block, preferred_element_type=jnp.float32)
    unit_gradient = lax.map(loss_gradient_pass, owner_blocks).reshape(EMBED_COUNT, EMBED_WIDTH) / SOFTMAX_TEMPER
    radial = lax.optimization_barrier(jnp.sum(unit32 * unit_gradient, axis=1, keepdims=True))
    grad = (unit_gradient - unit32 * radial) / norm
    return (loss, grad)
```

```python
import jax
import jax.numpy as jnp
import numpy as np
from jax import lax
from jax.experimental import pallas as pl
from jax.experimental.pallas import tpu as pltpu
from jax.sharding import Mesh
from jax.sharding import PartitionSpec as P

ROUNDS = 6
SOFTMAX_TEMPER = 0.1
AXES = ("zh", "x", "y", "zl", "core")
SHAPE = (4, 4, 4, 4, 2)
RUNS = 64
DEV_AXES = ("y", "zl", "core")
ROWS = 224
WIDTH = 1024

RECEIVED = np.array([[1, 2, 3], [3, 0, 2], [0, 3, 1], [2, 1, 0]], np.int32)


def crosses(run):
    return run % 16 == 15


def routes():
    names = ("P1", "P2", "P3a", "P3b", "Y1", "Y2", "Y3a", "Y3b", "X1", "X2", "X3", "X4", "X5", "X6")
    table = {name: [] for name in names}

    def chip(run, k):
        return (run % RUNS) * 4 + k

    def add(name, *pairs):
        for source, target in pairs:
            for core in (0, 1):
                table[name].append((2 * source + core, 2 * target + core))

    for run in range(RUNS):
        for name, moves in (
            ("P1", ((0, 2), (1, 0), (2, 3), (3, 1))),
            ("P2", ((1, 3), (2, 0), (0, 1), (3, 2))),
            ("P3a", ((2, 3), (1, 0))),
            ("P3b", ((1, 2), (2, 1))),
        ):
            add(name, *((chip(run, a), chip(run, b)) for a, b in moves))
        for name, ups, downs in (
            ("Y1", (0, 1), (2, 3)),
            ("Y2", (0, 2), (1, 3)),
            ("Y3a", (0,), (3,)),
            ("Y3b", (1,), (2,)),
        ):
            if not crosses(run):
                add(name, *((chip(run, k), chip(run + 1, k)) for k in ups))
            if not crosses(run - 1):
                add(name, *((chip(run, k), chip(run - 1, k)) for k in downs))
        if crosses(run):
            low = [chip(run, k) for k in range(4)]
            high = [chip(run + 1, k) for k in range(4)]
            for name in ("X1", "X3", "X4"):
                add(name, (low[3], high[0]), (high[0], low[3]))
            for name in ("X2", "X5"):
                add(name, (high[0], high[1]), (low[3], low[2]))
            add("X6", (high[1], high[2]), (low[2], low[1]))
    return table


ROUTES = routes()


def edge_routes():
    pairs = []
    for group in range(16):
        for inner in range(8):
            pairs.append((group * 32 + 24 + inner, ((group + 1) % 16) * 32 + inner))
            pairs.append((group * 32 + inner, ((group - 1) % 16) * 32 + 24 + inner))
    return pairs


EDGE = edge_routes()


def after(value, *others):
    return lax.optimization_barrier((value,) + others)[0]


def vmem(count):
    return [pl.BlockSpec(memory_space=pltpu.VMEM)] * count


def smem(count):
    return [pl.BlockSpec(memory_space=pltpu.SMEM)] * count


PARAMS = pltpu.CompilerParams(vmem_limit_bytes=48 * 1024 * 1024)


def scores(rows, columns):
    return lax.dot_general(rows, columns, (((1,), (1,)), ((), ())), preferred_element_type=jnp.float32)


def fold(values):
    tail = jnp.concatenate([values[:, 128:], jnp.zeros((ROWS, 256 - ROWS), jnp.float32)], axis=1)
    return values[:, :128] + tail


def own_kernel(unit_ref, other_ref, partner_ref, e_own_ref, e_other_ref, sum_own_ref, sum_other_ref, pos_ref):
    unit = unit_ref[...]
    row = lax.broadcasted_iota(jnp.int32, (ROWS, ROWS), 0)
    column = lax.broadcasted_iota(jnp.int32, (ROWS, ROWS), 1)
    partner = partner_ref[...]
    logits = scores(unit, unit) / SOFTMAX_TEMPER
    expo = jnp.where(row == column, 0.0, jnp.exp(logits - 1.0 / SOFTMAX_TEMPER))
    e_own_ref[...] = expo
    sum_own_ref[...] = fold(expo)
    picked = jnp.where(partner == row, logits, 0.0)
    logits = scores(other_ref[...], unit) / SOFTMAX_TEMPER
    expo = jnp.exp(logits - 1.0 / SOFTMAX_TEMPER)
    e_other_ref[...] = expo
    sum_other_ref[...] = fold(expo)
    picked = picked + jnp.where(partner == row + ROWS, logits, 0.0)
    pos_ref[...] = jnp.sum(fold(picked), axis=0, keepdims=True)


def own_call(unit, other, partner):
    f32 = jnp.float32
    return pl.pallas_call(
        own_kernel,
        out_shape=(
            jax.ShapeDtypeStruct((ROWS, ROWS), f32),
            jax.ShapeDtypeStruct((ROWS, ROWS), f32),
            jax.ShapeDtypeStruct((ROWS, 128), f32),
            jax.ShapeDtypeStruct((ROWS, 128), f32),
            jax.ShapeDtypeStruct((1, 128), f32),
        ),
        in_specs=vmem(3),
        out_specs=tuple(vmem(5)),
        compiler_params=PARAMS,
        cost_estimate=pl.CostEstimate(flops=2 * 448 * ROWS * WIDTH, bytes_accessed=2 << 20, transcendentals=448 * ROWS),
        name="own_scores",
    )(unit, other, partner)


def block_kernel(n_cand, last, *refs):
    flags_ref, unit_ref, other_ref, sum_own_ref, sum_other_ref = refs[:5]
    cands = refs[5 : 5 + n_cand]
    rest = refs[5 + n_cand :]
    if last:
        pos_ref, rest = rest[0], rest[1:]
    e_own_ref, e_other_ref = rest[:2]
    rest = rest[2:]
    if last:
        pay_ref, rest = rest[0], rest[1:]
    else:
        sum_own_out, sum_other_out = rest[:2]
        rest = rest[2:]
    if n_cand > 1:
        block_ref, rest = rest[0], rest[1:]
        block_ref[...] = cands[0][...]
        for number in range(1, n_cand):

            @pl.when(flags_ref[0] == number)
            def _(number=number):
                block_ref[...] = cands[number][...]
    else:
        block_ref = cands[0]
    block = block_ref[...]
    expo = jnp.exp(scores(unit_ref[...], block) / SOFTMAX_TEMPER - 1.0 / SOFTMAX_TEMPER)
    e_own_ref[...] = expo
    sum_own = sum_own_ref[...] + fold(expo)
    expo = jnp.exp(scores(other_ref[...], block) / SOFTMAX_TEMPER - 1.0 / SOFTMAX_TEMPER)
    expo = jnp.where(flags_ref[1] == 1, 0.0, expo)
    e_other_ref[...] = expo
    sum_other = sum_other_ref[...] + fold(expo)
    if last:
        pay_ref[...] = jnp.zeros((8, 128), jnp.float32)
        for half, total in enumerate((sum_own, sum_other)):
            across = jnp.sum(jnp.transpose(total), axis=0, keepdims=True)
            pay_ref[2 * half : 2 * half + 1, :] = across[:, :128]
            pay_ref[2 * half + 1 : 2 * half + 2, : ROWS - 128] = across[:, 128:]
        pay_ref[4:5, :] = pos_ref[...]
    else:
        sum_own_out[...] = sum_own
        sum_other_out[...] = sum_other


def block_call(flags, unit, other, sums, cands, pos=None):
    f32 = jnp.float32
    last = pos is not None
    n = len(cands)
    shapes = [jax.ShapeDtypeStruct((ROWS, ROWS), f32)] * 2
    if last:
        shapes.append(jax.ShapeDtypeStruct((8, 128), f32))
    else:
        shapes += [jax.ShapeDtypeStruct((ROWS, 128), f32)] * 2
    if n > 1:
        shapes.append(jax.ShapeDtypeStruct((ROWS, WIDTH), jnp.bfloat16))
    operands = [unit, other, *sums, *cands] + ([pos] if last else [])

    def kernel(*refs):
        block_kernel(n, last, *refs)

    out = pl.pallas_call(
        kernel,
        out_shape=tuple(shapes),
        in_specs=smem(1) + vmem(len(operands)),
        out_specs=tuple(vmem(len(shapes))),
        compiler_params=PARAMS,
        cost_estimate=pl.CostEstimate(flops=2 * 448 * ROWS * WIDTH, bytes_accessed=2 << 20, transcendentals=448 * ROWS),
        name="block_scores",
    )(flags, *operands)
    block = out[-1] if n > 1 else cands[0]
    if last:
        return out[:2], out[2], block
    return out[:2], out[2:4], block


def denom_kernel(place_ref, pay_ref, inv_ref, other_ref, edge_ref, loss_ref):
    y, k, core = place_ref[0], place_ref[1], place_ref[2]
    pay = pay_ref[...].reshape(16, 2, 8, 128)
    lane = lax.broadcasted_iota(jnp.int32, (16, 2, 128), 2)
    part = lax.broadcasted_iota(jnp.int32, (16, 2, 128), 1)
    real = part * 128 + lane < ROWS
    first = jnp.where(real, pay[:, 0, 0:2] + pay[:, 1, 2:4], 1.0)
    second = jnp.where(real, pay[:, 1, 0:2] + pay[:, 0, 2:4], 1.0)
    total = jnp.log(first) + jnp.log(second)
    total = jnp.sum(total.reshape(32, 128), axis=0, keepdims=True)
    total = total - jnp.sum(pay[:, :, 4].reshape(32, 128), axis=0, keepdims=True)
    loss_ref[...] = jnp.broadcast_to(jnp.sum(total, axis=1, keepdims=True), (8, 128))
    first, second = 1.0 / first, 1.0 / second
    inv_ref[...] = jnp.where(core == 0, first, second)
    other_all = jnp.where(core == 0, second, first)
    chip = lax.broadcasted_iota(jnp.int32, (16, 2, 128), 0)
    other_ref[...] = jnp.sum(jnp.where(chip == y * 4 + k, other_all, 0.0), axis=0)
    edge_ref[...] = inv_ref[pl.ds(jnp.where(y == 3, 12, 0), 4)]


def denom_call(place, pay):
    f32 = jnp.float32
    return pl.pallas_call(
        denom_kernel,
        out_shape=(
            jax.ShapeDtypeStruct((16, 2, 128), f32),
            jax.ShapeDtypeStruct((2, 128), f32),
            jax.ShapeDtypeStruct((4, 2, 128), f32),
            jax.ShapeDtypeStruct((8, 128), f32),
        ),
        in_specs=smem(1) + vmem(1),
        out_specs=tuple(vmem(4)),
        compiler_params=PARAMS,
        name="denoms",
    )(place, pay)


def lanes(pair):
    return jnp.concatenate([pair[0:1, :], pair[1:2, : ROWS - 128]], axis=1)


def grad_kernel(shift, *refs):
    where_ref, inv_ref, edge_ref, row_ref, partner_ref = refs[:5]
    expos, blocks = refs[5:12], refs[12:19]
    out_ref = refs[19]
    mine = lanes(row_ref[...])
    mine = jnp.transpose(jnp.broadcast_to(mine, (128, ROWS)))[:, 0:1]
    total = None
    for number in range(7):
        place = where_ref[number]
        inside = inv_ref[pl.ds(jnp.minimum(place, 15), 1)]
        outside = edge_ref[pl.ds(jnp.maximum(place - 16, 0), 1)]
        column = lanes(jnp.where(place < 16, inside, outside)[0])
        weight = expos[number][...] * (mine + column)
        if number == 0:
            row = lax.broadcasted_iota(jnp.int32, (ROWS, ROWS), 0) + shift
            weight = weight - jnp.where(partner_ref[...] == row, 2.0, 0.0)
        term = jnp.dot(weight.astype(jnp.bfloat16), blocks[number][...], preferred_element_type=jnp.float32)
        total = term if total is None else total + term
    out_ref[...] = total


def grad_call(shift, where, inv, edge, row, partner, expos, blocks):
    def kernel(*refs):
        grad_kernel(shift, *refs)

    return pl.pallas_call(
        kernel,
        out_shape=jax.ShapeDtypeStruct((ROWS, WIDTH), jnp.float32),
        in_specs=smem(1) + vmem(18),
        out_specs=pl.BlockSpec(memory_space=pltpu.VMEM),
        compiler_params=PARAMS,
        cost_estimate=pl.CostEstimate(flops=2 * 7 * ROWS * ROWS * WIDTH, bytes_accessed=6 << 20, transcendentals=0),
        name="unit_gradient",
    )(where, inv, edge, row, partner, *expos, *blocks)


def final_kernel(emb_ref, mine_ref, got_ref, out_ref):
    emb = emb_ref[...]
    norm = jnp.sqrt(jnp.sum(emb * emb, axis=1, keepdims=True) + 1e-06)
    unit32 = emb / norm
    unit_gradient = (mine_ref[...] + got_ref[...]) / SOFTMAX_TEMPER
    radial = jnp.sum(unit32 * unit_gradient, axis=1, keepdims=True)
    out_ref[...] = (unit_gradient - unit32 * radial) / norm


def final_call(emb, mine, got):
    spec = pl.BlockSpec((56, WIDTH), lambda i: (i, 0))
    return pl.pallas_call(
        final_kernel,
        out_shape=jax.ShapeDtypeStruct((ROWS, WIDTH), jnp.float32),
        grid=(4,),
        in_specs=[spec] * 3,
        out_specs=spec,
        compiler_params=PARAMS,
        cost_estimate=pl.CostEstimate(flops=10 * ROWS * WIDTH, bytes_accessed=16 * ROWS * WIDTH, transcendentals=0),
        name="final",
    )(emb, mine, got)


def send(value, name):
    return lax.ppermute(value, AXES, ROUTES[name])


def per_device(embeddings, partner):
    norm = jnp.sqrt(jnp.sum(embeddings * embeddings, axis=1, keepdims=True) + 1e-06)
    unit = (embeddings / norm).astype(jnp.bfloat16)

    core = lax.axis_index("core")
    k = lax.axis_index("zl")
    y = lax.axis_index("y")
    run = lax.axis_index(("zh", "x", "y"))
    below, above = run % 16 == 15, run % 16 == 0
    end = (below & (k == 3)) | (above & (k == 0))
    mid = (below & (k == 2)) | (above & (k == 1))
    inner = (k == 1) | (k == 2)

    local = (partner % (2 * ROWS) - core * ROWS) % (2 * ROWS)
    local = local.reshape(1, ROWS).astype(jnp.int32)

    sources = jnp.asarray(RECEIVED)[k]
    steps_in = sources - k
    steps_out = jnp.where(steps_in < 0, steps_in + 4, steps_in - 4)
    excluded = jnp.where(core == 0, -3, 3)
    out_in = (steps_in == excluded).astype(jnp.int32)
    out_out = (steps_out == excluded).astype(jnp.int32)
    line = y + jnp.where(steps_in < 0, 1, -1)
    place_in = y * 4 + sources
    place_out = jnp.where((line < 0) | (line > 3), 16 + sources, line * 4 + sources)
    where = jnp.concatenate([(y * 4 + k)[None], place_in, place_out]).astype(jnp.int32)
    pick3 = inner.astype(jnp.int32)
    pick_y1 = jnp.where(end, 2, jnp.where(mid, 1, 0)).astype(jnp.int32)
    pick_y2 = jnp.where(end, 1, jnp.where(mid_receiver(below, above, k), 2, 0)).astype(jnp.int32)
    pick_y3 = jnp.where(end, 2, jnp.where(mid, 3, inner.astype(jnp.int32))).astype(jnp.int32)
    zero = jnp.int32(0)

    other = lax.ppermute(unit, ("core",), [(0, 1), (1, 0)])
    r1 = send(unit, "P1")
    x1 = send(unit, "X1")
    expo0, pos = None, None
    e_own, e_other, sum_own, sum_other, pos = own_call(unit, other, local)
    expos, blocks, sums = [(e_own, e_other)], [unit], (sum_own, sum_other)

    def add(flags, cands, last=False):
        nonlocal sums
        pair, rest, block = block_call(jnp.stack(flags), unit, other, sums, cands, pos if last else None)
        expos.append(pair)
        blocks.append(block)
        if last:
            return rest
        sums = rest

    r2 = send(after(unit, sum_own), "P2")
    y1 = send(r1, "Y1")
    x2 = send(x1, "X2")
    x3 = send(r1, "X3")
    add([zero, out_in[0]], [r1])
    p3b = send(unit, "P3b")
    p3a = send(r1, "P3a")
    x5 = send(x3, "X5")
    y2 = send(r2, "Y2")
    x4 = send(r2, "X4")
    x6 = send(x2, "X6")
    add([zero, out_in[1]], [r2])
    y3a = send(p3a, "Y3a")
    y3b = send(p3b, "Y3b")
    add([pick3, out_in[2]], [p3a, p3b])
    add([pick_y1, out_out[0]], [y1, x2, x4])
    add([pick_y2, out_out[1]], [y2, x3, x6])
    pay = add([pick_y3, out_out[2]], [y3a, y3b, x1, x5], last=True)

    pays = lax.all_to_all(jnp.broadcast_to(pay[None], (32, 8, 128)), DEV_AXES, 0, 0)
    place = jnp.stack([y, k, core]).astype(jnp.int32)
    inv, other_inv, edge, loss = denom_call(place, pays)
    edge = lax.ppermute(edge, AXES, EDGE)
    mine_inv = lax.dynamic_index_in_dim(inv, y * 4 + k, 0, keepdims=False)

    for_other = grad_call(ROWS, where, inv, edge, other_inv, local, [e[1] for e in expos], blocks)
    got = lax.ppermute(for_other, ("core",), [(0, 1), (1, 0)])
    mine = grad_call(0, where, inv, edge, mine_inv, local, [e[0] for e in expos], blocks)
    grad = final_call(embeddings, mine, got)

    for axis, bit in (("x", 1), ("x", 2), ("zh", 1), ("zh", 2)):
        loss = loss + lax.ppermute(loss, (axis,), [(i, i ^ bit) for i in range(4)])
    total_rows = ROWS * 512
    loss = loss[0, 0] / total_rows + 1.0 / SOFTMAX_TEMPER
    return (loss, grad)


def mid_receiver(below, above, k):
    return (below & (k == 1)) | (above & (k == 2))


def solution(mesh):
    split = Mesh(mesh.devices.reshape(SHAPE), AXES)
    in_specs = (P(AXES, None), P(AXES))
    out_specs = (P(), P(AXES, None))
    return jax.shard_map(per_device, mesh=split, in_specs=in_specs, out_specs=out_specs, check_vma=False)
```

```python
import jax
import jax.numpy as jnp
from jax import lax
from jax.experimental import pallas as pl
from jax.experimental.pallas import tpu as pltpu
from jax.sharding import Mesh
from jax.sharding import PartitionSpec as P

ROUNDS = 6
SOFTMAX_TEMPER = 0.1
AXES = ("zh", "x", "y", "zl", "core")
SHAPE = (4, 4, 4, 4, 2)
RUNS = 64
DEV_AXES = ("y", "zl", "core")
ROWS = 224
WIDTH = 1024

def crosses(run):
    return run % 16 == 15


def routes():
    names = ("P1", "P2", "P3a", "P3b", "Y1", "Y2", "Y3a", "Y3b", "X1", "X2", "X3", "X4", "X5", "X6")
    table = {name: [] for name in names}

    def chip(run, k):
        return (run % RUNS) * 4 + k

    def add(name, *pairs):
        for source, target in pairs:
            for core in (0, 1):
                table[name].append((2 * source + core, 2 * target + core))

    for run in range(RUNS):
        for name, moves in (
            ("P1", ((0, 2), (1, 0), (2, 3), (3, 1))),
            ("P2", ((1, 3), (2, 0), (0, 1), (3, 2))),
            ("P3a", ((2, 3), (1, 0))),
            ("P3b", ((1, 2), (2, 1))),
        ):
            add(name, *((chip(run, a), chip(run, b)) for a, b in moves))
        for name, ups, downs in (
            ("Y1", (0, 1), (2, 3)),
            ("Y2", (0, 2), (1, 3)),
            ("Y3a", (0,), (3,)),
            ("Y3b", (1,), (2,)),
        ):
            if not crosses(run):
                add(name, *((chip(run, k), chip(run + 1, k)) for k in ups))
            if not crosses(run - 1):
                add(name, *((chip(run, k), chip(run - 1, k)) for k in downs))
        if crosses(run):
            low = [chip(run, k) for k in range(4)]
            high = [chip(run + 1, k) for k in range(4)]
            for name in ("X1", "X3", "X4"):
                add(name, (low[3], high[0]), (high[0], low[3]))
            for name in ("X2", "X5"):
                add(name, (high[0], high[1]), (low[3], low[2]))
            add("X6", (high[1], high[2]), (low[2], low[1]))
    return table


ROUTES = routes()


def edge_routes():
    pairs = []
    for group in range(16):
        for inner in range(8):
            pairs.append((group * 32 + 24 + inner, ((group + 1) % 16) * 32 + inner))
            pairs.append((group * 32 + inner, ((group - 1) % 16) * 32 + 24 + inner))
    return pairs


EDGE = edge_routes()


def after(value, *others):
    return lax.optimization_barrier((value,) + others)[0]


def vmem(count):
    return [pl.BlockSpec(memory_space=pltpu.VMEM)] * count


def smem(count):
    return [pl.BlockSpec(memory_space=pltpu.SMEM)] * count


PARAMS = pltpu.CompilerParams(vmem_limit_bytes=12 * 1024 * 1024)


def scores(rows, columns):
    return lax.dot_general(rows, columns, (((1,), (1,)), ((), ())), preferred_element_type=jnp.float32)


def fold(values):
    tail = jnp.concatenate([values[:, 128:], jnp.zeros((ROWS, 256 - ROWS), jnp.float32)], axis=1)
    return values[:, :128] + tail


def own_kernel(ids_ref, unit_ref, other_ref, partner_ref, local_ref, e_own_ref, e_other_ref, sum_own_ref, sum_other_ref, pos_ref):
    unit = unit_ref[...]
    row = lax.broadcasted_iota(jnp.int32, (ROWS, ROWS), 0)
    column = lax.broadcasted_iota(jnp.int32, (ROWS, ROWS), 1)
    shift = ids_ref[2] * ROWS
    partner = partner_ref[...] - (ids_ref[3] * (8 * ROWS) + ids_ref[1] * (2 * ROWS) + shift)
    partner = jnp.where(partner < 0, partner + 2 * ROWS, partner)
    local_ref[...] = partner
    logits = scores(unit, unit) / SOFTMAX_TEMPER
    expo = jnp.where(row == column, 0.0, jnp.exp(logits - 1.0 / SOFTMAX_TEMPER))
    e_own_ref[...] = expo
    sum_own_ref[...] = fold(expo)
    picked = jnp.where(partner == row, logits, 0.0)
    logits = scores(other_ref[...], unit) / SOFTMAX_TEMPER
    expo = jnp.exp(logits - 1.0 / SOFTMAX_TEMPER)
    e_other_ref[...] = expo
    sum_other_ref[...] = fold(expo)
    picked = picked + jnp.where(partner == row + ROWS, logits, 0.0)
    pos_ref[...] = jnp.sum(fold(picked), axis=0, keepdims=True)


def own_call(ids, unit, other, partner):
    f32 = jnp.float32
    return pl.pallas_call(
        own_kernel,
        out_shape=(
            jax.ShapeDtypeStruct((1, ROWS), jnp.int32),
            jax.ShapeDtypeStruct((ROWS, ROWS), f32),
            jax.ShapeDtypeStruct((ROWS, ROWS), f32),
            jax.ShapeDtypeStruct((ROWS, 128), f32),
            jax.ShapeDtypeStruct((ROWS, 128), f32),
            jax.ShapeDtypeStruct((1, 128), f32),
        ),
        in_specs=smem(1) + vmem(3),
        out_specs=tuple(vmem(6)),
        compiler_params=PARAMS,
        cost_estimate=pl.CostEstimate(flops=2 * 448 * ROWS * WIDTH, bytes_accessed=2 << 20, transcendentals=448 * ROWS),
        name="own_scores",
    )(ids, unit, other, partner)


def received(number, k):
    first = jnp.where(k == 0, 1, jnp.where(k == 1, 3, jnp.where(k == 2, 0, 2)))
    return (first, 3 - first, 3 - k)[number]


def pick(number, ids_ref):
    k, run = ids_ref[1], ids_ref[3]
    below, above = run % 16 == 15, run % 16 == 0
    end = (below & (k == 3)) | (above & (k == 0))
    mid = (below & (k == 2)) | (above & (k == 1))
    far = (below & (k == 1)) | (above & (k == 2))
    inner = jnp.where((k == 1) | (k == 2), 1, 0)
    if number == 2:
        return inner
    if number == 3:
        return jnp.where(end, 2, jnp.where(mid, 1, 0))
    if number == 4:
        return jnp.where(end, 1, jnp.where(far, 2, 0))
    return jnp.where(end, 2, jnp.where(mid, 3, inner))


def block_kernel(number_in, n_cand, last, *refs):
    ids_ref, unit_ref, other_ref, sum_own_ref, sum_other_ref = refs[:5]
    cands = refs[5 : 5 + n_cand]
    rest = refs[5 + n_cand :]
    if last:
        pos_ref, rest = rest[0], rest[1:]
    e_own_ref, e_other_ref = rest[:2]
    rest = rest[2:]
    if last:
        pay_ref, rest = rest[0], rest[1:]
    else:
        sum_own_out, sum_other_out = rest[:2]
        rest = rest[2:]
    k, core = ids_ref[1], ids_ref[2]
    steps = received(number_in % 3, k) - k
    if number_in > 2:
        steps = jnp.where(steps < 0, steps + 4, steps - 4)
    outside = steps == jnp.where(core == 0, -3, 3)
    if n_cand > 1:
        choice = pick(number_in, ids_ref)
        block_ref, rest = rest[0], rest[1:]
        block_ref[...] = cands[0][...]
        for number in range(1, n_cand):

            @pl.when(choice == number)
            def _(number=number):
                block_ref[...] = cands[number][...]
    else:
        block_ref = cands[0]
    block = block_ref[...]
    expo = jnp.exp(scores(unit_ref[...], block) / SOFTMAX_TEMPER - 1.0 / SOFTMAX_TEMPER)
    e_own_ref[...] = expo
    sum_own = sum_own_ref[...] + fold(expo)
    expo = jnp.exp(scores(other_ref[...], block) / SOFTMAX_TEMPER - 1.0 / SOFTMAX_TEMPER)
    expo = jnp.where(outside, 0.0, expo)
    e_other_ref[...] = expo
    sum_other = sum_other_ref[...] + fold(expo)
    if last:
        pay_ref[...] = jnp.zeros((8, 128), jnp.float32)
        for half, total in enumerate((sum_own, sum_other)):
            across = jnp.sum(jnp.transpose(total), axis=0, keepdims=True)
            pay_ref[2 * half : 2 * half + 1, :] = across[:, :128]
            pay_ref[2 * half + 1 : 2 * half + 2, : ROWS - 128] = across[:, 128:]
        pay_ref[4:5, :] = pos_ref[...]
    else:
        sum_own_out[...] = sum_own
        sum_other_out[...] = sum_other


def block_call(number_in, ids, unit, other, sums, cands, pos=None):
    f32 = jnp.float32
    last = pos is not None
    n = len(cands)
    shapes = [jax.ShapeDtypeStruct((ROWS, ROWS), f32)] * 2
    if last:
        shapes.append(jax.ShapeDtypeStruct((8, 128), f32))
    else:
        shapes += [jax.ShapeDtypeStruct((ROWS, 128), f32)] * 2
    if n > 1:
        shapes.append(jax.ShapeDtypeStruct((ROWS, WIDTH), jnp.bfloat16))
    operands = [unit, other, *sums, *cands] + ([pos] if last else [])

    def kernel(*refs):
        block_kernel(number_in, n, last, *refs)

    out = pl.pallas_call(
        kernel,
        out_shape=tuple(shapes),
        in_specs=smem(1) + vmem(len(operands)),
        out_specs=tuple(vmem(len(shapes))),
        compiler_params=PARAMS,
        cost_estimate=pl.CostEstimate(flops=2 * 448 * ROWS * WIDTH, bytes_accessed=2 << 20, transcendentals=448 * ROWS),
        name="block_scores",
    )(ids, *operands)
    block = out[-1] if n > 1 else cands[0]
    if last:
        return out[:2], out[2], block
    return out[:2], out[2:4], block


def denom_kernel(ids_ref, pay_ref, inv_ref, mine_ref, other_ref, edge_ref, loss_ref):
    y, k, core = ids_ref[0], ids_ref[1], ids_ref[2]
    pay = pay_ref[...].reshape(16, 2, 8, 128)
    lane = lax.broadcasted_iota(jnp.int32, (16, 2, 128), 2)
    part = lax.broadcasted_iota(jnp.int32, (16, 2, 128), 1)
    real = part * 128 + lane < ROWS
    first = jnp.where(real, pay[:, 0, 0:2] + pay[:, 1, 2:4], 1.0)
    second = jnp.where(real, pay[:, 1, 0:2] + pay[:, 0, 2:4], 1.0)
    total = jnp.log(first) + jnp.log(second)
    total = jnp.sum(total.reshape(32, 128), axis=0, keepdims=True)
    total = total - jnp.sum(pay[:, :, 4].reshape(32, 128), axis=0, keepdims=True)
    loss_ref[...] = jnp.broadcast_to(jnp.sum(total, axis=1, keepdims=True), (8, 128))
    first, second = 1.0 / first, 1.0 / second
    inv_ref[...] = jnp.where(core == 0, first, second)
    other_all = jnp.where(core == 0, second, first)
    chip = lax.broadcasted_iota(jnp.int32, (16, 2, 128), 0)
    here = chip == y * 4 + k
    mine_ref[...] = jnp.sum(jnp.where(here, inv_ref[...], 0.0), axis=0)
    other_ref[...] = jnp.sum(jnp.where(here, other_all, 0.0), axis=0)
    edge_ref[...] = inv_ref[pl.ds(jnp.where(y == 3, 12, 0), 4)]


def denom_call(ids, pay):
    f32 = jnp.float32
    return pl.pallas_call(
        denom_kernel,
        out_shape=(
            jax.ShapeDtypeStruct((16, 2, 128), f32),
            jax.ShapeDtypeStruct((2, 128), f32),
            jax.ShapeDtypeStruct((2, 128), f32),
            jax.ShapeDtypeStruct((4, 2, 128), f32),
            jax.ShapeDtypeStruct((8, 128), f32),
        ),
        in_specs=smem(1) + vmem(1),
        out_specs=tuple(vmem(5)),
        compiler_params=PARAMS,
        name="denoms",
    )(ids, pay)


def lanes(pair):
    return jnp.concatenate([pair[0:1, :], pair[1:2, : ROWS - 128]], axis=1)


def grad_kernel(shift, *refs):
    ids_ref, inv_ref, edge_ref, row_ref, partner_ref = refs[:5]
    expos, blocks = refs[5:12], refs[12:19]
    out_ref = refs[19]
    mine = lanes(row_ref[...])
    mine = jnp.transpose(jnp.broadcast_to(mine, (128, ROWS)))[:, 0:1]
    total = None
    y, k = ids_ref[0], ids_ref[1]
    for number in range(7):
        chip, line = k, y
        if number:
            chip = received((number - 1) % 3, k)
        if number > 3:
            line = y + jnp.where(chip < k, 1, -1)
        inside = inv_ref[pl.ds(jnp.clip(line, 0, 3) * 4 + chip, 1)]
        if number > 3:
            inside = jnp.where((line < 0) | (line > 3), edge_ref[pl.ds(chip, 1)], inside)
        column = lanes(inside[0])
        weight = expos[number][...] * (mine + column)
        if number == 0:
            row = lax.broadcasted_iota(jnp.int32, (ROWS, ROWS), 0) + shift
            weight = weight - jnp.where(partner_ref[...] == row, 2.0, 0.0)
        term = jnp.dot(weight.astype(jnp.bfloat16), blocks[number][...], preferred_element_type=jnp.float32)
        total = term if total is None else total + term
    out_ref[...] = total


def grad_call(shift, ids, inv, edge, row, partner, expos, blocks):
    def kernel(*refs):
        grad_kernel(shift, *refs)

    return pl.pallas_call(
        kernel,
        out_shape=jax.ShapeDtypeStruct((ROWS, WIDTH), jnp.float32),
        in_specs=smem(1) + vmem(18),
        out_specs=pl.BlockSpec(memory_space=pltpu.VMEM),
        compiler_params=PARAMS,
        cost_estimate=pl.CostEstimate(flops=2 * 7 * ROWS * ROWS * WIDTH, bytes_accessed=6 << 20, transcendentals=0),
        name="unit_gradient",
    )(ids, inv, edge, row, partner, *expos, *blocks)


def final_kernel(emb_ref, mine_ref, got_ref, out_ref):
    emb = emb_ref[...]
    norm = jnp.sqrt(jnp.sum(emb * emb, axis=1, keepdims=True) + 1e-06)
    unit32 = emb / norm
    unit_gradient = (mine_ref[...] + got_ref[...]) / SOFTMAX_TEMPER
    radial = jnp.sum(unit32 * unit_gradient, axis=1, keepdims=True)
    out_ref[...] = (unit_gradient - unit32 * radial) / norm


def final_call(emb, mine, got):
    spec = pl.BlockSpec((56, WIDTH), lambda i: (i, 0))
    return pl.pallas_call(
        final_kernel,
        out_shape=jax.ShapeDtypeStruct((ROWS, WIDTH), jnp.float32),
        grid=(4,),
        in_specs=[spec] * 3,
        out_specs=spec,
        compiler_params=PARAMS,
        cost_estimate=pl.CostEstimate(flops=10 * ROWS * WIDTH, bytes_accessed=16 * ROWS * WIDTH, transcendentals=0),
        name="final",
    )(emb, mine, got)


def send(value, name):
    return lax.ppermute(value, AXES, ROUTES[name])


def per_device(embeddings, partner):
    norm = jnp.sqrt(jnp.sum(embeddings * embeddings, axis=1, keepdims=True) + 1e-06)
    unit = (embeddings / norm).astype(jnp.bfloat16)

    run = lax.axis_index(("zh", "x", "y"))
    ids = jnp.stack([lax.axis_index(name) for name in DEV_AXES] + [run]).astype(jnp.int32)
    partner = partner.reshape(1, ROWS)

    other = lax.ppermute(unit, ("core",), [(0, 1), (1, 0)])
    r1 = send(unit, "P1")
    local, e_own, e_other, sum_own, sum_other, pos = own_call(ids, unit, other, partner)
    expos, blocks, sums = [(e_own, e_other)] + [None] * 6, [unit] + [None] * 6, (sum_own, sum_other)

    def add(number, cands):
        nonlocal sums
        last = number == 5
        pair, rest, block = block_call(number, ids, unit, other, sums, cands, pos if last else None)
        expos[number + 1] = pair
        blocks[number + 1] = block
        if last:
            return rest
        sums = rest

    x1 = send(after(unit, sums[0]), "X1")
    r1 = after(r1, sums[0])
    r2 = send(after(unit, r1), "P2")
    y1 = send(r1, "Y1")
    x2 = send(after(x1, r1), "X2")
    x3 = send(r1, "X3")
    add(0, [r1])
    r2 = after(r2, sums[0])
    p3b = send(after(unit, r2), "P3b")
    p3a = send(after(r1, r2), "P3a")
    y2 = send(after(r2, y1), "Y2")
    x4 = send(after(r2, x3), "X4")
    x6 = send(after(x2, r2), "X6")
    add(1, [r2])
    p3a = after(p3a, sums[0])
    p3b = after(p3b, sums[0])
    y3a = send(after(p3a, y2), "Y3a")
    y3b = send(after(p3b, y2), "Y3b")
    x5 = send(after(x3, p3a, p3b), "X5")
    add(2, [p3a, p3b])
    add(3, [y1, x2, x4])
    add(4, [y2, x3, x6])
    pay = add(5, [y3a, y3b, x1, x5])

    pays = lax.all_to_all(jnp.broadcast_to(pay[None], (32, 8, 128)), DEV_AXES, 0, 0)
    inv, mine_inv, other_inv, edge, loss = denom_call(ids, pays)
    def exchange(value, axis, bit, *meanwhile):
        got = lax.ppermute(value, (axis,), [(i, i ^ bit) for i in range(4)])
        return value + after(got, *meanwhile)

    edge = lax.ppermute(edge, AXES, EDGE)
    loss = exchange(loss, "x", 1)
    for_other = grad_call(ROWS, ids, after(inv, loss), edge, other_inv, local, [e[1] for e in expos], blocks)
    loss = exchange(loss, "x", 2, for_other)
    got = lax.ppermute(after(for_other, loss), ("core",), [(0, 1), (1, 0)])
    mine = grad_call(0, ids, after(inv, loss), edge, mine_inv, local, [e[0] for e in expos], blocks)
    loss = exchange(loss, "zh", 1, mine)
    grad = final_call(embeddings, mine, after(got, loss))
    loss = exchange(loss, "zh", 2, grad)
    total_rows = ROWS * 512
    loss = loss[0, 0] / total_rows + 1.0 / SOFTMAX_TEMPER
    return (loss, grad)


def solution(mesh):
    split = Mesh(mesh.devices.reshape(SHAPE), AXES)
    in_specs = (P(AXES, None), P(AXES))
    out_specs = (P(), P(AXES, None))
    return jax.shard_map(per_device, mesh=split, in_specs=in_specs, out_specs=out_specs, check_vma=False)
```

```python
import jax
import jax.numpy as jnp
from jax import lax
from jax.experimental import pallas as pl
from jax.experimental.pallas import tpu as pltpu
from jax.sharding import Mesh
from jax.sharding import PartitionSpec as P

ROUNDS = 6
SOFTMAX_TEMPER = 0.1
AXES = ("zh", "x", "y", "zl", "core")
SHAPE = (4, 4, 4, 4, 2)
RUNS = 64
DEV_AXES = ("y", "zl", "core")
ROWS = 224
WIDTH = 1024

def crosses(run):
    return run % 16 == 15


def routes():
    names = ("P1", "P2", "P3a", "P3b", "Y1", "Y2", "Y3a", "Y3b", "X1", "X2", "X3", "X4", "X5", "X6")
    table = {name: [] for name in names}

    def chip(run, k):
        return (run % RUNS) * 4 + k

    def add(name, *pairs):
        for source, target in pairs:
            for core in (0, 1):
                table[name].append((2 * source + core, 2 * target + core))

    for run in range(RUNS):
        for name, moves in (
            ("P1", ((0, 2), (1, 0), (2, 3), (3, 1))),
            ("P2", ((1, 3), (2, 0), (0, 1), (3, 2))),
            ("P3a", ((2, 3), (1, 0))),
            ("P3b", ((1, 2), (2, 1))),
        ):
            add(name, *((chip(run, a), chip(run, b)) for a, b in moves))
        for name, ups, downs in (
            ("Y1", (0, 1), (2, 3)),
            ("Y2", (0, 2), (1, 3)),
            ("Y3a", (0,), (3,)),
            ("Y3b", (1,), (2,)),
        ):
            if not crosses(run):
                add(name, *((chip(run, k), chip(run + 1, k)) for k in ups))
            if not crosses(run - 1):
                add(name, *((chip(run, k), chip(run - 1, k)) for k in downs))
        if crosses(run):
            low = [chip(run, k) for k in range(4)]
            high = [chip(run + 1, k) for k in range(4)]
            for name in ("X1", "X3", "X4"):
                add(name, (low[3], high[0]), (high[0], low[3]))
            for name in ("X2", "X5"):
                add(name, (high[0], high[1]), (low[3], low[2]))
            add("X6", (high[1], high[2]), (low[2], low[1]))
    return table


ROUTES = routes()


def edge_routes():
    pairs = []
    for group in range(16):
        for inner in range(8):
            pairs.append((group * 32 + 24 + inner, ((group + 1) % 16) * 32 + inner))
            pairs.append((group * 32 + inner, ((group - 1) % 16) * 32 + 24 + inner))
    return pairs


EDGE = edge_routes()


def after(value, *others):
    return lax.optimization_barrier((value,) + others)[0]


def vmem(count):
    return [pl.BlockSpec(memory_space=pltpu.VMEM)] * count


def smem(count):
    return [pl.BlockSpec(memory_space=pltpu.SMEM)] * count


PARAMS = pltpu.CompilerParams(vmem_limit_bytes=12 * 1024 * 1024)


def scores(rows, columns):
    return lax.dot_general(rows, columns, (((1,), (1,)), ((), ())), preferred_element_type=jnp.float32)


def fold(values):
    tail = jnp.concatenate([values[:, 128:], jnp.zeros((ROWS, 256 - ROWS), jnp.float32)], axis=1)
    return values[:, :128] + tail


def own_kernel(ids_ref, unit_ref, other_ref, partner_ref, local_ref, e_own_ref, e_other_ref, sum_own_ref, sum_other_ref, pos_ref):
    unit = unit_ref[...]
    row = lax.broadcasted_iota(jnp.int32, (ROWS, ROWS), 0)
    column = lax.broadcasted_iota(jnp.int32, (ROWS, ROWS), 1)
    shift = ids_ref[2] * ROWS
    partner = partner_ref[...] - (ids_ref[3] * (8 * ROWS) + ids_ref[1] * (2 * ROWS) + shift)
    partner = jnp.where(partner < 0, partner + 2 * ROWS, partner)
    local_ref[...] = partner
    logits = scores(unit, unit) / SOFTMAX_TEMPER
    expo = jnp.where(row == column, 0.0, jnp.exp(logits - 1.0 / SOFTMAX_TEMPER))
    e_own_ref[...] = expo
    sum_own_ref[...] = fold(expo)
    picked = jnp.where(partner == row, logits, 0.0)
    logits = scores(other_ref[...], unit) / SOFTMAX_TEMPER
    expo = jnp.exp(logits - 1.0 / SOFTMAX_TEMPER)
    e_other_ref[...] = expo
    sum_other_ref[...] = fold(expo)
    picked = picked + jnp.where(partner == row + ROWS, logits, 0.0)
    pos_ref[...] = jnp.sum(fold(picked), axis=0, keepdims=True)


def own_call(ids, unit, other, partner):
    f32 = jnp.float32
    return pl.pallas_call(
        own_kernel,
        out_shape=(
            jax.ShapeDtypeStruct((1, ROWS), jnp.int32),
            jax.ShapeDtypeStruct((ROWS, ROWS), f32),
            jax.ShapeDtypeStruct((ROWS, ROWS), f32),
            jax.ShapeDtypeStruct((ROWS, 128), f32),
            jax.ShapeDtypeStruct((ROWS, 128), f32),
            jax.ShapeDtypeStruct((1, 128), f32),
        ),
        in_specs=smem(1) + vmem(3),
        out_specs=tuple(vmem(6)),
        compiler_params=PARAMS,
        cost_estimate=pl.CostEstimate(flops=2 * 448 * ROWS * WIDTH, bytes_accessed=2 << 20, transcendentals=448 * ROWS),
        name="own_scores",
    )(ids, unit, other, partner)


def received(number, k):
    first = jnp.where(k == 0, 1, jnp.where(k == 1, 3, jnp.where(k == 2, 0, 2)))
    return (first, 3 - first, 3 - k)[number]


def pick(number, ids_ref):
    k, run = ids_ref[1], ids_ref[3]
    below, above = run % 16 == 15, run % 16 == 0
    end = (below & (k == 3)) | (above & (k == 0))
    mid = (below & (k == 2)) | (above & (k == 1))
    far = (below & (k == 1)) | (above & (k == 2))
    inner = jnp.where((k == 1) | (k == 2), 1, 0)
    if number == 2:
        return inner
    if number == 3:
        return jnp.where(end, 2, jnp.where(mid, 1, 0))
    if number == 4:
        return jnp.where(end, 1, jnp.where(far, 2, 0))
    return jnp.where(end, 2, jnp.where(mid, 3, inner))


def block_kernel(number_in, n_cand, last, *refs):
    ids_ref, unit_ref, other_ref, sum_own_ref, sum_other_ref = refs[:5]
    cands = refs[5 : 5 + n_cand]
    rest = refs[5 + n_cand :]
    if last:
        pos_ref, rest = rest[0], rest[1:]
    e_own_ref, e_other_ref = rest[:2]
    rest = rest[2:]
    if last:
        pay_ref, rest = rest[0], rest[1:]
    else:
        sum_own_out, sum_other_out = rest[:2]
        rest = rest[2:]
    k, core = ids_ref[1], ids_ref[2]
    steps = received(number_in % 3, k) - k
    if number_in > 2:
        steps = jnp.where(steps < 0, steps + 4, steps - 4)
    outside = steps == jnp.where(core == 0, -3, 3)
    if n_cand > 1:
        choice = pick(number_in, ids_ref)
        block_ref, rest = rest[0], rest[1:]
        block_ref[...] = cands[0][...]
        for number in range(1, n_cand):

            @pl.when(choice == number)
            def _(number=number):
                block_ref[...] = cands[number][...]
    else:
        block_ref = cands[0]
    block = block_ref[...]
    expo = jnp.exp(scores(unit_ref[...], block) / SOFTMAX_TEMPER - 1.0 / SOFTMAX_TEMPER)
    e_own_ref[...] = expo
    sum_own = sum_own_ref[...] + fold(expo)
    expo = jnp.exp(scores(other_ref[...], block) / SOFTMAX_TEMPER - 1.0 / SOFTMAX_TEMPER)
    expo = jnp.where(outside, 0.0, expo)
    e_other_ref[...] = expo
    sum_other = sum_other_ref[...] + fold(expo)
    if last:
        pay_ref[...] = jnp.zeros((8, 128), jnp.float32)
        for half, total in enumerate((sum_own, sum_other)):
            across = jnp.sum(jnp.transpose(total), axis=0, keepdims=True)
            pay_ref[2 * half : 2 * half + 1, :] = across[:, :128]
            pay_ref[2 * half + 1 : 2 * half + 2, : ROWS - 128] = across[:, 128:]
        pay_ref[4:5, :] = pos_ref[...]
    else:
        sum_own_out[...] = sum_own
        sum_other_out[...] = sum_other


def block_call(number_in, ids, unit, other, sums, cands, pos=None):
    f32 = jnp.float32
    last = pos is not None
    n = len(cands)
    shapes = [jax.ShapeDtypeStruct((ROWS, ROWS), f32)] * 2
    if last:
        shapes.append(jax.ShapeDtypeStruct((8, 128), f32))
    else:
        shapes += [jax.ShapeDtypeStruct((ROWS, 128), f32)] * 2
    if n > 1:
        shapes.append(jax.ShapeDtypeStruct((ROWS, WIDTH), jnp.bfloat16))
    operands = [unit, other, *sums, *cands] + ([pos] if last else [])

    def kernel(*refs):
        block_kernel(number_in, n, last, *refs)

    out = pl.pallas_call(
        kernel,
        out_shape=tuple(shapes),
        in_specs=smem(1) + vmem(len(operands)),
        out_specs=tuple(vmem(len(shapes))),
        compiler_params=PARAMS,
        cost_estimate=pl.CostEstimate(flops=2 * 448 * ROWS * WIDTH, bytes_accessed=2 << 20, transcendentals=448 * ROWS),
        name="block_scores",
    )(ids, *operands)
    block = out[-1] if n > 1 else cands[0]
    if last:
        return out[:2], out[2], block
    return out[:2], out[2:4], block


def denom_kernel(ids_ref, pay_ref, inv_ref, mine_ref, other_ref, edge_ref, loss_ref):
    y, k, core = ids_ref[0], ids_ref[1], ids_ref[2]
    pay = pay_ref[...].reshape(16, 2, 8, 128)
    lane = lax.broadcasted_iota(jnp.int32, (16, 2, 128), 2)
    part = lax.broadcasted_iota(jnp.int32, (16, 2, 128), 1)
    real = part * 128 + lane < ROWS
    first = jnp.where(real, pay[:, 0, 0:2] + pay[:, 1, 2:4], 1.0)
    second = jnp.where(real, pay[:, 1, 0:2] + pay[:, 0, 2:4], 1.0)
    total = jnp.log(first) + jnp.log(second)
    total = jnp.sum(total.reshape(32, 128), axis=0, keepdims=True)
    total = total - jnp.sum(pay[:, :, 4].reshape(32, 128), axis=0, keepdims=True)
    loss_ref[...] = jnp.broadcast_to(jnp.sum(total, axis=1, keepdims=True), (16, 128))
    first, second = 1.0 / first, 1.0 / second
    inv_ref[...] = jnp.where(core == 0, first, second)
    other_all = jnp.where(core == 0, second, first)
    chip = lax.broadcasted_iota(jnp.int32, (16, 2, 128), 0)
    here = chip == y * 4 + k
    mine_ref[...] = jnp.sum(jnp.where(here, inv_ref[...], 0.0), axis=0)
    other_ref[...] = jnp.sum(jnp.where(here, other_all, 0.0), axis=0)
    edge_ref[...] = inv_ref[pl.ds(jnp.where(y == 3, 12, 0), 4)]


def denom_call(ids, pay):
    f32 = jnp.float32
    return pl.pallas_call(
        denom_kernel,
        out_shape=(
            jax.ShapeDtypeStruct((16, 2, 128), f32),
            jax.ShapeDtypeStruct((2, 128), f32),
            jax.ShapeDtypeStruct((2, 128), f32),
            jax.ShapeDtypeStruct((4, 2, 128), f32),
            jax.ShapeDtypeStruct((16, 128), f32),
        ),
        in_specs=smem(1) + vmem(1),
        out_specs=tuple(vmem(5)),
        compiler_params=PARAMS,
        name="denoms",
    )(ids, pay)


def lanes(pair):
    return jnp.concatenate([pair[0:1, :], pair[1:2, : ROWS - 128]], axis=1)


def grad_kernel(shift, *refs):
    ids_ref, inv_ref, edge_ref, row_ref, partner_ref = refs[:5]
    expos, blocks = refs[5:12], refs[12:19]
    out_ref = refs[19]
    mine = lanes(row_ref[...])
    mine = jnp.transpose(jnp.broadcast_to(mine, (128, ROWS)))[:, 0:1]
    total = None
    y, k = ids_ref[0], ids_ref[1]
    for number in range(7):
        chip, line = k, y
        if number:
            chip = received((number - 1) % 3, k)
        if number > 3:
            line = y + jnp.where(chip < k, 1, -1)
        inside = inv_ref[pl.ds(jnp.clip(line, 0, 3) * 4 + chip, 1)]
        if number > 3:
            inside = jnp.where((line < 0) | (line > 3), edge_ref[pl.ds(chip, 1)], inside)
        column = lanes(inside[0])
        weight = expos[number][...] * (mine + column)
        if number == 0:
            row = lax.broadcasted_iota(jnp.int32, (ROWS, ROWS), 0) + shift
            weight = weight - jnp.where(partner_ref[...] == row, 2.0, 0.0)
        term = jnp.dot(weight.astype(jnp.bfloat16), blocks[number][...], preferred_element_type=jnp.float32)
        total = term if total is None else total + term
    out_ref[...] = total


def grad_call(shift, ids, inv, edge, row, partner, expos, blocks):
    def kernel(*refs):
        grad_kernel(shift, *refs)

    return pl.pallas_call(
        kernel,
        out_shape=jax.ShapeDtypeStruct((ROWS, WIDTH), jnp.float32),
        in_specs=smem(1) + vmem(18),
        out_specs=pl.BlockSpec(memory_space=pltpu.VMEM),
        compiler_params=PARAMS,
        cost_estimate=pl.CostEstimate(flops=2 * 7 * ROWS * ROWS * WIDTH, bytes_accessed=6 << 20, transcendentals=0),
        name="unit_gradient",
    )(ids, inv, edge, row, partner, *expos, *blocks)


def final_kernel(emb_ref, mine_ref, got_ref, out_ref):
    emb = emb_ref[...]
    norm = jnp.sqrt(jnp.sum(emb * emb, axis=1, keepdims=True) + 1e-06)
    unit32 = emb / norm
    unit_gradient = (mine_ref[...] + got_ref[...]) / SOFTMAX_TEMPER
    radial = jnp.sum(unit32 * unit_gradient, axis=1, keepdims=True)
    out_ref[...] = (unit_gradient - unit32 * radial) / norm


def final_call(emb, mine, got):
    spec = pl.BlockSpec((56, WIDTH), lambda i: (i, 0))
    return pl.pallas_call(
        final_kernel,
        out_shape=jax.ShapeDtypeStruct((ROWS, WIDTH), jnp.float32),
        grid=(4,),
        in_specs=[spec] * 3,
        out_specs=spec,
        compiler_params=PARAMS,
        cost_estimate=pl.CostEstimate(flops=10 * ROWS * WIDTH, bytes_accessed=16 * ROWS * WIDTH, transcendentals=0),
        name="final",
    )(emb, mine, got)


def send(value, name):
    return lax.ppermute(value, AXES, ROUTES[name])


def per_device(embeddings, partner):
    norm = jnp.sqrt(jnp.sum(embeddings * embeddings, axis=1, keepdims=True) + 1e-06)
    unit = (embeddings / norm).astype(jnp.bfloat16)

    run = lax.axis_index(("zh", "x", "y"))
    ids = jnp.stack([lax.axis_index(name) for name in DEV_AXES] + [run]).astype(jnp.int32)
    partner = partner.reshape(1, ROWS)

    r1 = send(unit, "P1")
    x1 = send(unit, "X1")
    other = lax.ppermute(after(unit, ids), ("core",), [(0, 1), (1, 0)])
    local, e_own, e_other, sum_own, sum_other, pos = own_call(ids, unit, other, partner)
    expos, blocks, sums = [(e_own, e_other)] + [None] * 6, [unit] + [None] * 6, (sum_own, sum_other)

    def add(number, cands):
        nonlocal sums
        last = number == 5
        pair, rest, block = block_call(number, ids, unit, other, sums, cands, pos if last else None)
        expos[number + 1] = pair
        blocks[number + 1] = block
        if last:
            return rest
        sums = rest

    r1 = after(r1, x1, sums[0])
    r2 = send(after(unit, r1), "P2")
    y1 = send(r1, "Y1")
    x2 = send(after(x1, r1), "X2")
    x3 = send(r1, "X3")
    add(0, [r1])
    r2 = after(r2, sums[0])
    y2 = send(after(r2, y1), "Y2")
    p3b = send(after(unit, r2), "P3b")
    p3a = send(after(r1, r2), "P3a")
    x4 = send(after(r2, x3), "X4")
    x6 = send(after(x2, r2), "X6")
    add(1, [r2])
    p3a = after(p3a, sums[0])
    p3b = after(p3b, sums[0])
    y3a = send(after(p3a, y2), "Y3a")
    y3b = send(after(p3b, y2), "Y3b")
    x5 = send(after(x3, p3a, p3b), "X5")
    add(2, [p3a, p3b])
    add(3, [y1, x2, x4])
    add(4, [y2, x3, x6])
    pay = add(5, [y3a, y3b, x1, x5])

    pays = lax.all_to_all(jnp.broadcast_to(pay[None], (32, 8, 128)), DEV_AXES, 0, 0)
    inv, mine_inv, other_inv, edge, loss = denom_call(ids, pays)
    losses = lax.all_to_all(loss, ("zh", "x"), 0, 0)
    edge = lax.ppermute(edge, AXES, EDGE)
    inv = after(inv, losses)
    for_other = grad_call(ROWS, ids, inv, edge, other_inv, local, [e[1] for e in expos], blocks)
    got = lax.ppermute(for_other, ("core",), [(0, 1), (1, 0)])
    mine = grad_call(0, ids, after(inv, for_other), edge, mine_inv, local, [e[0] for e in expos], blocks)
    grad = final_call(embeddings, mine, got)
    losses = after(losses, mine)
    loss = jnp.sum(losses[:, 0]) / (ROWS * 512) + 1.0 / SOFTMAX_TEMPER
    return (loss, grad)


def solution(mesh):
    split = Mesh(mesh.devices.reshape(SHAPE), AXES)
    in_specs = (P(AXES, None), P(AXES))
    out_specs = (P(), P(AXES, None))
    return jax.shard_map(per_device, mesh=split, in_specs=in_specs, out_specs=out_specs, check_vma=False)
```

```python
import jax
import jax.numpy as jnp
from jax import lax
from jax.experimental import pallas as pl
from jax.experimental.pallas import tpu as pltpu
from jax.sharding import Mesh
from jax.sharding import PartitionSpec as P

ROUNDS = 6
SOFTMAX_TEMPER = 0.1
AXES = ("zh", "x", "y", "zl", "core")
SHAPE = (4, 4, 4, 4, 2)
RUNS = 64
DEV_AXES = ("y", "zl", "core")
ROWS = 224
WIDTH = 1024

def crosses(run):
    return run % 16 == 15


def routes():
    names = ("P1", "P2", "P3a", "P3b", "Y1", "Y2", "Y3a", "Y3b", "X1", "X2", "X3", "X4", "X5", "X6")
    table = {name: [] for name in names}

    def chip(run, k):
        return (run % RUNS) * 4 + k

    def add(name, *pairs):
        for source, target in pairs:
            for core in (0, 1):
                table[name].append((2 * source + core, 2 * target + core))

    for run in range(RUNS):
        for name, moves in (
            ("P1", ((0, 2), (1, 0), (2, 3), (3, 1))),
            ("P2", ((1, 3), (2, 0), (0, 1), (3, 2))),
            ("P3a", ((2, 3), (1, 0))),
            ("P3b", ((1, 2), (2, 1))),
        ):
            add(name, *((chip(run, a), chip(run, b)) for a, b in moves))
        for name, ups, downs in (
            ("Y1", (0, 1), (2, 3)),
            ("Y2", (0, 2), (1, 3)),
            ("Y3a", (0,), (3,)),
            ("Y3b", (1,), (2,)),
        ):
            if not crosses(run):
                add(name, *((chip(run, k), chip(run + 1, k)) for k in ups))
            if not crosses(run - 1):
                add(name, *((chip(run, k), chip(run - 1, k)) for k in downs))
        if crosses(run):
            low = [chip(run, k) for k in range(4)]
            high = [chip(run + 1, k) for k in range(4)]
            for name in ("X1", "X3", "X4"):
                add(name, (low[3], high[0]), (high[0], low[3]))
            for name in ("X2", "X5"):
                add(name, (high[0], high[1]), (low[3], low[2]))
            add("X6", (high[1], high[2]), (low[2], low[1]))
    return table


ROUTES = routes()


def after(value, *others):
    return lax.optimization_barrier((value,) + others)[0]


def vmem(count):
    return [pl.BlockSpec(memory_space=pltpu.VMEM)] * count


def smem(count):
    return [pl.BlockSpec(memory_space=pltpu.SMEM)] * count


PARAMS = pltpu.CompilerParams(vmem_limit_bytes=12 * 1024 * 1024)


def scores(rows, columns):
    return lax.dot_general(rows, columns, (((1,), (1,)), ((), ())), preferred_element_type=jnp.float32)


def fold(values):
    tail = jnp.concatenate([values[:, 128:], jnp.zeros((ROWS, 256 - ROWS), jnp.float32)], axis=1)
    return values[:, :128] + tail


def own_kernel(ids_ref, unit_ref, other_ref, partner_ref, local_ref, e_own_ref, e_other_ref, sum_own_ref, sum_other_ref, pos_ref):
    unit = unit_ref[...]
    row = lax.broadcasted_iota(jnp.int32, (ROWS, ROWS), 0)
    column = lax.broadcasted_iota(jnp.int32, (ROWS, ROWS), 1)
    shift = ids_ref[2] * ROWS
    partner = partner_ref[...] - (ids_ref[3] * (8 * ROWS) + ids_ref[1] * (2 * ROWS) + shift)
    partner = jnp.where(partner < 0, partner + 2 * ROWS, partner)
    local_ref[...] = partner
    logits = scores(unit, unit) / SOFTMAX_TEMPER
    expo = jnp.where(row == column, 0.0, jnp.exp(logits - 1.0 / SOFTMAX_TEMPER))
    e_own_ref[...] = expo
    sum_own_ref[...] = fold(expo)
    picked = jnp.where(partner == row, logits, 0.0)
    logits = scores(other_ref[...], unit) / SOFTMAX_TEMPER
    expo = jnp.exp(logits - 1.0 / SOFTMAX_TEMPER)
    e_other_ref[...] = expo
    sum_other_ref[...] = fold(expo)
    picked = picked + jnp.where(partner == row + ROWS, logits, 0.0)
    pos_ref[...] = jnp.sum(fold(picked), axis=0, keepdims=True)


def own_call(ids, unit, other, partner):
    f32 = jnp.float32
    return pl.pallas_call(
        own_kernel,
        out_shape=(
            jax.ShapeDtypeStruct((1, ROWS), jnp.int32),
            jax.ShapeDtypeStruct((ROWS, ROWS), f32),
            jax.ShapeDtypeStruct((ROWS, ROWS), f32),
            jax.ShapeDtypeStruct((ROWS, 128), f32),
            jax.ShapeDtypeStruct((ROWS, 128), f32),
            jax.ShapeDtypeStruct((1, 128), f32),
        ),
        in_specs=smem(1) + vmem(3),
        out_specs=tuple(vmem(6)),
        compiler_params=PARAMS,
        cost_estimate=pl.CostEstimate(flops=2 * 448 * ROWS * WIDTH, bytes_accessed=2 << 20, transcendentals=448 * ROWS),
        name="own_scores",
    )(ids, unit, other, partner)


def received(number, k):
    first = jnp.where(k == 0, 1, jnp.where(k == 1, 3, jnp.where(k == 2, 0, 2)))
    return (first, 3 - first, 3 - k)[number]


def pick(number, ids_ref):
    k, run = ids_ref[1], ids_ref[3]
    below, above = run % 16 == 15, run % 16 == 0
    end = (below & (k == 3)) | (above & (k == 0))
    mid = (below & (k == 2)) | (above & (k == 1))
    far = (below & (k == 1)) | (above & (k == 2))
    inner = jnp.where((k == 1) | (k == 2), 1, 0)
    if number == 2:
        return inner
    if number == 3:
        return jnp.where(end, 2, jnp.where(mid, 1, 0))
    if number == 4:
        return jnp.where(end, 1, jnp.where(far, 2, 0))
    return jnp.where(end, 2, jnp.where(mid, 3, inner))


def block_kernel(number_in, n_cand, last, *refs):
    ids_ref, unit_ref, other_ref, sum_own_ref, sum_other_ref = refs[:5]
    cands = refs[5 : 5 + n_cand]
    rest = refs[5 + n_cand :]
    if last:
        pos_ref, rest = rest[0], rest[1:]
    e_own_ref, e_other_ref = rest[:2]
    rest = rest[2:]
    if last:
        pay_ref, rest = rest[0], rest[1:]
    else:
        sum_own_out, sum_other_out = rest[:2]
        rest = rest[2:]
    k, core = ids_ref[1], ids_ref[2]
    steps = received(number_in % 3, k) - k
    if number_in > 2:
        steps = jnp.where(steps < 0, steps + 4, steps - 4)
    outside = steps == jnp.where(core == 0, -3, 3)
    if n_cand > 1:
        choice = pick(number_in, ids_ref)
        block_ref, rest = rest[0], rest[1:]
        block_ref[...] = cands[0][...]
        for number in range(1, n_cand):

            @pl.when(choice == number)
            def _(number=number):
                block_ref[...] = cands[number][...]
    else:
        block_ref = cands[0]
    block = block_ref[...]
    expo = jnp.exp(scores(unit_ref[...], block) / SOFTMAX_TEMPER - 1.0 / SOFTMAX_TEMPER)
    e_own_ref[...] = expo
    sum_own = sum_own_ref[...] + fold(expo)
    expo = jnp.exp(scores(other_ref[...], block) / SOFTMAX_TEMPER - 1.0 / SOFTMAX_TEMPER)
    expo = jnp.where(outside, 0.0, expo)
    e_other_ref[...] = expo
    sum_other = sum_other_ref[...] + fold(expo)
    if last:
        pay_ref[...] = jnp.zeros((8, 128), jnp.float32)
        for half, total in enumerate((sum_own, sum_other)):
            across = jnp.sum(jnp.transpose(total), axis=0, keepdims=True)
            pay_ref[2 * half : 2 * half + 1, :] = across[:, :128]
            pay_ref[2 * half + 1 : 2 * half + 2, : ROWS - 128] = across[:, 128:]
        pay_ref[4:5, :] = pos_ref[...]
    else:
        sum_own_out[...] = sum_own
        sum_other_out[...] = sum_other


def block_call(number_in, ids, unit, other, sums, cands, pos=None):
    f32 = jnp.float32
    last = pos is not None
    n = len(cands)
    shapes = [jax.ShapeDtypeStruct((ROWS, ROWS), f32)] * 2
    if last:
        shapes.append(jax.ShapeDtypeStruct((8, 128), f32))
    else:
        shapes += [jax.ShapeDtypeStruct((ROWS, 128), f32)] * 2
    if n > 1:
        shapes.append(jax.ShapeDtypeStruct((ROWS, WIDTH), jnp.bfloat16))
    operands = [unit, other, *sums, *cands] + ([pos] if last else [])

    def kernel(*refs):
        block_kernel(number_in, n, last, *refs)

    out = pl.pallas_call(
        kernel,
        out_shape=tuple(shapes),
        in_specs=smem(1) + vmem(len(operands)),
        out_specs=tuple(vmem(len(shapes))),
        compiler_params=PARAMS,
        cost_estimate=pl.CostEstimate(flops=2 * 448 * ROWS * WIDTH, bytes_accessed=2 << 20, transcendentals=448 * ROWS),
        name="block_scores",
    )(ids, *operands)
    block = out[-1] if n > 1 else cands[0]
    if last:
        return out[:2], out[2], block
    return out[:2], out[2:4], block


def denom_kernel(ids_ref, pay_ref, inv_ref, mine_ref, other_ref, post_ref):
    y, k, core, group = ids_ref[0], ids_ref[1], ids_ref[2], ids_ref[3] // 4
    pay = pay_ref[...].reshape(16, 2, 8, 128)
    lane = lax.broadcasted_iota(jnp.int32, (16, 2, 128), 2)
    part = lax.broadcasted_iota(jnp.int32, (16, 2, 128), 1)
    real = part * 128 + lane < ROWS
    first = jnp.where(real, pay[:, 0, 0:2] + pay[:, 1, 2:4], 1.0)
    second = jnp.where(real, pay[:, 1, 0:2] + pay[:, 0, 2:4], 1.0)
    total = jnp.log(first) + jnp.log(second)
    total = jnp.sum(total.reshape(32, 128), axis=0, keepdims=True)
    total = total - jnp.sum(pay[:, :, 4].reshape(32, 128), axis=0, keepdims=True)
    total = jnp.sum(total, axis=1, keepdims=True)
    first, second = 1.0 / first, 1.0 / second
    inv = jnp.where(core == 0, first, second)
    other_all = jnp.where(core == 0, second, first)
    inv_ref[...] = inv
    here = lax.broadcasted_iota(jnp.int32, (16, 2, 128), 0) == y * 4 + k
    mine_ref[...] = jnp.sum(jnp.where(here, inv, 0.0), axis=0)
    other_ref[...] = jnp.sum(jnp.where(here, other_all, 0.0), axis=0)
    low = jnp.where(real[:4], inv[:4], total)
    high = jnp.where(real[:4], inv[12:], total)
    post_ref[...] = jnp.broadcast_to(low[None], (16, 4, 2, 128))
    post_ref[pl.ds((group + 1) % 16, 1)] = high[None]


def denom_call(ids, pay):
    f32 = jnp.float32
    return pl.pallas_call(
        denom_kernel,
        out_shape=(
            jax.ShapeDtypeStruct((16, 2, 128), f32),
            jax.ShapeDtypeStruct((2, 128), f32),
            jax.ShapeDtypeStruct((2, 128), f32),
            jax.ShapeDtypeStruct((16, 4, 2, 128), f32),
        ),
        in_specs=smem(1) + vmem(1),
        out_specs=tuple(vmem(4)),
        compiler_params=PARAMS,
        name="denoms",
    )(ids, pay)


def lanes(pair):
    return jnp.concatenate([pair[0:1, :], pair[1:2, : ROWS - 128]], axis=1)


def grad_kernel(shift, *refs):
    ids_ref, inv_ref, edge_ref, row_ref, partner_ref = refs[:5]
    expos, blocks = refs[5:12], refs[12:19]
    out_ref = refs[19]
    mine = lanes(row_ref[...])
    mine = jnp.transpose(jnp.broadcast_to(mine, (128, ROWS)))[:, 0:1]
    total = None
    y, k, group = ids_ref[0], ids_ref[1], ids_ref[3] // 4
    beside = jnp.where(y == 0, group + 15, group + 1) % 16
    for number in range(7):
        chip, line = k, y
        if number:
            chip = received((number - 1) % 3, k)
        if number > 3:
            line = y + jnp.where(chip < k, 1, -1)
        inside = inv_ref[pl.ds(jnp.clip(line, 0, 3) * 4 + chip, 1)]
        if number > 3:
            inside = jnp.where((line < 0) | (line > 3), edge_ref[pl.ds(beside, 1), pl.ds(chip, 1)][0], inside)
        column = lanes(inside[0])
        weight = expos[number][...] * (mine + column)
        if number == 0:
            row = lax.broadcasted_iota(jnp.int32, (ROWS, ROWS), 0) + shift
            weight = weight - jnp.where(partner_ref[...] == row, 2.0, 0.0)
        term = jnp.dot(weight.astype(jnp.bfloat16), blocks[number][...], preferred_element_type=jnp.float32)
        total = term if total is None else total + term
    out_ref[...] = total


def grad_call(shift, ids, inv, edge, row, partner, expos, blocks):
    def kernel(*refs):
        grad_kernel(shift, *refs)

    return pl.pallas_call(
        kernel,
        out_shape=jax.ShapeDtypeStruct((ROWS, WIDTH), jnp.float32),
        in_specs=smem(1) + vmem(18),
        out_specs=pl.BlockSpec(memory_space=pltpu.VMEM),
        compiler_params=PARAMS,
        cost_estimate=pl.CostEstimate(flops=2 * 7 * ROWS * ROWS * WIDTH, bytes_accessed=6 << 20, transcendentals=0),
        name="unit_gradient",
    )(ids, inv, edge, row, partner, *expos, *blocks)


def final_kernel(emb_ref, mine_ref, got_ref, out_ref):
    emb = emb_ref[...]
    norm = jnp.sqrt(jnp.sum(emb * emb, axis=1, keepdims=True) + 1e-06)
    unit32 = emb / norm
    unit_gradient = (mine_ref[...] + got_ref[...]) / SOFTMAX_TEMPER
    radial = jnp.sum(unit32 * unit_gradient, axis=1, keepdims=True)
    out_ref[...] = (unit_gradient - unit32 * radial) / norm


def final_call(emb, mine, got):
    spec = pl.BlockSpec((56, WIDTH), lambda i: (i, 0))
    return pl.pallas_call(
        final_kernel,
        out_shape=jax.ShapeDtypeStruct((ROWS, WIDTH), jnp.float32),
        grid=(4,),
        in_specs=[spec] * 3,
        out_specs=spec,
        compiler_params=PARAMS,
        cost_estimate=pl.CostEstimate(flops=10 * ROWS * WIDTH, bytes_accessed=16 * ROWS * WIDTH, transcendentals=0),
        name="final",
    )(emb, mine, got)


def send(value, name):
    return lax.ppermute(value, AXES, ROUTES[name])


def per_device(embeddings, partner):
    norm = jnp.sqrt(jnp.sum(embeddings * embeddings, axis=1, keepdims=True) + 1e-06)
    unit = (embeddings / norm).astype(jnp.bfloat16)

    run = lax.axis_index(("zh", "x", "y"))
    ids = jnp.stack([lax.axis_index(name) for name in DEV_AXES] + [run]).astype(jnp.int32)
    partner = partner.reshape(1, ROWS)

    r1 = send(unit, "P1")
    x1 = send(unit, "X1")
    other = lax.ppermute(after(unit, ids), ("core",), [(0, 1), (1, 0)])
    local, e_own, e_other, sum_own, sum_other, pos = own_call(ids, unit, other, partner)
    expos, blocks, sums = [(e_own, e_other)] + [None] * 6, [unit] + [None] * 6, (sum_own, sum_other)

    def add(number, cands):
        nonlocal sums
        last = number == 5
        pair, rest, block = block_call(number, ids, unit, other, sums, cands, pos if last else None)
        expos[number + 1] = pair
        blocks[number + 1] = block
        if last:
            return rest
        sums = rest

    r1 = after(r1, x1)
    r2 = send(after(unit, r1), "P2")
    y1 = send(r1, "Y1")
    x2 = send(after(x1, r1), "X2")
    x3 = send(r1, "X3")
    add(0, [r1])
    r2 = after(r2, sums[0])
    y2 = send(after(r2, y1), "Y2")
    p3b = send(after(unit, r2), "P3b")
    p3a = send(after(r1, r2), "P3a")
    x4 = send(after(r2, x3), "X4")
    x6 = send(after(x2, r2), "X6")
    add(1, [r2])
    p3a = after(p3a, sums[0])
    p3b = after(p3b, sums[0])
    y3a = send(after(p3a, y2), "Y3a")
    y3b = send(after(p3b, y2), "Y3b")
    x5 = send(after(x3, p3a, p3b), "X5")
    add(2, [p3a, p3b])
    add(3, [y1, x2, x4])
    add(4, [y2, x3, x6])
    pay = add(5, [y3a, y3b, x1, x5])

    pays = lax.all_to_all(jnp.broadcast_to(pay[None], (32, 8, 128)), DEV_AXES, 0, 0)
    inv, mine_inv, other_inv, post = denom_call(ids, pays)
    posts = lax.all_to_all(post, ("zh", "x"), 0, 0)
    for_other = grad_call(ROWS, ids, inv, posts, other_inv, local, [e[1] for e in expos], blocks)
    got = lax.ppermute(for_other, ("core",), [(0, 1), (1, 0)])
    mine = grad_call(0, ids, after(inv, for_other), posts, mine_inv, local, [e[0] for e in expos], blocks)
    grad = final_call(embeddings, mine, got)
    total = jnp.sum(after(posts, mine)[:, 0, 1, 127])
    loss = total / (ROWS * 512) + 1.0 / SOFTMAX_TEMPER
    return (loss, grad)


def solution(mesh):
    split = Mesh(mesh.devices.reshape(SHAPE), AXES)
    in_specs = (P(AXES, None), P(AXES))
    out_specs = (P(), P(AXES, None))
    return jax.shard_map(per_device, mesh=split, in_specs=in_specs, out_specs=out_specs, check_vma=False)
```

```python
import jax
import jax.numpy as jnp
from jax import lax
from jax.experimental import pallas as pl
from jax.experimental.pallas import tpu as pltpu
from jax.sharding import Mesh
from jax.sharding import PartitionSpec as P

ROUNDS = 6
SOFTMAX_TEMPER = 0.1
AXES = ("zh", "x", "y", "zl", "core")
SHAPE = (4, 4, 4, 4, 2)
RUNS = 64
DEV_AXES = ("y", "zl", "core")
ROWS = 224
WIDTH = 1024

def crosses(run):
    return run % 16 == 15


def routes():
    names = ("P1", "P2", "P3a", "P3b", "Y1", "Y2", "Y3a", "Y3b", "X1", "X2", "X3")
    table = {name: [] for name in names}

    def chip(run, k):
        return (run % RUNS) * 4 + k

    def add(name, *pairs):
        for source, target in pairs:
            for core in (0, 1):
                table[name].append((2 * source + core, 2 * target + core))

    for run in range(RUNS):
        for name, moves in (
            ("P1", ((0, 2), (1, 0), (2, 3), (3, 1))),
            ("P2", ((1, 3), (2, 0), (0, 1), (3, 2))),
            ("P3a", ((2, 3), (1, 0))),
            ("P3b", ((1, 2), (2, 1))),
        ):
            add(name, *((chip(run, a), chip(run, b)) for a, b in moves))
        for name, ups, downs in (
            ("Y1", (0, 1), (2, 3)),
            ("Y2", (0, 2), (1, 3)),
            ("Y3a", (0,), (3,)),
            ("Y3b", (1,), (2,)),
        ):
            if not crosses(run):
                add(name, *((chip(run, k), chip(run + 1, k)) for k in ups))
            if not crosses(run - 1):
                add(name, *((chip(run, k), chip(run - 1, k)) for k in downs))
        if crosses(run):
            low = [chip(run, k) for k in range(4)]
            high = [chip(run + 1, k) for k in range(4)]
            for name in ("X1", "X2", "P3b"):
                add(name, (low[3], high[0]), (high[0], low[3]))
            for name in ("P3a", "X3"):
                add(name, (high[0], high[1]), (low[3], low[2]))
            add("X3", (high[1], high[2]), (low[2], low[1]))
    return table


ROUTES = routes()


def after(value, *others):
    return lax.optimization_barrier((value,) + others)[0]


def vmem(count):
    return [pl.BlockSpec(memory_space=pltpu.VMEM)] * count


def smem(count):
    return [pl.BlockSpec(memory_space=pltpu.SMEM)] * count


PARAMS = pltpu.CompilerParams(vmem_limit_bytes=8 * 1024 * 1024)


def scores(rows, columns):
    return lax.dot_general(rows, columns, (((1,), (1,)), ((), ())), preferred_element_type=jnp.float32)


def fold(values):
    tail = jnp.concatenate([values[:, 128:], jnp.zeros((ROWS, 256 - ROWS), jnp.float32)], axis=1)
    return values[:, :128] + tail


def own_kernel(ids_ref, unit_ref, other_ref, partner_ref, local_ref, e_own_ref, e_other_ref, sum_own_ref, sum_other_ref, pos_ref):
    unit = unit_ref[...]
    row = lax.broadcasted_iota(jnp.int32, (ROWS, ROWS), 0)
    column = lax.broadcasted_iota(jnp.int32, (ROWS, ROWS), 1)
    shift = ids_ref[2] * ROWS
    partner = partner_ref[...] - (ids_ref[3] * (8 * ROWS) + ids_ref[1] * (2 * ROWS) + shift)
    partner = jnp.where(partner < 0, partner + 2 * ROWS, partner)
    local_ref[...] = partner
    logits = scores(unit, unit) / SOFTMAX_TEMPER
    expo = jnp.where(row == column, 0.0, jnp.exp(logits - 1.0 / SOFTMAX_TEMPER))
    e_own_ref[...] = expo
    sum_own_ref[...] = fold(expo)
    picked = jnp.where(partner == row, logits, 0.0)
    logits = scores(other_ref[...], unit) / SOFTMAX_TEMPER
    expo = jnp.exp(logits - 1.0 / SOFTMAX_TEMPER)
    e_other_ref[...] = expo
    sum_other_ref[...] = fold(expo)
    picked = picked + jnp.where(partner == row + ROWS, logits, 0.0)
    pos_ref[...] = jnp.sum(fold(picked), axis=0, keepdims=True)


def own_call(ids, unit, other, partner):
    f32 = jnp.float32
    return pl.pallas_call(
        own_kernel,
        out_shape=(
            jax.ShapeDtypeStruct((1, ROWS), jnp.int32),
            jax.ShapeDtypeStruct((ROWS, ROWS), f32),
            jax.ShapeDtypeStruct((ROWS, ROWS), f32),
            jax.ShapeDtypeStruct((ROWS, 128), f32),
            jax.ShapeDtypeStruct((ROWS, 128), f32),
            jax.ShapeDtypeStruct((1, 128), f32),
        ),
        in_specs=smem(1) + vmem(3),
        out_specs=tuple(vmem(6)),
        compiler_params=PARAMS,
        cost_estimate=pl.CostEstimate(flops=2 * 448 * ROWS * WIDTH, bytes_accessed=2 << 20, transcendentals=448 * ROWS),
        name="own_scores",
    )(ids, unit, other, partner)


def received(number, k):
    first = jnp.where(k == 0, 1, jnp.where(k == 1, 3, jnp.where(k == 2, 0, 2)))
    return (first, 3 - first, 3 - k)[number]


def pick(number, ids_ref):
    k, run = ids_ref[1], ids_ref[3]
    below, above = run % 16 == 15, run % 16 == 0
    end = (below & (k == 3)) | (above & (k == 0))
    mid = (below & (k == 2)) | (above & (k == 1))
    far = (below & (k == 1)) | (above & (k == 2))
    inner = jnp.where((k == 1) | (k == 2), 1, 0)
    if number == 2:
        return inner
    if number == 3:
        return jnp.where(end, 2, jnp.where(mid, 1, 0))
    if number == 4:
        return jnp.where(end, 1, jnp.where(far, 2, 0))
    return jnp.where(end, 2, jnp.where(mid, 3, inner))


def block_kernel(number_in, n_cand, last, *refs):
    ids_ref, unit_ref, other_ref, sum_own_ref, sum_other_ref = refs[:5]
    cands = refs[5 : 5 + n_cand]
    rest = refs[5 + n_cand :]
    if last:
        pos_ref, rest = rest[0], rest[1:]
    e_own_ref, e_other_ref = rest[:2]
    rest = rest[2:]
    if last:
        pay_ref, rest = rest[0], rest[1:]
    else:
        sum_own_out, sum_other_out = rest[:2]
        rest = rest[2:]
    k, core = ids_ref[1], ids_ref[2]
    steps = received(number_in % 3, k) - k
    if number_in > 2:
        steps = jnp.where(steps < 0, steps + 4, steps - 4)
    outside = steps == jnp.where(core == 0, -3, 3)
    if n_cand > 1:
        choice = pick(number_in, ids_ref)
        block_ref, rest = rest[0], rest[1:]
        block_ref[...] = cands[0][...]
        for number in range(1, n_cand):

            @pl.when(choice == number)
            def _(number=number):
                block_ref[...] = cands[number][...]
    else:
        block_ref = cands[0]
    block = block_ref[...]
    expo = jnp.exp(scores(unit_ref[...], block) / SOFTMAX_TEMPER - 1.0 / SOFTMAX_TEMPER)
    e_own_ref[...] = expo
    sum_own = sum_own_ref[...] + fold(expo)
    expo = jnp.exp(scores(other_ref[...], block) / SOFTMAX_TEMPER - 1.0 / SOFTMAX_TEMPER)
    expo = jnp.where(outside, 0.0, expo)
    e_other_ref[...] = expo
    sum_other = sum_other_ref[...] + fold(expo)
    if last:
        pay_ref[...] = jnp.zeros((8, 128), jnp.float32)
        for half, total in enumerate((sum_own, sum_other)):
            across = jnp.sum(jnp.transpose(total), axis=0, keepdims=True)
            pay_ref[2 * half : 2 * half + 1, :] = across[:, :128]
            pay_ref[2 * half + 1 : 2 * half + 2, : ROWS - 128] = across[:, 128:]
        pay_ref[4:5, :] = pos_ref[...]
    else:
        sum_own_out[...] = sum_own
        sum_other_out[...] = sum_other


def block_call(number_in, ids, unit, other, sums, cands, pos=None):
    f32 = jnp.float32
    last = pos is not None
    n = len(cands)
    shapes = [jax.ShapeDtypeStruct((ROWS, ROWS), f32)] * 2
    if last:
        shapes.append(jax.ShapeDtypeStruct((8, 128), f32))
    else:
        shapes += [jax.ShapeDtypeStruct((ROWS, 128), f32)] * 2
    if n > 1:
        shapes.append(jax.ShapeDtypeStruct((ROWS, WIDTH), jnp.bfloat16))
    operands = [unit, other, *sums, *cands] + ([pos] if last else [])

    def kernel(*refs):
        block_kernel(number_in, n, last, *refs)

    out = pl.pallas_call(
        kernel,
        out_shape=tuple(shapes),
        in_specs=smem(1) + vmem(len(operands)),
        out_specs=tuple(vmem(len(shapes))),
        compiler_params=PARAMS,
        cost_estimate=pl.CostEstimate(flops=2 * 448 * ROWS * WIDTH, bytes_accessed=2 << 20, transcendentals=448 * ROWS),
        name="block_scores",
    )(ids, *operands)
    block = out[-1] if n > 1 else cands[0]
    if last:
        return out[:2], out[2], block
    return out[:2], out[2:4], block


def denom_kernel(ids_ref, pay_ref, inv_ref, mine_ref, other_ref, post_ref):
    y, k, core, group = ids_ref[0], ids_ref[1], ids_ref[2], ids_ref[3] // 4
    pay = pay_ref[...].reshape(16, 2, 8, 128)
    lane = lax.broadcasted_iota(jnp.int32, (16, 2, 128), 2)
    part = lax.broadcasted_iota(jnp.int32, (16, 2, 128), 1)
    real = part * 128 + lane < ROWS
    first = jnp.where(real, pay[:, 0, 0:2] + pay[:, 1, 2:4], 1.0)
    second = jnp.where(real, pay[:, 1, 0:2] + pay[:, 0, 2:4], 1.0)
    total = jnp.log(first) + jnp.log(second)
    total = jnp.sum(total.reshape(32, 128), axis=0, keepdims=True)
    total = total - jnp.sum(pay[:, :, 4].reshape(32, 128), axis=0, keepdims=True)
    total = jnp.sum(total, axis=1, keepdims=True)
    first, second = 1.0 / first, 1.0 / second
    inv = jnp.where(core == 0, first, second)
    other_all = jnp.where(core == 0, second, first)
    inv_ref[...] = inv
    here = lax.broadcasted_iota(jnp.int32, (16, 2, 128), 0) == y * 4 + k
    mine_ref[...] = jnp.sum(jnp.where(here, inv, 0.0), axis=0)
    other_ref[...] = jnp.sum(jnp.where(here, other_all, 0.0), axis=0)
    low = jnp.where(real[:4], inv[:4], total)
    high = jnp.where(real[:4], inv[12:], total)
    post_ref[...] = jnp.broadcast_to(low[None], (16, 4, 2, 128))
    post_ref[pl.ds((group + 1) % 16, 1)] = high[None]


def denom_call(ids, pay):
    f32 = jnp.float32
    return pl.pallas_call(
        denom_kernel,
        out_shape=(
            jax.ShapeDtypeStruct((16, 2, 128), f32),
            jax.ShapeDtypeStruct((2, 128), f32),
            jax.ShapeDtypeStruct((2, 128), f32),
            jax.ShapeDtypeStruct((16, 4, 2, 128), f32),
        ),
        in_specs=smem(1) + vmem(1),
        out_specs=tuple(vmem(4)),
        compiler_params=PARAMS,
        name="denoms",
    )(ids, pay)


def lanes(pair):
    return jnp.concatenate([pair[0:1, :], pair[1:2, : ROWS - 128]], axis=1)


def grad_kernel(shift, *refs):
    ids_ref, inv_ref, edge_ref, row_ref, partner_ref = refs[:5]
    expos, blocks = refs[5:12], refs[12:19]
    out_ref = refs[19]
    if shift:
        posted = edge_ref[:, 0, 1, :]
        lane = lax.broadcasted_iota(jnp.int32, (16, 128), 1)
        total = jnp.sum(jnp.where(lane == 127, posted, 0.0), axis=0, keepdims=True)
        total = jnp.sum(total, axis=1, keepdims=True)
        refs[20][...] = total / (ROWS * 512) + 1.0 / SOFTMAX_TEMPER
    mine = lanes(row_ref[...])
    mine = jnp.transpose(jnp.broadcast_to(mine, (128, ROWS)))[:, 0:1]
    total = None
    y, k, group = ids_ref[0], ids_ref[1], ids_ref[3] // 4
    beside = jnp.where(y == 0, group + 15, group + 1) % 16
    for number in range(7):
        chip, line = k, y
        if number:
            chip = received((number - 1) % 3, k)
        if number > 3:
            line = y + jnp.where(chip < k, 1, -1)
        inside = inv_ref[pl.ds(jnp.clip(line, 0, 3) * 4 + chip, 1)]
        if number > 3:
            inside = jnp.where((line < 0) | (line > 3), edge_ref[pl.ds(beside, 1), pl.ds(chip, 1)][0], inside)
        column = lanes(inside[0])
        weight = expos[number][...] * (mine + column)
        if number == 0:
            row = lax.broadcasted_iota(jnp.int32, (ROWS, ROWS), 0) + shift
            weight = weight - jnp.where(partner_ref[...] == row, 2.0, 0.0)
        term = jnp.dot(weight.astype(jnp.bfloat16), blocks[number][...], preferred_element_type=jnp.float32)
        total = term if total is None else total + term
    out_ref[...] = total


def grad_call(shift, ids, inv, edge, row, partner, expos, blocks):
    shapes = [jax.ShapeDtypeStruct((ROWS, WIDTH), jnp.float32)]
    if shift:
        shapes.append(jax.ShapeDtypeStruct((1, 1), jnp.float32))

    def kernel(*refs):
        grad_kernel(shift, *refs)

    return pl.pallas_call(
        kernel,
        out_shape=tuple(shapes),
        in_specs=smem(1) + vmem(18),
        out_specs=tuple(vmem(len(shapes))),
        compiler_params=PARAMS,
        cost_estimate=pl.CostEstimate(flops=2 * 7 * ROWS * ROWS * WIDTH, bytes_accessed=6 << 20, transcendentals=0),
        name="unit_gradient",
    )(ids, inv, edge, row, partner, *expos, *blocks)


def final_kernel(emb_ref, mine_ref, got_ref, out_ref):
    emb = emb_ref[...]
    norm = jnp.sqrt(jnp.sum(emb * emb, axis=1, keepdims=True) + 1e-06)
    unit32 = emb / norm
    unit_gradient = (mine_ref[...] + got_ref[...]) / SOFTMAX_TEMPER
    radial = jnp.sum(unit32 * unit_gradient, axis=1, keepdims=True)
    out_ref[...] = (unit_gradient - unit32 * radial) / norm


def final_call(emb, mine, got):
    return pl.pallas_call(
        final_kernel,
        out_shape=jax.ShapeDtypeStruct((ROWS, WIDTH), jnp.float32),
        in_specs=vmem(3),
        out_specs=pl.BlockSpec(memory_space=pltpu.VMEM),
        compiler_params=PARAMS,
        cost_estimate=pl.CostEstimate(flops=10 * ROWS * WIDTH, bytes_accessed=16 * ROWS * WIDTH, transcendentals=0),
        name="final",
    )(emb, mine, got)


def send(value, name):
    return lax.ppermute(value, AXES, ROUTES[name])


def per_device(embeddings, partner):
    norm = jnp.sqrt(jnp.sum(embeddings * embeddings, axis=1, keepdims=True) + 1e-06)
    unit = (embeddings / norm).astype(jnp.bfloat16)

    run = lax.axis_index(("zh", "x", "y"))
    ids = jnp.stack([lax.axis_index(name) for name in DEV_AXES] + [run]).astype(jnp.int32)
    partner = partner.reshape(1, ROWS)

    r1 = send(unit, "P1")
    x1 = send(after(unit, ids), "X1")
    other = lax.ppermute(after(unit, ids), ("core",), [(0, 1), (1, 0)])
    local, e_own, e_other, sum_own, sum_other, pos = own_call(ids, unit, other, partner)
    expos, blocks, sums = [(e_own, e_other)] + [None] * 6, [unit] + [None] * 6, (sum_own, sum_other)

    def add(number, cands):
        nonlocal sums
        last = number == 5
        pair, rest, block = block_call(number, ids, unit, other, sums, cands, pos if last else None)
        expos[number + 1] = pair
        blocks[number + 1] = block
        if last:
            return rest
        sums = rest

    outer = (ids[1] == 0) | (ids[1] == 3)
    end = ((ids[3] % 16 == 15) & (ids[1] == 3)) | ((ids[3] % 16 == 0) & (ids[1] == 0))
    r1 = after(r1, x1)
    r2 = send(after(unit, r1), "P2")
    y1 = send(r1, "Y1")
    x2 = send(r1, "X2")
    add(0, [r1])
    r2 = after(r2, sums[0])
    y2 = send(r2, "Y2")
    p3b = send(jnp.where(outer, r2, unit), "P3b")
    p3a = send(jnp.where(end, x1, after(r1, r2)), "P3a")
    add(1, [after(r2, y1, x2)])
    p3a = after(p3a, sums[0])
    p3b = after(p3b, sums[0])
    y3a = send(after(p3a, y2), "Y3a")
    y3b = send(after(p3b, y2), "Y3b")
    x3 = send(jnp.where(outer, x2, p3a), "X3")
    add(2, [p3a, p3b])
    add(3, [y1, p3a, p3b])
    add(4, [y2, x2, x3])
    pay = add(5, [y3a, y3b, x1, x3])

    pays = lax.all_to_all(jnp.broadcast_to(pay[None], (32, 8, 128)), DEV_AXES, 0, 0)
    inv, mine_inv, other_inv, post = denom_call(ids, pays)
    posts = lax.all_to_all(post, ("zh", "x"), 0, 0)
    for_other, loss = grad_call(ROWS, ids, inv, posts, other_inv, local, [e[1] for e in expos], blocks)
    got = lax.ppermute(for_other, ("core",), [(0, 1), (1, 0)])
    (mine,) = grad_call(0, ids, after(inv, for_other), posts, mine_inv, local, [e[0] for e in expos], blocks)
    grad = final_call(embeddings, mine, got)
    loss = loss.reshape(())
    return (loss, grad)


def solution(mesh):
    split = Mesh(mesh.devices.reshape(SHAPE), AXES)
    in_specs = (P(AXES, None), P(AXES))
    out_specs = (P(), P(AXES, None))
    return jax.shard_map(per_device, mesh=split, in_specs=in_specs, out_specs=out_specs, check_vma=False)
```

```python
import jax
import jax.numpy as jnp
from jax import lax
from jax.experimental import pallas as pl
from jax.experimental.pallas import tpu as pltpu
from jax.sharding import Mesh
from jax.sharding import PartitionSpec as P

ROUNDS = 6
SOFTMAX_TEMPER = 0.1
AXES = ("zh", "x", "y", "zl", "core")
SHAPE = (4, 4, 4, 4, 2)
RUNS = 64
DEV_AXES = ("y", "zl", "core")
ROWS = 224
WIDTH = 1024

def crosses(run):
    return run % 16 == 15


def routes():
    names = ("P1", "P2", "P3a", "P3b", "Y1", "Y2", "Y3a", "Y3b", "X1", "X2", "X3", "X4", "X5")
    table = {name: [] for name in names}

    def chip(run, k):
        return (run % RUNS) * 4 + k

    def add(name, *pairs):
        for source, target in pairs:
            for core in (0, 1):
                table[name].append((2 * source + core, 2 * target + core))

    for run in range(RUNS):
        for name, moves in (
            ("P1", ((0, 2), (1, 0), (2, 3), (3, 1))),
            ("P2", ((1, 3), (2, 0), (0, 1), (3, 2))),
            ("P3a", ((2, 3), (1, 0))),
            ("P3b", ((1, 2), (2, 1))),
        ):
            add(name, *((chip(run, a), chip(run, b)) for a, b in moves))
        for name, ups, downs in (
            ("Y1", (0, 1), (2, 3)),
            ("Y2", (0, 2), (1, 3)),
            ("Y3a", (0,), (3,)),
            ("Y3b", (1,), (2,)),
        ):
            if not crosses(run):
                add(name, *((chip(run, k), chip(run + 1, k)) for k in ups))
            if not crosses(run - 1):
                add(name, *((chip(run, k), chip(run - 1, k)) for k in downs))
        if crosses(run):
            low = [chip(run, k) for k in range(4)]
            high = [chip(run + 1, k) for k in range(4)]
            for name in ("X1", "X3", "X4"):
                add(name, (low[3], high[0]), (high[0], low[3]))
            for name in ("X2", "X5"):
                add(name, (high[0], high[1]), (low[3], low[2]))
            add("X5", (high[1], high[2]), (low[2], low[1]))
    return table


ROUTES = routes()


def after(value, *others):
    return lax.optimization_barrier((value,) + others)[0]


def vmem(count):
    return [pl.BlockSpec(memory_space=pltpu.VMEM)] * count


def smem(count):
    return [pl.BlockSpec(memory_space=pltpu.SMEM)] * count


PARAMS = pltpu.CompilerParams(vmem_limit_bytes=12 * 1024 * 1024)


def scores(rows, columns):
    return lax.dot_general(rows, columns, (((1,), (1,)), ((), ())), preferred_element_type=jnp.float32)


def fold(values):
    tail = jnp.concatenate([values[:, 128:], jnp.zeros((ROWS, 256 - ROWS), jnp.float32)], axis=1)
    return values[:, :128] + tail


def own_kernel(ids_ref, unit_ref, other_ref, partner_ref, local_ref, e_own_ref, e_other_ref, sum_own_ref, sum_other_ref, pos_ref):
    unit = unit_ref[...]
    row = lax.broadcasted_iota(jnp.int32, (ROWS, ROWS), 0)
    column = lax.broadcasted_iota(jnp.int32, (ROWS, ROWS), 1)
    shift = ids_ref[2] * ROWS
    partner = partner_ref[...] - (ids_ref[3] * (8 * ROWS) + ids_ref[1] * (2 * ROWS) + shift)
    partner = jnp.where(partner < 0, partner + 2 * ROWS, partner)
    local_ref[...] = partner
    logits = scores(unit, unit) / SOFTMAX_TEMPER
    expo = jnp.where(row == column, 0.0, jnp.exp(logits - 1.0 / SOFTMAX_TEMPER))
    e_own_ref[...] = expo
    sum_own_ref[...] = fold(expo)
    picked = jnp.where(partner == row, logits, 0.0)
    logits = scores(other_ref[...], unit) / SOFTMAX_TEMPER
    expo = jnp.exp(logits - 1.0 / SOFTMAX_TEMPER)
    e_other_ref[...] = expo
    sum_other_ref[...] = fold(expo)
    picked = picked + jnp.where(partner == row + ROWS, logits, 0.0)
    pos_ref[...] = jnp.sum(fold(picked), axis=0, keepdims=True)


def own_call(ids, unit, other, partner):
    f32 = jnp.float32
    return pl.pallas_call(
        own_kernel,
        out_shape=(
            jax.ShapeDtypeStruct((1, ROWS), jnp.int32),
            jax.ShapeDtypeStruct((ROWS, ROWS), f32),
            jax.ShapeDtypeStruct((ROWS, ROWS), f32),
            jax.ShapeDtypeStruct((ROWS, 128), f32),
            jax.ShapeDtypeStruct((ROWS, 128), f32),
            jax.ShapeDtypeStruct((1, 128), f32),
        ),
        in_specs=smem(1) + vmem(3),
        out_specs=tuple(vmem(6)),
        compiler_params=PARAMS,
        cost_estimate=pl.CostEstimate(flops=2 * 448 * ROWS * WIDTH, bytes_accessed=2 << 20, transcendentals=448 * ROWS),
        name="own_scores",
    )(ids, unit, other, partner)


def received(number, k):
    first = jnp.where(k == 0, 1, jnp.where(k == 1, 3, jnp.where(k == 2, 0, 2)))
    return (first, 3 - first, 3 - k)[number]


def pick(number, ids_ref):
    k, run = ids_ref[1], ids_ref[3]
    below, above = run % 16 == 15, run % 16 == 0
    end = (below & (k == 3)) | (above & (k == 0))
    mid = (below & (k == 2)) | (above & (k == 1))
    far = (below & (k == 1)) | (above & (k == 2))
    inner = jnp.where((k == 1) | (k == 2), 1, 0)
    if number == 2:
        return inner
    if number == 3:
        return jnp.where(end, 2, jnp.where(mid, 1, 0))
    if number == 4:
        return jnp.where(end, 1, jnp.where(far, 2, 0))
    return jnp.where(end, 2, jnp.where(mid, 3, inner))


def block_kernel(number_in, n_cand, last, *refs):
    ids_ref, unit_ref, other_ref, sum_own_ref, sum_other_ref = refs[:5]
    cands = refs[5 : 5 + n_cand]
    rest = refs[5 + n_cand :]
    if last:
        pos_ref, rest = rest[0], rest[1:]
    e_own_ref, e_other_ref = rest[:2]
    rest = rest[2:]
    if last:
        pay_ref, rest = rest[0], rest[1:]
    else:
        sum_own_out, sum_other_out = rest[:2]
        rest = rest[2:]
    k, core = ids_ref[1], ids_ref[2]
    steps = received(number_in % 3, k) - k
    if number_in > 2:
        steps = jnp.where(steps < 0, steps + 4, steps - 4)
    outside = steps == jnp.where(core == 0, -3, 3)
    if n_cand > 1:
        choice = pick(number_in, ids_ref)
        block_ref, rest = rest[0], rest[1:]
        block_ref[...] = cands[0][...]
        for number in range(1, n_cand):

            @pl.when(choice == number)
            def _(number=number):
                block_ref[...] = cands[number][...]
    else:
        block_ref = cands[0]
    block = block_ref[...]
    expo = jnp.exp(scores(unit_ref[...], block) / SOFTMAX_TEMPER - 1.0 / SOFTMAX_TEMPER)
    e_own_ref[...] = expo
    sum_own = sum_own_ref[...] + fold(expo)
    expo = jnp.exp(scores(other_ref[...], block) / SOFTMAX_TEMPER - 1.0 / SOFTMAX_TEMPER)
    expo = jnp.where(outside, 0.0, expo)
    e_other_ref[...] = expo
    sum_other = sum_other_ref[...] + fold(expo)
    if last:
        positive = jnp.broadcast_to(jnp.sum(pos_ref[...], axis=1, keepdims=True), (1, 256 - ROWS))
        rows = []
        for total in (sum_own, sum_other):
            across = jnp.sum(jnp.transpose(total), axis=0, keepdims=True)
            rows += [across[:, :128], jnp.concatenate([across[:, 128:], positive], axis=1)]
        pay_ref[...] = jnp.broadcast_to(jnp.concatenate(rows, axis=0)[None], (32, 4, 128))
    else:
        sum_own_out[...] = sum_own
        sum_other_out[...] = sum_other


def block_call(number_in, ids, unit, other, sums, cands, pos=None):
    f32 = jnp.float32
    last = pos is not None
    n = len(cands)
    shapes = [jax.ShapeDtypeStruct((ROWS, ROWS), f32)] * 2
    if last:
        shapes.append(jax.ShapeDtypeStruct((32, 4, 128), f32))
    else:
        shapes += [jax.ShapeDtypeStruct((ROWS, 128), f32)] * 2
    if n > 1:
        shapes.append(jax.ShapeDtypeStruct((ROWS, WIDTH), jnp.bfloat16))
    operands = [unit, other, *sums, *cands] + ([pos] if last else [])

    def kernel(*refs):
        block_kernel(number_in, n, last, *refs)

    out = pl.pallas_call(
        kernel,
        out_shape=tuple(shapes),
        in_specs=smem(1) + vmem(len(operands)),
        out_specs=tuple(vmem(len(shapes))),
        compiler_params=PARAMS,
        cost_estimate=pl.CostEstimate(flops=2 * 448 * ROWS * WIDTH, bytes_accessed=2 << 20, transcendentals=448 * ROWS),
        name="block_scores",
    )(ids, *operands)
    block = out[-1] if n > 1 else cands[0]
    if last:
        return out[:2], out[2], block
    return out[:2], out[2:4], block


def choose_kernel(ids_ref, outer_ref, inner_ref, out_ref):
    outer = (ids_ref[1] == 0) | (ids_ref[1] == 3)

    @pl.when(outer)
    def _():
        out_ref[...] = outer_ref[...]

    @pl.when(jnp.logical_not(outer))
    def _():
        out_ref[...] = inner_ref[...]


def choose_call(ids, outer, inner):
    return pl.pallas_call(
        choose_kernel,
        out_shape=jax.ShapeDtypeStruct((ROWS, WIDTH), jnp.bfloat16),
        in_specs=smem(1) + vmem(2),
        out_specs=pl.BlockSpec(memory_space=pltpu.VMEM),
        compiler_params=PARAMS,
        name="choose",
    )(ids, outer, inner)


def denom_kernel(ids_ref, pay_ref, inv_ref, mine_ref, other_ref, post_ref):
    y, k, core, group = ids_ref[0], ids_ref[1], ids_ref[2], ids_ref[3] // 4
    pay = pay_ref[...].reshape(16, 2, 4, 128)
    lane = lax.broadcasted_iota(jnp.int32, (16, 2, 128), 2)
    part = lax.broadcasted_iota(jnp.int32, (16, 2, 128), 1)
    real = part * 128 + lane < ROWS
    first = jnp.where(real, pay[:, 0, 0:2] + pay[:, 1, 2:4], 1.0)
    second = jnp.where(real, pay[:, 1, 0:2] + pay[:, 0, 2:4], 1.0)
    total = jnp.log(first) + jnp.log(second)
    total = jnp.sum(total.reshape(32, 128), axis=0, keepdims=True)
    last = lax.broadcasted_iota(jnp.int32, (1, 128), 1) == 127
    positive = jnp.sum(pay[:, :, 1].reshape(32, 128), axis=0, keepdims=True)
    total = jnp.sum(total - jnp.where(last, positive, 0.0), axis=1, keepdims=True)
    first, second = 1.0 / first, 1.0 / second
    inv = jnp.where(core == 0, first, second)
    other_all = jnp.where(core == 0, second, first)
    inv_ref[...] = inv
    here = lax.broadcasted_iota(jnp.int32, (16, 2, 128), 0) == y * 4 + k
    mine_ref[...] = jnp.sum(jnp.where(here, inv, 0.0), axis=0)
    other_ref[...] = jnp.sum(jnp.where(here, other_all, 0.0), axis=0)
    low = jnp.where(real[:4], inv[:4], total)
    high = jnp.where(real[:4], inv[12:], total)
    post_ref[...] = jnp.broadcast_to(low[None], (16, 4, 2, 128))
    post_ref[pl.ds((group + 1) % 16, 1)] = high[None]


def denom_call(ids, pay):
    f32 = jnp.float32
    return pl.pallas_call(
        denom_kernel,
        out_shape=(
            jax.ShapeDtypeStruct((16, 2, 128), f32),
            jax.ShapeDtypeStruct((2, 128), f32),
            jax.ShapeDtypeStruct((2, 128), f32),
            jax.ShapeDtypeStruct((16, 4, 2, 128), f32),
        ),
        in_specs=smem(1) + vmem(1),
        out_specs=tuple(vmem(4)),
        compiler_params=PARAMS,
        name="denoms",
    )(ids, pay)


def lanes(pair):
    return jnp.concatenate([pair[0:1, :], pair[1:2, : ROWS - 128]], axis=1)


def grad_kernel(shift, *refs):
    ids_ref, inv_ref, edge_ref, row_ref, partner_ref = refs[:5]
    expos, blocks = refs[5:12], refs[12:19]
    out_ref = refs[19]
    if shift:
        posted = edge_ref[:, 0, 1, :]
        lane = lax.broadcasted_iota(jnp.int32, (16, 128), 1)
        total = jnp.sum(jnp.where(lane == 127, posted, 0.0), axis=0, keepdims=True)
        total = jnp.sum(total, axis=1, keepdims=True)
        refs[20][...] = total / (ROWS * 512) + 1.0 / SOFTMAX_TEMPER
    mine = lanes(row_ref[...])
    mine = jnp.transpose(jnp.broadcast_to(mine, (128, ROWS)))[:, 0:1]
    total = None
    y, k, group = ids_ref[0], ids_ref[1], ids_ref[3] // 4
    beside = jnp.where(y == 0, group + 15, group + 1) % 16
    for number in range(7):
        chip, line = k, y
        if number:
            chip = received((number - 1) % 3, k)
        if number > 3:
            line = y + jnp.where(chip < k, 1, -1)
        inside = inv_ref[pl.ds(jnp.clip(line, 0, 3) * 4 + chip, 1)]
        if number > 3:
            inside = jnp.where((line < 0) | (line > 3), edge_ref[pl.ds(beside, 1), pl.ds(chip, 1)][0], inside)
        column = lanes(inside[0])
        weight = expos[number][...] * (mine + column)
        if number == 0:
            row = lax.broadcasted_iota(jnp.int32, (ROWS, ROWS), 0) + shift
            weight = weight - jnp.where(partner_ref[...] == row, 2.0, 0.0)
        term = jnp.dot(weight.astype(jnp.bfloat16), blocks[number][...], preferred_element_type=jnp.float32)
        total = term if total is None else total + term
    out_ref[...] = total


def grad_call(shift, ids, inv, edge, row, partner, expos, blocks):
    shapes = [jax.ShapeDtypeStruct((ROWS, WIDTH), jnp.float32)]
    if shift:
        shapes.append(jax.ShapeDtypeStruct((1, 1), jnp.float32))

    def kernel(*refs):
        grad_kernel(shift, *refs)

    return pl.pallas_call(
        kernel,
        out_shape=tuple(shapes),
        in_specs=smem(1) + vmem(18),
        out_specs=tuple(vmem(len(shapes))),
        compiler_params=PARAMS,
        cost_estimate=pl.CostEstimate(flops=2 * 7 * ROWS * ROWS * WIDTH, bytes_accessed=6 << 20, transcendentals=0),
        name="unit_gradient",
    )(ids, inv, edge, row, partner, *expos, *blocks)


def final_kernel(emb_ref, mine_ref, got_ref, out_ref):
    emb = emb_ref[...]
    norm = jnp.sqrt(jnp.sum(emb * emb, axis=1, keepdims=True) + 1e-06)
    unit32 = emb / norm
    unit_gradient = (mine_ref[...] + got_ref[...]) / SOFTMAX_TEMPER
    radial = jnp.sum(unit32 * unit_gradient, axis=1, keepdims=True)
    out_ref[...] = (unit_gradient - unit32 * radial) / norm


def final_call(emb, mine, got):
    return pl.pallas_call(
        final_kernel,
        out_shape=jax.ShapeDtypeStruct((ROWS, WIDTH), jnp.float32),
        in_specs=vmem(3),
        out_specs=pl.BlockSpec(memory_space=pltpu.VMEM),
        compiler_params=PARAMS,
        cost_estimate=pl.CostEstimate(flops=10 * ROWS * WIDTH, bytes_accessed=16 * ROWS * WIDTH, transcendentals=0),
        name="final",
    )(emb, mine, got)


def send(value, name):
    return lax.ppermute(value, AXES, ROUTES[name])


def per_device(embeddings, partner):
    norm = jnp.sqrt(jnp.sum(embeddings * embeddings, axis=1, keepdims=True) + 1e-06)
    unit = (embeddings / norm).astype(jnp.bfloat16)

    run = lax.axis_index(("zh", "x", "y"))
    ids = jnp.stack([lax.axis_index(name) for name in DEV_AXES] + [run]).astype(jnp.int32)
    partner = partner.reshape(1, ROWS)

    r1 = send(unit, "P1")
    x1 = send(unit, "X1")
    other = lax.ppermute(after(unit, ids), ("core",), [(0, 1), (1, 0)])
    local, e_own, e_other, sum_own, sum_other, pos = own_call(ids, unit, other, partner)
    expos, blocks, sums = [(e_own, e_other)] + [None] * 6, [unit] + [None] * 6, (sum_own, sum_other)

    def add(number, cands):
        nonlocal sums
        last = number == 5
        pair, rest, block = block_call(number, ids, unit, other, sums, cands, pos if last else None)
        expos[number + 1] = pair
        blocks[number + 1] = block
        if last:
            return rest
        sums = rest

    r2 = send(after(unit, r1), "P2")
    y1 = send(r1, "Y1")
    x2 = send(after(x1, r1), "X2")
    x3 = send(r1, "X3")
    add(0, [r1])
    r2 = after(r2, sums[0])
    y2 = send(after(r2, y1), "Y2")
    p3b = send(after(unit, r2), "P3b")
    p3a = send(after(r1, r2), "P3a")
    x4 = send(after(r2, x3), "X4")
    x5 = send(choose_call(ids, x3, after(x2, r2)), "X5")
    add(1, [r2])
    p3a = after(p3a, sums[0])
    p3b = after(p3b, sums[0])
    y3a = send(after(p3a, y2), "Y3a")
    y3b = send(after(p3b, y2), "Y3b")
    add(2, [p3a, p3b])
    add(3, [y1, x2, x4])
    add(4, [y2, x3, x5])
    pay = add(5, [y3a, y3b, x1, x5])

    pays = lax.all_to_all(pay, DEV_AXES, 0, 0)
    inv, mine_inv, other_inv, post = denom_call(ids, pays)
    posts = lax.all_to_all(post, ("zh", "x"), 0, 0)
    for_other, loss = grad_call(ROWS, ids, inv, posts, other_inv, local, [e[1] for e in expos], blocks)
    got = lax.ppermute(for_other, ("core",), [(0, 1), (1, 0)])
    (mine,) = grad_call(0, ids, after(inv, for_other), posts, mine_inv, local, [e[0] for e in expos], blocks)
    grad = final_call(embeddings, mine, got)
    loss = loss.reshape(())
    return (loss, grad)


def solution(mesh):
    split = Mesh(mesh.devices.reshape(SHAPE), AXES)
    in_specs = (P(AXES, None), P(AXES))
    out_specs = (P(), P(AXES, None))
    return jax.shard_map(per_device, mesh=split, in_specs=in_specs, out_specs=out_specs, check_vma=False)
```

```python
import jax
import jax.numpy as jnp
from jax import lax
from jax.experimental import pallas as pl
from jax.experimental.pallas import tpu as pltpu
from jax.sharding import Mesh
from jax.sharding import PartitionSpec as P

ROUNDS = 6
SOFTMAX_TEMPER = 0.1
AXES = ("zh", "x", "y", "zl", "core")
SHAPE = (4, 4, 4, 4, 2)
RUNS = 64
DEV_AXES = ("y", "zl", "core")
ROWS = 224
WIDTH = 1024

def crosses(run):
    return run % 16 == 15


def routes():
    names = ("P1a", "P1b", "P2", "P3a", "P3b", "Y1", "Y2", "Y3a", "Y3b", "X1", "X2", "X3", "X4", "X5")
    table = {name: [] for name in names}

    def chip(run, k):
        return (run % RUNS) * 4 + k

    def add(name, *pairs, cores=(0, 1)):
        for source, target in pairs:
            for core in cores:
                table[name].append((2 * source + core, 2 * target + core))

    for run in range(RUNS):
        for name, moves in (
            ("P2", ((1, 3), (2, 0), (0, 1), (3, 2))),
            ("P3a", ((2, 3), (1, 0))),
            ("P3b", ((1, 2), (2, 1))),
        ):
            add(name, *((chip(run, a), chip(run, b)) for a, b in moves))
        for name, core in (("P1a", 0), ("P1b", 1)):
            add(name, *((chip(run, a), chip(run, b)) for a, b in ((0, 2), (1, 0), (2, 3), (3, 1))), cores=(core,))
        for name, ups, downs in (
            ("Y1", (0, 1), (2, 3)),
            ("Y2", (0, 2), (1, 3)),
            ("Y3a", (0,), (3,)),
            ("Y3b", (1,), (2,)),
        ):
            if not crosses(run):
                add(name, *((chip(run, k), chip(run + 1, k)) for k in ups))
            if not crosses(run - 1):
                add(name, *((chip(run, k), chip(run - 1, k)) for k in downs))
        if crosses(run):
            low = [chip(run, k) for k in range(4)]
            high = [chip(run + 1, k) for k in range(4)]
            for name in ("X1", "X3", "X4"):
                add(name, (low[3], high[0]), (high[0], low[3]))
            for name in ("X2", "X5"):
                add(name, (high[0], high[1]), (low[3], low[2]))
            add("X5", (high[1], high[2]), (low[2], low[1]))
    return table


ROUTES = routes()


def after(value, *others):
    return lax.optimization_barrier((value,) + others)[0]


def vmem(count):
    return [pl.BlockSpec(memory_space=pltpu.VMEM)] * count


def smem(count):
    return [pl.BlockSpec(memory_space=pltpu.SMEM)] * count


PARAMS = pltpu.CompilerParams(vmem_limit_bytes=12 * 1024 * 1024)


def scores(rows, columns):
    return lax.dot_general(rows, columns, (((1,), (1,)), ((), ())), preferred_element_type=jnp.float32)


def fold(values):
    tail = jnp.concatenate([values[:, 128:], jnp.zeros((ROWS, 256 - ROWS), jnp.float32)], axis=1)
    return values[:, :128] + tail


def own_kernel(ids_ref, unit_ref, other_ref, partner_ref, local_ref, e_own_ref, e_other_ref, sum_own_ref, sum_other_ref, pos_ref):
    unit = unit_ref[...]
    row = lax.broadcasted_iota(jnp.int32, (ROWS, ROWS), 0)
    column = lax.broadcasted_iota(jnp.int32, (ROWS, ROWS), 1)
    shift = ids_ref[2] * ROWS
    partner = partner_ref[...] - (ids_ref[3] * (8 * ROWS) + ids_ref[1] * (2 * ROWS) + shift)
    partner = jnp.where(partner < 0, partner + 2 * ROWS, partner)
    local_ref[...] = partner
    logits = scores(unit, unit) / SOFTMAX_TEMPER
    expo = jnp.where(row == column, 0.0, jnp.exp(logits - 1.0 / SOFTMAX_TEMPER))
    e_own_ref[...] = expo
    sum_own_ref[...] = fold(expo)
    picked = jnp.where(partner == row, logits, 0.0)
    logits = scores(other_ref[...], unit) / SOFTMAX_TEMPER
    expo = jnp.exp(logits - 1.0 / SOFTMAX_TEMPER)
    e_other_ref[...] = expo
    sum_other_ref[...] = fold(expo)
    picked = picked + jnp.where(partner == row + ROWS, logits, 0.0)
    pos_ref[...] = jnp.sum(fold(picked), axis=0, keepdims=True)


def own_call(ids, unit, other, partner):
    f32 = jnp.float32
    return pl.pallas_call(
        own_kernel,
        out_shape=(
            jax.ShapeDtypeStruct((1, ROWS), jnp.int32),
            jax.ShapeDtypeStruct((ROWS, ROWS), f32),
            jax.ShapeDtypeStruct((ROWS, ROWS), f32),
            jax.ShapeDtypeStruct((ROWS, 128), f32),
            jax.ShapeDtypeStruct((ROWS, 128), f32),
            jax.ShapeDtypeStruct((1, 128), f32),
        ),
        in_specs=smem(1) + vmem(3),
        out_specs=tuple(vmem(6)),
        compiler_params=PARAMS,
        cost_estimate=pl.CostEstimate(flops=2 * 448 * ROWS * WIDTH, bytes_accessed=2 << 20, transcendentals=448 * ROWS),
        name="own_scores",
    )(ids, unit, other, partner)


def received(number, k):
    first = jnp.where(k == 0, 1, jnp.where(k == 1, 3, jnp.where(k == 2, 0, 2)))
    return (first, 3 - first, 3 - k)[number]


def pick(number, ids_ref):
    k, run = ids_ref[1], ids_ref[3]
    below, above = run % 16 == 15, run % 16 == 0
    end = (below & (k == 3)) | (above & (k == 0))
    mid = (below & (k == 2)) | (above & (k == 1))
    far = (below & (k == 1)) | (above & (k == 2))
    inner = jnp.where((k == 1) | (k == 2), 1, 0)
    if number == 2:
        return inner
    if number == 3:
        return jnp.where(end, 2, jnp.where(mid, 1, 0))
    if number == 4:
        return jnp.where(end, 1, jnp.where(far, 2, 0))
    return jnp.where(end, 2, jnp.where(mid, 3, inner))


def block_kernel(number_in, n_cand, last, *refs):
    ids_ref, unit_ref, other_ref, sum_own_ref, sum_other_ref = refs[:5]
    cands = refs[5 : 5 + n_cand]
    rest = refs[5 + n_cand :]
    if last:
        pos_ref, rest = rest[0], rest[1:]
    e_own_ref, e_other_ref = rest[:2]
    rest = rest[2:]
    if last:
        pay_ref, rest = rest[0], rest[1:]
    else:
        sum_own_out, sum_other_out = rest[:2]
        rest = rest[2:]
    k, core = ids_ref[1], ids_ref[2]
    steps = received(number_in % 3, k) - k
    if number_in > 2:
        steps = jnp.where(steps < 0, steps + 4, steps - 4)
    outside = steps == jnp.where(core == 0, -3, 3)
    if n_cand > 1:
        choice = pick(number_in, ids_ref)
        block_ref, rest = rest[0], rest[1:]
        block_ref[...] = cands[0][...]
        for number in range(1, n_cand):

            @pl.when(choice == number)
            def _(number=number):
                block_ref[...] = cands[number][...]
    else:
        block_ref = cands[0]
    block = block_ref[...]
    expo = jnp.exp(scores(unit_ref[...], block) / SOFTMAX_TEMPER - 1.0 / SOFTMAX_TEMPER)
    e_own_ref[...] = expo
    sum_own = sum_own_ref[...] + fold(expo)
    expo = jnp.exp(scores(other_ref[...], block) / SOFTMAX_TEMPER - 1.0 / SOFTMAX_TEMPER)
    expo = jnp.where(outside, 0.0, expo)
    e_other_ref[...] = expo
    sum_other = sum_other_ref[...] + fold(expo)
    if last:
        positive = jnp.broadcast_to(jnp.sum(pos_ref[...], axis=1, keepdims=True), (1, 256 - ROWS))
        rows = []
        for total in (sum_own, sum_other):
            across = jnp.sum(jnp.transpose(total), axis=0, keepdims=True)
            rows += [across[:, :128], jnp.concatenate([across[:, 128:], positive], axis=1)]
        pay_ref[...] = jnp.broadcast_to(jnp.concatenate(rows, axis=0)[None], (32, 4, 128))
    else:
        sum_own_out[...] = sum_own
        sum_other_out[...] = sum_other


def block_call(number_in, ids, unit, other, sums, cands, pos=None):
    f32 = jnp.float32
    last = pos is not None
    n = len(cands)
    shapes = [jax.ShapeDtypeStruct((ROWS, ROWS), f32)] * 2
    if last:
        shapes.append(jax.ShapeDtypeStruct((32, 4, 128), f32))
    else:
        shapes += [jax.ShapeDtypeStruct((ROWS, 128), f32)] * 2
    if n > 1:
        shapes.append(jax.ShapeDtypeStruct((ROWS, WIDTH), jnp.bfloat16))
    operands = [unit, other, *sums, *cands] + ([pos] if last else [])

    def kernel(*refs):
        block_kernel(number_in, n, last, *refs)

    out = pl.pallas_call(
        kernel,
        out_shape=tuple(shapes),
        in_specs=smem(1) + vmem(len(operands)),
        out_specs=tuple(vmem(len(shapes))),
        compiler_params=PARAMS,
        cost_estimate=pl.CostEstimate(flops=2 * 448 * ROWS * WIDTH, bytes_accessed=2 << 20, transcendentals=448 * ROWS),
        name="block_scores",
    )(ids, *operands)
    block = out[-1] if n > 1 else cands[0]
    if last:
        return out[:2], out[2], block
    return out[:2], out[2:4], block


def choose_call(by_core, ids, first, second):
    def kernel(ids_ref, first_ref, second_ref, out_ref):
        is_first = ids_ref[2] == 0 if by_core else (ids_ref[1] == 0) | (ids_ref[1] == 3)

        @pl.when(is_first)
        def _():
            out_ref[...] = first_ref[...]

        @pl.when(jnp.logical_not(is_first))
        def _():
            out_ref[...] = second_ref[...]

    return pl.pallas_call(
        kernel,
        out_shape=jax.ShapeDtypeStruct((ROWS, WIDTH), jnp.bfloat16),
        in_specs=smem(1) + vmem(2),
        out_specs=pl.BlockSpec(memory_space=pltpu.VMEM),
        compiler_params=PARAMS,
        name="choose",
    )(ids, first, second)


def denom_kernel(ids_ref, pay_ref, inv_ref, mine_ref, other_ref, post_ref):
    y, k, core, group = ids_ref[0], ids_ref[1], ids_ref[2], ids_ref[3] // 4
    pay = pay_ref[...].reshape(16, 2, 4, 128)
    lane = lax.broadcasted_iota(jnp.int32, (16, 2, 128), 2)
    part = lax.broadcasted_iota(jnp.int32, (16, 2, 128), 1)
    real = part * 128 + lane < ROWS
    first = jnp.where(real, pay[:, 0, 0:2] + pay[:, 1, 2:4], 1.0)
    second = jnp.where(real, pay[:, 1, 0:2] + pay[:, 0, 2:4], 1.0)
    total = jnp.log(first) + jnp.log(second)
    total = jnp.sum(total.reshape(32, 128), axis=0, keepdims=True)
    last = lax.broadcasted_iota(jnp.int32, (1, 128), 1) == 127
    positive = jnp.sum(pay[:, :, 1].reshape(32, 128), axis=0, keepdims=True)
    total = jnp.sum(total - jnp.where(last, positive, 0.0), axis=1, keepdims=True)
    first, second = 1.0 / first, 1.0 / second
    inv = jnp.where(core == 0, first, second)
    other_all = jnp.where(core == 0, second, first)
    inv_ref[...] = inv
    here = lax.broadcasted_iota(jnp.int32, (16, 2, 128), 0) == y * 4 + k
    mine_ref[...] = jnp.sum(jnp.where(here, inv, 0.0), axis=0)
    other_ref[...] = jnp.sum(jnp.where(here, other_all, 0.0), axis=0)
    low = jnp.where(real[:4], inv[:4], total)
    high = jnp.where(real[:4], inv[12:], total)
    post_ref[...] = jnp.broadcast_to(low[None], (16, 4, 2, 128))
    post_ref[pl.ds((group + 1) % 16, 1)] = high[None]


def denom_call(ids, pay):
    f32 = jnp.float32
    return pl.pallas_call(
        denom_kernel,
        out_shape=(
            jax.ShapeDtypeStruct((16, 2, 128), f32),
            jax.ShapeDtypeStruct((2, 128), f32),
            jax.ShapeDtypeStruct((2, 128), f32),
            jax.ShapeDtypeStruct((16, 4, 2, 128), f32),
        ),
        in_specs=smem(1) + vmem(1),
        out_specs=tuple(vmem(4)),
        compiler_params=PARAMS,
        name="denoms",
    )(ids, pay)


def lanes(pair):
    return jnp.concatenate([pair[0:1, :], pair[1:2, : ROWS - 128]], axis=1)


def grad_kernel(shift, *refs):
    ids_ref, inv_ref, edge_ref, row_ref, partner_ref = refs[:5]
    expos, blocks = refs[5:12], refs[12:19]
    out_ref = refs[19]
    if not shift:
        posted = edge_ref[:, 0, 1, :]
        lane = lax.broadcasted_iota(jnp.int32, (16, 128), 1)
        total = jnp.sum(jnp.where(lane == 127, posted, 0.0), axis=0, keepdims=True)
        total = jnp.sum(total, axis=1, keepdims=True)
        refs[20][...] = total / (ROWS * 512) + 1.0 / SOFTMAX_TEMPER
    mine = lanes(row_ref[...])
    mine = jnp.transpose(jnp.broadcast_to(mine, (128, ROWS)))[:, 0:1]
    total = None
    y, k, group = ids_ref[0], ids_ref[1], ids_ref[3] // 4
    beside = jnp.where(y == 0, group + 15, group + 1) % 16
    for number in range(7):
        chip, line = k, y
        if number:
            chip = received((number - 1) % 3, k)
        if number > 3:
            line = y + jnp.where(chip < k, 1, -1)
        inside = inv_ref[pl.ds(jnp.clip(line, 0, 3) * 4 + chip, 1)]
        if number > 3:
            inside = jnp.where((line < 0) | (line > 3), edge_ref[pl.ds(beside, 1), pl.ds(chip, 1)][0], inside)
        column = lanes(inside[0])
        weight = expos[number][...] * (mine + column)
        if number == 0:
            row = lax.broadcasted_iota(jnp.int32, (ROWS, ROWS), 0) + shift
            weight = weight - jnp.where(partner_ref[...] == row, 2.0, 0.0)
        term = jnp.dot(weight.astype(jnp.bfloat16), blocks[number][...], preferred_element_type=jnp.float32)
        total = term if total is None else total + term
    out_ref[...] = total


def grad_call(shift, ids, inv, edge, row, partner, expos, blocks):
    shapes = [jax.ShapeDtypeStruct((ROWS, WIDTH), jnp.float32)]
    if not shift:
        shapes.append(jax.ShapeDtypeStruct((1, 1), jnp.float32))

    def kernel(*refs):
        grad_kernel(shift, *refs)

    return pl.pallas_call(
        kernel,
        out_shape=tuple(shapes),
        in_specs=smem(1) + vmem(18),
        out_specs=tuple(vmem(len(shapes))),
        compiler_params=PARAMS,
        cost_estimate=pl.CostEstimate(flops=2 * 7 * ROWS * ROWS * WIDTH, bytes_accessed=6 << 20, transcendentals=0),
        name="unit_gradient",
    )(ids, inv, edge, row, partner, *expos, *blocks)


def final_kernel(emb_ref, mine_ref, got_ref, out_ref):
    emb = emb_ref[...]
    norm = jnp.sqrt(jnp.sum(emb * emb, axis=1, keepdims=True) + 1e-06)
    unit32 = emb / norm
    unit_gradient = (mine_ref[...] + got_ref[...]) / SOFTMAX_TEMPER
    radial = jnp.sum(unit32 * unit_gradient, axis=1, keepdims=True)
    out_ref[...] = (unit_gradient - unit32 * radial) / norm


def final_call(emb, mine, got):
    return pl.pallas_call(
        final_kernel,
        out_shape=jax.ShapeDtypeStruct((ROWS, WIDTH), jnp.float32),
        in_specs=vmem(3),
        out_specs=pl.BlockSpec(memory_space=pltpu.VMEM),
        compiler_params=PARAMS,
        cost_estimate=pl.CostEstimate(flops=10 * ROWS * WIDTH, bytes_accessed=16 * ROWS * WIDTH, transcendentals=0),
        name="final",
    )(emb, mine, got)


def send(value, name):
    return lax.ppermute(value, AXES, ROUTES[name])


def per_device(embeddings, partner):
    norm = jnp.sqrt(jnp.sum(embeddings * embeddings, axis=1, keepdims=True) + 1e-06)
    unit = (embeddings / norm).astype(jnp.bfloat16)

    run = lax.axis_index(("zh", "x", "y"))
    ids = jnp.stack([lax.axis_index(name) for name in DEV_AXES] + [run]).astype(jnp.int32)
    partner = partner.reshape(1, ROWS)

    p1b = send(unit, "P1b")
    x1 = send(unit, "X1")
    other = lax.ppermute(after(unit, ids), ("core",), [(0, 1), (1, 0)])
    local, e_own, e_other, sum_own, sum_other, pos = own_call(ids, unit, other, partner)
    expos, blocks, sums = [(e_own, e_other)] + [None] * 6, [unit] + [None] * 6, (sum_own, sum_other)

    def add(number, cands):
        nonlocal sums
        last = number == 5
        pair, rest, block = block_call(number, ids, unit, other, sums, cands, pos if last else None)
        expos[number + 1] = pair
        blocks[number + 1] = block
        if last:
            return rest
        sums = rest

    p1a = send(after(unit, sums[0]), "P1a")
    r2 = send(after(unit, p1a, p1b), "P2")
    r1 = choose_call(True, ids, p1a, p1b)
    y1 = send(r1, "Y1")
    x2 = send(after(x1, r1), "X2")
    x3 = send(r1, "X3")
    add(0, [r1])
    r2 = after(r2, sums[0])
    y2 = send(after(r2, y1), "Y2")
    p3b = send(after(unit, r2), "P3b")
    p3a = send(after(r1, r2), "P3a")
    x4 = send(after(r2, x3), "X4")
    x5 = send(choose_call(False, ids, x3, after(x2, r2)), "X5")
    add(1, [r2])
    p3a = after(p3a, sums[0])
    p3b = after(p3b, sums[0])
    y3a = send(after(p3a, y2), "Y3a")
    y3b = send(after(p3b, y2), "Y3b")
    add(2, [p3a, p3b])
    add(3, [y1, x2, x4])
    add(4, [y2, x3, x5])
    pay = add(5, [y3a, y3b, x1, x5])

    pays = lax.all_to_all(pay, DEV_AXES, 0, 0)
    inv, mine_inv, other_inv, post = denom_call(ids, pays)
    posts = lax.all_to_all(post, ("zh", "x"), 0, 0)
    (for_other,) = grad_call(ROWS, ids, inv, posts, other_inv, local, [e[1] for e in expos], blocks)
    got = lax.ppermute(for_other, ("core",), [(0, 1), (1, 0)])
    mine, loss = grad_call(0, ids, after(inv, for_other), posts, mine_inv, local, [e[0] for e in expos], blocks)
    grad = final_call(embeddings, mine, got)
    loss = loss.reshape(())
    return (loss, grad)


def solution(mesh):
    split = Mesh(mesh.devices.reshape(SHAPE), AXES)
    in_specs = (P(AXES, None), P(AXES))
    out_specs = (P(), P(AXES, None))
    return jax.shard_map(per_device, mesh=split, in_specs=in_specs, out_specs=out_specs, check_vma=False)
```

```python
import jax
import jax.numpy as jnp
from jax import lax
from jax.experimental import pallas as pl
from jax.experimental.pallas import tpu as pltpu
from jax.sharding import Mesh
from jax.sharding import PartitionSpec as P

ROUNDS = 6
SOFTMAX_TEMPER = 0.1
AXES = ("zh", "x", "y", "zl", "core")
SHAPE = (4, 4, 4, 4, 2)
RUNS = 64
DEV_AXES = ("y", "zl", "core")
ROWS = 224
WIDTH = 1024

def crosses(run):
    return run % 16 == 15


def routes():
    names = ("P1a", "P1b", "P2", "P3a", "P3b", "Y1", "Y2", "Y3a", "Y3b", "X1", "X2", "X3", "X4", "X5")
    table = {name: [] for name in names}

    def chip(run, k):
        return (run % RUNS) * 4 + k

    def add(name, *pairs, cores=(0, 1)):
        for source, target in pairs:
            for core in cores:
                table[name].append((2 * source + core, 2 * target + core))

    for run in range(RUNS):
        for name, moves in (
            ("P2", ((1, 3), (2, 0), (0, 1), (3, 2))),
            ("P3a", ((2, 3), (1, 0))),
            ("P3b", ((1, 2), (2, 1))),
        ):
            add(name, *((chip(run, a), chip(run, b)) for a, b in moves))
        for name, core in (("P1a", 0), ("P1b", 1)):
            add(name, *((chip(run, a), chip(run, b)) for a, b in ((0, 2), (1, 0), (2, 3), (3, 1))), cores=(core,))
        for name, ups, downs in (
            ("Y1", (0, 1), (2, 3)),
            ("Y2", (0, 2), (1, 3)),
            ("Y3a", (0,), (3,)),
            ("Y3b", (1,), (2,)),
        ):
            if not crosses(run):
                add(name, *((chip(run, k), chip(run + 1, k)) for k in ups))
            if not crosses(run - 1):
                add(name, *((chip(run, k), chip(run - 1, k)) for k in downs))
        if crosses(run):
            low = [chip(run, k) for k in range(4)]
            high = [chip(run + 1, k) for k in range(4)]
            for name in ("X1", "X3", "X4"):
                add(name, (low[3], high[0]), (high[0], low[3]))
            for name in ("X2", "X5"):
                add(name, (high[0], high[1]), (low[3], low[2]))
            add("X5", (high[1], high[2]), (low[2], low[1]))
    return table


ROUTES = routes()


def after(value, *others):
    return lax.optimization_barrier((value,) + others)[0]


def vmem(count):
    return [pl.BlockSpec(memory_space=pltpu.VMEM)] * count


def smem(count):
    return [pl.BlockSpec(memory_space=pltpu.SMEM)] * count


PARAMS = pltpu.CompilerParams(vmem_limit_bytes=12 * 1024 * 1024)


def scores(rows, columns):
    return lax.dot_general(rows, columns, (((1,), (1,)), ((), ())), preferred_element_type=jnp.float32)


def fold(values):
    tail = jnp.concatenate([values[:, 128:], jnp.zeros((ROWS, 256 - ROWS), jnp.float32)], axis=1)
    return values[:, :128] + tail


def own_kernel(ids_ref, unit_ref, partner_ref, local_ref, expo_ref, sum_ref, pos_ref):
    unit = unit_ref[...]
    row = lax.broadcasted_iota(jnp.int32, (ROWS, ROWS), 0)
    column = lax.broadcasted_iota(jnp.int32, (ROWS, ROWS), 1)
    partner = partner_ref[...] - (ids_ref[3] * (8 * ROWS) + ids_ref[1] * (2 * ROWS) + ids_ref[2] * ROWS)
    partner = jnp.where(partner < 0, partner + 2 * ROWS, partner)
    local_ref[...] = partner
    logits = scores(unit, unit) / SOFTMAX_TEMPER
    expo = jnp.where(row == column, 0.0, jnp.exp(logits - 1.0 / SOFTMAX_TEMPER))
    expo_ref[...] = expo
    sum_ref[...] = fold(expo)
    pos_ref[...] = jnp.sum(fold(jnp.where(partner == row, logits, 0.0)), axis=0, keepdims=True)


def own_call(ids, unit, partner):
    f32 = jnp.float32
    return pl.pallas_call(
        own_kernel,
        out_shape=(
            jax.ShapeDtypeStruct((1, ROWS), jnp.int32),
            jax.ShapeDtypeStruct((ROWS, ROWS), f32),
            jax.ShapeDtypeStruct((ROWS, 128), f32),
            jax.ShapeDtypeStruct((1, 128), f32),
        ),
        in_specs=smem(1) + vmem(2),
        out_specs=tuple(vmem(4)),
        compiler_params=PARAMS,
        cost_estimate=pl.CostEstimate(flops=2 * ROWS * ROWS * WIDTH, bytes_accessed=1 << 20, transcendentals=ROWS * ROWS),
        name="own_scores",
    )(ids, unit, partner)


def other_kernel(unit_ref, other_ref, local_ref, pos_in_ref, expo_ref, sum_ref, pos_ref):
    row = lax.broadcasted_iota(jnp.int32, (ROWS, ROWS), 0) + ROWS
    logits = scores(other_ref[...], unit_ref[...]) / SOFTMAX_TEMPER
    expo = jnp.exp(logits - 1.0 / SOFTMAX_TEMPER)
    expo_ref[...] = expo
    sum_ref[...] = fold(expo)
    picked = jnp.where(local_ref[...] == row, logits, 0.0)
    pos_ref[...] = pos_in_ref[...] + jnp.sum(fold(picked), axis=0, keepdims=True)


def other_call(unit, other, local, pos):
    f32 = jnp.float32
    return pl.pallas_call(
        other_kernel,
        out_shape=(
            jax.ShapeDtypeStruct((ROWS, ROWS), f32),
            jax.ShapeDtypeStruct((ROWS, 128), f32),
            jax.ShapeDtypeStruct((1, 128), f32),
        ),
        in_specs=vmem(4),
        out_specs=tuple(vmem(3)),
        compiler_params=PARAMS,
        cost_estimate=pl.CostEstimate(flops=2 * ROWS * ROWS * WIDTH, bytes_accessed=1 << 20, transcendentals=ROWS * ROWS),
        name="other_scores",
    )(unit, other, local, pos)


def received(number, k):
    first = jnp.where(k == 0, 1, jnp.where(k == 1, 3, jnp.where(k == 2, 0, 2)))
    return (first, 3 - first, 3 - k)[number]


def pick(number, ids_ref):
    k, run = ids_ref[1], ids_ref[3]
    below, above = run % 16 == 15, run % 16 == 0
    end = (below & (k == 3)) | (above & (k == 0))
    mid = (below & (k == 2)) | (above & (k == 1))
    far = (below & (k == 1)) | (above & (k == 2))
    inner = jnp.where((k == 1) | (k == 2), 1, 0)
    if number == 2:
        return inner
    if number == 3:
        return jnp.where(end, 2, jnp.where(mid, 1, 0))
    if number == 4:
        return jnp.where(end, 1, jnp.where(far, 2, 0))
    return jnp.where(end, 2, jnp.where(mid, 3, inner))


def block_kernel(number_in, n_cand, last, *refs):
    ids_ref, unit_ref, other_ref, sum_own_ref, sum_other_ref = refs[:5]
    cands = refs[5 : 5 + n_cand]
    rest = refs[5 + n_cand :]
    if last:
        pos_ref, rest = rest[0], rest[1:]
    e_own_ref, e_other_ref = rest[:2]
    rest = rest[2:]
    if last:
        pay_ref, rest = rest[0], rest[1:]
    else:
        sum_own_out, sum_other_out = rest[:2]
        rest = rest[2:]
    k, core = ids_ref[1], ids_ref[2]
    steps = received(number_in % 3, k) - k
    if number_in > 2:
        steps = jnp.where(steps < 0, steps + 4, steps - 4)
    outside = steps == jnp.where(core == 0, -3, 3)
    if n_cand > 1:
        choice = pick(number_in, ids_ref)
        block_ref, rest = rest[0], rest[1:]
        block_ref[...] = cands[0][...]
        for number in range(1, n_cand):

            @pl.when(choice == number)
            def _(number=number):
                block_ref[...] = cands[number][...]
    else:
        block_ref = cands[0]
    block = block_ref[...]
    expo = jnp.exp(scores(unit_ref[...], block) / SOFTMAX_TEMPER - 1.0 / SOFTMAX_TEMPER)
    e_own_ref[...] = expo
    sum_own = sum_own_ref[...] + fold(expo)
    expo = jnp.exp(scores(other_ref[...], block) / SOFTMAX_TEMPER - 1.0 / SOFTMAX_TEMPER)
    expo = jnp.where(outside, 0.0, expo)
    e_other_ref[...] = expo
    sum_other = sum_other_ref[...] + fold(expo)
    if last:
        positive = jnp.broadcast_to(jnp.sum(pos_ref[...], axis=1, keepdims=True), (1, 256 - ROWS))
        rows = []
        for total in (sum_own, sum_other):
            across = jnp.sum(jnp.transpose(total), axis=0, keepdims=True)
            rows += [across[:, :128], jnp.concatenate([across[:, 128:], positive], axis=1)]
        pay_ref[...] = jnp.broadcast_to(jnp.concatenate(rows, axis=0)[None], (32, 4, 128))
    else:
        sum_own_out[...] = sum_own
        sum_other_out[...] = sum_other


def block_call(number_in, ids, unit, other, sums, cands, pos=None):
    f32 = jnp.float32
    last = pos is not None
    n = len(cands)
    shapes = [jax.ShapeDtypeStruct((ROWS, ROWS), f32)] * 2
    if last:
        shapes.append(jax.ShapeDtypeStruct((32, 4, 128), f32))
    else:
        shapes += [jax.ShapeDtypeStruct((ROWS, 128), f32)] * 2
    if n > 1:
        shapes.append(jax.ShapeDtypeStruct((ROWS, WIDTH), jnp.bfloat16))
    operands = [unit, other, *sums, *cands] + ([pos] if last else [])

    def kernel(*refs):
        block_kernel(number_in, n, last, *refs)

    out = pl.pallas_call(
        kernel,
        out_shape=tuple(shapes),
        in_specs=smem(1) + vmem(len(operands)),
        out_specs=tuple(vmem(len(shapes))),
        compiler_params=PARAMS,
        cost_estimate=pl.CostEstimate(flops=2 * 448 * ROWS * WIDTH, bytes_accessed=2 << 20, transcendentals=448 * ROWS),
        name="block_scores",
    )(ids, *operands)
    block = out[-1] if n > 1 else cands[0]
    if last:
        return out[:2], out[2], block
    return out[:2], out[2:4], block


def choose_call(by_core, ids, first, second):
    def kernel(ids_ref, first_ref, second_ref, out_ref):
        is_first = ids_ref[2] == 0 if by_core else (ids_ref[1] == 0) | (ids_ref[1] == 3)

        @pl.when(is_first)
        def _():
            out_ref[...] = first_ref[...]

        @pl.when(jnp.logical_not(is_first))
        def _():
            out_ref[...] = second_ref[...]

    return pl.pallas_call(
        kernel,
        out_shape=jax.ShapeDtypeStruct((ROWS, WIDTH), jnp.bfloat16),
        in_specs=smem(1) + vmem(2),
        out_specs=pl.BlockSpec(memory_space=pltpu.VMEM),
        compiler_params=PARAMS,
        name="choose",
    )(ids, first, second)


def denom_kernel(ids_ref, pay_ref, inv_ref, mine_ref, other_ref, post_ref):
    y, k, core, group = ids_ref[0], ids_ref[1], ids_ref[2], ids_ref[3] // 4
    pay = pay_ref[...].reshape(16, 2, 4, 128)
    lane = lax.broadcasted_iota(jnp.int32, (16, 2, 128), 2)
    part = lax.broadcasted_iota(jnp.int32, (16, 2, 128), 1)
    real = part * 128 + lane < ROWS
    first = jnp.where(real, pay[:, 0, 0:2] + pay[:, 1, 2:4], 1.0)
    second = jnp.where(real, pay[:, 1, 0:2] + pay[:, 0, 2:4], 1.0)
    total = jnp.log(first) + jnp.log(second)
    total = jnp.sum(total.reshape(32, 128), axis=0, keepdims=True)
    last = lax.broadcasted_iota(jnp.int32, (1, 128), 1) == 127
    positive = jnp.sum(pay[:, :, 1].reshape(32, 128), axis=0, keepdims=True)
    total = jnp.sum(total - jnp.where(last, positive, 0.0), axis=1, keepdims=True)
    first, second = 1.0 / first, 1.0 / second
    inv = jnp.where(core == 0, first, second)
    other_all = jnp.where(core == 0, second, first)
    inv_ref[...] = inv
    here = lax.broadcasted_iota(jnp.int32, (16, 2, 128), 0) == y * 4 + k
    mine_ref[...] = jnp.sum(jnp.where(here, inv, 0.0), axis=0)
    other_ref[...] = jnp.sum(jnp.where(here, other_all, 0.0), axis=0)
    low = jnp.where(real[:4], inv[:4], total)
    high = jnp.where(real[:4], inv[12:], total)
    post_ref[...] = jnp.broadcast_to(low[None], (16, 4, 2, 128))
    post_ref[pl.ds((group + 1) % 16, 1)] = high[None]


def denom_call(ids, pay):
    f32 = jnp.float32
    return pl.pallas_call(
        denom_kernel,
        out_shape=(
            jax.ShapeDtypeStruct((16, 2, 128), f32),
            jax.ShapeDtypeStruct((2, 128), f32),
            jax.ShapeDtypeStruct((2, 128), f32),
            jax.ShapeDtypeStruct((16, 4, 2, 128), f32),
        ),
        in_specs=smem(1) + vmem(1),
        out_specs=tuple(vmem(4)),
        compiler_params=PARAMS,
        name="denoms",
    )(ids, pay)


def lanes(pair):
    return jnp.concatenate([pair[0:1, :], pair[1:2, : ROWS - 128]], axis=1)


def grad_kernel(shift, *refs):
    ids_ref, inv_ref, edge_ref, row_ref, partner_ref = refs[:5]
    expos, blocks = refs[5:12], refs[12:19]
    out_ref = refs[19]
    if not shift:
        posted = edge_ref[:, 0, 1, :]
        lane = lax.broadcasted_iota(jnp.int32, (16, 128), 1)
        total = jnp.sum(jnp.where(lane == 127, posted, 0.0), axis=0, keepdims=True)
        total = jnp.sum(total, axis=1, keepdims=True)
        refs[20][...] = total / (ROWS * 512) + 1.0 / SOFTMAX_TEMPER
    mine = lanes(row_ref[...])
    mine = jnp.transpose(jnp.broadcast_to(mine, (128, ROWS)))[:, 0:1]
    total = None
    y, k, group = ids_ref[0], ids_ref[1], ids_ref[3] // 4
    beside = jnp.where(y == 0, group + 15, group + 1) % 16
    for number in range(7):
        chip, line = k, y
        if number:
            chip = received((number - 1) % 3, k)
        if number > 3:
            line = y + jnp.where(chip < k, 1, -1)
        inside = inv_ref[pl.ds(jnp.clip(line, 0, 3) * 4 + chip, 1)]
        if number > 3:
            inside = jnp.where((line < 0) | (line > 3), edge_ref[pl.ds(beside, 1), pl.ds(chip, 1)][0], inside)
        column = lanes(inside[0])
        weight = expos[number][...] * (mine + column)
        if number == 0:
            row = lax.broadcasted_iota(jnp.int32, (ROWS, ROWS), 0) + shift
            weight = weight - jnp.where(partner_ref[...] == row, 2.0, 0.0)
        term = jnp.dot(weight.astype(jnp.bfloat16), blocks[number][...], preferred_element_type=jnp.float32)
        total = term if total is None else total + term
    out_ref[...] = total


def grad_call(shift, ids, inv, edge, row, partner, expos, blocks):
    shapes = [jax.ShapeDtypeStruct((ROWS, WIDTH), jnp.float32)]
    if not shift:
        shapes.append(jax.ShapeDtypeStruct((1, 1), jnp.float32))

    def kernel(*refs):
        grad_kernel(shift, *refs)

    return pl.pallas_call(
        kernel,
        out_shape=tuple(shapes),
        in_specs=smem(1) + vmem(18),
        out_specs=tuple(vmem(len(shapes))),
        compiler_params=PARAMS,
        cost_estimate=pl.CostEstimate(flops=2 * 7 * ROWS * ROWS * WIDTH, bytes_accessed=6 << 20, transcendentals=0),
        name="unit_gradient",
    )(ids, inv, edge, row, partner, *expos, *blocks)


def final_kernel(emb_ref, mine_ref, got_ref, out_ref):
    emb = emb_ref[...]
    norm = jnp.sqrt(jnp.sum(emb * emb, axis=1, keepdims=True) + 1e-06)
    unit32 = emb / norm
    unit_gradient = (mine_ref[...] + got_ref[...]) / SOFTMAX_TEMPER
    radial = jnp.sum(unit32 * unit_gradient, axis=1, keepdims=True)
    out_ref[...] = (unit_gradient - unit32 * radial) / norm


def final_call(emb, mine, got):
    return pl.pallas_call(
        final_kernel,
        out_shape=jax.ShapeDtypeStruct((ROWS, WIDTH), jnp.float32),
        in_specs=vmem(3),
        out_specs=pl.BlockSpec(memory_space=pltpu.VMEM),
        compiler_params=PARAMS,
        cost_estimate=pl.CostEstimate(flops=10 * ROWS * WIDTH, bytes_accessed=16 * ROWS * WIDTH, transcendentals=0),
        name="final",
    )(emb, mine, got)


def send(value, name):
    return lax.ppermute(value, AXES, ROUTES[name])


def per_device(embeddings, partner):
    norm = jnp.sqrt(jnp.sum(embeddings * embeddings, axis=1, keepdims=True) + 1e-06)
    unit = (embeddings / norm).astype(jnp.bfloat16)

    run = lax.axis_index(("zh", "x", "y"))
    ids = jnp.stack([lax.axis_index(name) for name in DEV_AXES] + [run]).astype(jnp.int32)
    partner = partner.reshape(1, ROWS)

    p1b = send(unit, "P1b")
    x1 = send(unit, "X1")
    local, e_own, sum_own, pos = own_call(ids, unit, partner)
    p1a = send(after(unit, sum_own), "P1a")
    other = lax.ppermute(after(unit, p1b), ("core",), [(0, 1), (1, 0)])
    e_other, sum_other, pos = other_call(unit, other, local, pos)
    expos, blocks, sums = [(e_own, e_other)] + [None] * 6, [unit] + [None] * 6, (sum_own, sum_other)

    def add(number, cands):
        nonlocal sums
        last = number == 5
        pair, rest, block = block_call(number, ids, unit, other, sums, cands, pos if last else None)
        expos[number + 1] = pair
        blocks[number + 1] = block
        if last:
            return rest
        sums = rest

    r2 = send(after(unit, p1a, p1b), "P2")
    r1 = choose_call(True, ids, p1a, p1b)
    y1 = send(r1, "Y1")
    x2 = send(after(x1, r1), "X2")
    x3 = send(r1, "X3")
    add(0, [r1])
    r2 = after(r2, sums[0])
    y2 = send(after(r2, y1), "Y2")
    p3b = send(after(unit, r2), "P3b")
    p3a = send(after(r1, r2), "P3a")
    x4 = send(after(r2, x3), "X4")
    x5 = send(choose_call(False, ids, x3, after(x2, r2)), "X5")
    add(1, [r2])
    p3a = after(p3a, sums[0])
    p3b = after(p3b, sums[0])
    y3a = send(after(p3a, y2), "Y3a")
    y3b = send(after(p3b, y2), "Y3b")
    add(2, [p3a, p3b])
    add(3, [y1, x2, x4])
    add(4, [y2, x3, x5])
    pay = add(5, [y3a, y3b, x1, x5])

    pays = lax.all_to_all(pay, DEV_AXES, 0, 0)
    inv, mine_inv, other_inv, post = denom_call(ids, pays)
    posts = lax.all_to_all(post, ("zh", "x"), 0, 0)
    (for_other,) = grad_call(ROWS, ids, inv, posts, other_inv, local, [e[1] for e in expos], blocks)
    got = lax.ppermute(for_other, ("core",), [(0, 1), (1, 0)])
    mine, loss = grad_call(0, ids, after(inv, for_other), posts, mine_inv, local, [e[0] for e in expos], blocks)
    grad = final_call(embeddings, mine, got)
    loss = loss.reshape(())
    return (loss, grad)


def solution(mesh):
    split = Mesh(mesh.devices.reshape(SHAPE), AXES)
    in_specs = (P(AXES, None), P(AXES))
    out_specs = (P(), P(AXES, None))
    return jax.shard_map(per_device, mesh=split, in_specs=in_specs, out_specs=out_specs, check_vma=False)
```

```python
import jax
import jax.numpy as jnp
from jax import lax
from jax.experimental import pallas as pl
from jax.experimental.pallas import tpu as pltpu
from jax.sharding import Mesh
from jax.sharding import PartitionSpec as P

ROUNDS = 6
SOFTMAX_TEMPER = 0.1
AXES = ("zh", "x", "y", "zl", "core")
SHAPE = (4, 4, 4, 4, 2)
RUNS = 64
DEV_AXES = ("y", "zl", "core")
ROWS = 224
WIDTH = 1024

def crosses(run):
    return run % 16 == 15


def routes():
    names = ("P1a", "P1b", "P2", "P3a", "P3b", "Y1", "Y2", "Y3a", "Y3b", "X1", "X2", "X3", "X4", "X5")
    table = {name: [] for name in names}

    def chip(run, k):
        return (run % RUNS) * 4 + k

    def add(name, *pairs, cores=(0, 1)):
        for source, target in pairs:
            for core in cores:
                table[name].append((2 * source + core, 2 * target + core))

    for run in range(RUNS):
        for name, moves in (
            ("P2", ((1, 3), (2, 0), (0, 1), (3, 2))),
            ("P3a", ((2, 3), (1, 0))),
            ("P3b", ((1, 2), (2, 1))),
        ):
            add(name, *((chip(run, a), chip(run, b)) for a, b in moves))
        for name, core in (("P1a", 0), ("P1b", 1)):
            add(name, *((chip(run, a), chip(run, b)) for a, b in ((0, 2), (1, 0), (2, 3), (3, 1))), cores=(core,))
        for name, ups, downs in (
            ("Y1", (0, 1), (2, 3)),
            ("Y2", (0, 2), (1, 3)),
            ("Y3a", (0,), (3,)),
            ("Y3b", (1,), (2,)),
        ):
            if not crosses(run):
                add(name, *((chip(run, k), chip(run + 1, k)) for k in ups))
            if not crosses(run - 1):
                add(name, *((chip(run, k), chip(run - 1, k)) for k in downs))
        if crosses(run):
            low = [chip(run, k) for k in range(4)]
            high = [chip(run + 1, k) for k in range(4)]
            for name in ("X1", "X3", "X4"):
                add(name, (low[3], high[0]), (high[0], low[3]))
            for name in ("X2", "X5"):
                add(name, (high[0], high[1]), (low[3], low[2]))
            add("X5", (high[1], high[2]), (low[2], low[1]))
    return table


ROUTES = routes()


def after(value, *others):
    return lax.optimization_barrier((value,) + others)[0]


def vmem(count):
    return [pl.BlockSpec(memory_space=pltpu.VMEM)] * count


def smem(count):
    return [pl.BlockSpec(memory_space=pltpu.SMEM)] * count


PARAMS = pltpu.CompilerParams(vmem_limit_bytes=12 * 1024 * 1024)


def scores(rows, columns):
    return lax.dot_general(rows, columns, (((1,), (1,)), ((), ())), preferred_element_type=jnp.float32)


def fold(values):
    tail = jnp.concatenate([values[:, 128:], jnp.zeros((ROWS, 256 - ROWS), jnp.float32)], axis=1)
    return values[:, :128] + tail


def own_kernel(ids_ref, unit_ref, partner_ref, local_ref, expo_ref, sum_ref, pos_ref):
    unit = unit_ref[...]
    row = lax.broadcasted_iota(jnp.int32, (ROWS, ROWS), 0)
    column = lax.broadcasted_iota(jnp.int32, (ROWS, ROWS), 1)
    partner = partner_ref[...] - (ids_ref[3] * (8 * ROWS) + ids_ref[1] * (2 * ROWS) + ids_ref[2] * ROWS)
    partner = jnp.where(partner < 0, partner + 2 * ROWS, partner)
    local_ref[...] = partner
    logits = scores(unit, unit) / SOFTMAX_TEMPER
    expo = jnp.where(row == column, 0.0, jnp.exp(logits - 1.0 / SOFTMAX_TEMPER))
    expo_ref[...] = expo
    sum_ref[...] = fold(expo)
    pos_ref[...] = jnp.sum(fold(jnp.where(partner == row, logits, 0.0)), axis=0, keepdims=True)


def own_call(ids, unit, partner):
    f32 = jnp.float32
    return pl.pallas_call(
        own_kernel,
        out_shape=(
            jax.ShapeDtypeStruct((1, ROWS), jnp.int32),
            jax.ShapeDtypeStruct((ROWS, ROWS), f32),
            jax.ShapeDtypeStruct((ROWS, 128), f32),
            jax.ShapeDtypeStruct((1, 128), f32),
        ),
        in_specs=smem(1) + vmem(2),
        out_specs=tuple(vmem(4)),
        compiler_params=PARAMS,
        cost_estimate=pl.CostEstimate(flops=2 * ROWS * ROWS * WIDTH, bytes_accessed=1 << 20, transcendentals=ROWS * ROWS),
        name="own_scores",
    )(ids, unit, partner)


def other_kernel(unit_ref, other_ref, local_ref, pos_in_ref, expo_ref, sum_ref, pos_ref):
    row = lax.broadcasted_iota(jnp.int32, (ROWS, ROWS), 0) + ROWS
    logits = scores(other_ref[...], unit_ref[...]) / SOFTMAX_TEMPER
    expo = jnp.exp(logits - 1.0 / SOFTMAX_TEMPER)
    expo_ref[...] = expo
    sum_ref[...] = fold(expo)
    picked = jnp.where(local_ref[...] == row, logits, 0.0)
    pos_ref[...] = pos_in_ref[...] + jnp.sum(fold(picked), axis=0, keepdims=True)


def other_call(unit, other, local, pos):
    f32 = jnp.float32
    return pl.pallas_call(
        other_kernel,
        out_shape=(
            jax.ShapeDtypeStruct((ROWS, ROWS), f32),
            jax.ShapeDtypeStruct((ROWS, 128), f32),
            jax.ShapeDtypeStruct((1, 128), f32),
        ),
        in_specs=vmem(4),
        out_specs=tuple(vmem(3)),
        compiler_params=PARAMS,
        cost_estimate=pl.CostEstimate(flops=2 * ROWS * ROWS * WIDTH, bytes_accessed=1 << 20, transcendentals=ROWS * ROWS),
        name="other_scores",
    )(unit, other, local, pos)


def received(number, k):
    first = jnp.where(k == 0, 1, jnp.where(k == 1, 3, jnp.where(k == 2, 0, 2)))
    return (first, 3 - first, 3 - k)[number]


def pick(number, ids_ref):
    k, run = ids_ref[1], ids_ref[3]
    below, above = run % 16 == 15, run % 16 == 0
    end = (below & (k == 3)) | (above & (k == 0))
    mid = (below & (k == 2)) | (above & (k == 1))
    far = (below & (k == 1)) | (above & (k == 2))
    inner = jnp.where((k == 1) | (k == 2), 1, 0)
    if number == 2:
        return inner
    if number == 3:
        return jnp.where(end, 2, jnp.where(mid, 1, 0))
    if number == 4:
        return jnp.where(end, 1, jnp.where(far, 2, 0))
    return jnp.where(end, 2, jnp.where(mid, 3, inner))


def block_kernel(number_in, n_cand, last, *refs):
    ids_ref, unit_ref, other_ref, sum_own_ref, sum_other_ref = refs[:5]
    cands = refs[5 : 5 + n_cand]
    rest = refs[5 + n_cand :]
    if last:
        pos_ref, rest = rest[0], rest[1:]
    e_own_ref, e_other_ref = rest[:2]
    rest = rest[2:]
    if last:
        pay_ref, rest = rest[0], rest[1:]
    else:
        sum_own_out, sum_other_out = rest[:2]
        rest = rest[2:]
    k, core = ids_ref[1], ids_ref[2]
    steps = received(number_in % 3, k) - k
    if number_in > 2:
        steps = jnp.where(steps < 0, steps + 4, steps - 4)
    outside = steps == jnp.where(core == 0, -3, 3)
    if n_cand > 1:
        choice = pick(number_in, ids_ref)
        block_ref, rest = rest[0], rest[1:]
        block_ref[...] = cands[0][...]
        for number in range(1, n_cand):

            @pl.when(choice == number)
            def _(number=number):
                block_ref[...] = cands[number][...]
    else:
        block_ref = cands[0]
    block = block_ref[...]
    expo = jnp.exp(scores(unit_ref[...], block) / SOFTMAX_TEMPER - 1.0 / SOFTMAX_TEMPER)
    e_own_ref[...] = expo
    sum_own = sum_own_ref[...] + fold(expo)
    expo = jnp.exp(scores(other_ref[...], block) / SOFTMAX_TEMPER - 1.0 / SOFTMAX_TEMPER)
    expo = jnp.where(outside, 0.0, expo)
    e_other_ref[...] = expo
    sum_other = sum_other_ref[...] + fold(expo)
    if last:
        positive = jnp.broadcast_to(jnp.sum(pos_ref[...], axis=1, keepdims=True), (1, 256 - ROWS))
        rows = []
        for total in (sum_own, sum_other):
            across = jnp.sum(jnp.transpose(total), axis=0, keepdims=True)
            rows += [across[:, :128], jnp.concatenate([across[:, 128:], positive], axis=1)]
        pay_ref[...] = jnp.broadcast_to(jnp.concatenate(rows, axis=0)[None], (32, 4, 128))
    else:
        sum_own_out[...] = sum_own
        sum_other_out[...] = sum_other


def block_call(number_in, ids, unit, other, sums, cands, pos=None):
    f32 = jnp.float32
    last = pos is not None
    n = len(cands)
    shapes = [jax.ShapeDtypeStruct((ROWS, ROWS), f32)] * 2
    if last:
        shapes.append(jax.ShapeDtypeStruct((32, 4, 128), f32))
    else:
        shapes += [jax.ShapeDtypeStruct((ROWS, 128), f32)] * 2
    if n > 1:
        shapes.append(jax.ShapeDtypeStruct((ROWS, WIDTH), jnp.bfloat16))
    operands = [unit, other, *sums, *cands] + ([pos] if last else [])

    def kernel(*refs):
        block_kernel(number_in, n, last, *refs)

    out = pl.pallas_call(
        kernel,
        out_shape=tuple(shapes),
        in_specs=smem(1) + vmem(len(operands)),
        out_specs=tuple(vmem(len(shapes))),
        compiler_params=PARAMS,
        cost_estimate=pl.CostEstimate(flops=2 * 448 * ROWS * WIDTH, bytes_accessed=2 << 20, transcendentals=448 * ROWS),
        name="block_scores",
    )(ids, *operands)
    block = out[-1] if n > 1 else cands[0]
    if last:
        return out[:2], out[2], block
    return out[:2], out[2:4], block


def choose_call(by_core, ids, first, second):
    def kernel(ids_ref, first_ref, second_ref, out_ref):
        is_first = ids_ref[2] == 0 if by_core else (ids_ref[1] == 0) | (ids_ref[1] == 3)

        @pl.when(is_first)
        def _():
            out_ref[...] = first_ref[...]

        @pl.when(jnp.logical_not(is_first))
        def _():
            out_ref[...] = second_ref[...]

    return pl.pallas_call(
        kernel,
        out_shape=jax.ShapeDtypeStruct((ROWS, WIDTH), jnp.bfloat16),
        in_specs=smem(1) + vmem(2),
        out_specs=pl.BlockSpec(memory_space=pltpu.VMEM),
        compiler_params=PARAMS,
        name="choose",
    )(ids, first, second)


def denom_kernel(ids_ref, pay_ref, inv_ref, mine_ref, other_ref, post_ref):
    y, k, core, group = ids_ref[0], ids_ref[1], ids_ref[2], ids_ref[3] // 4
    pay = pay_ref[...].reshape(16, 2, 4, 128)
    lane = lax.broadcasted_iota(jnp.int32, (16, 2, 128), 2)
    part = lax.broadcasted_iota(jnp.int32, (16, 2, 128), 1)
    real = part * 128 + lane < ROWS
    first = jnp.where(real, pay[:, 0, 0:2] + pay[:, 1, 2:4], 1.0)
    second = jnp.where(real, pay[:, 1, 0:2] + pay[:, 0, 2:4], 1.0)
    total = jnp.log(first) + jnp.log(second)
    total = jnp.sum(total.reshape(32, 128), axis=0, keepdims=True)
    last = lax.broadcasted_iota(jnp.int32, (1, 128), 1) == 127
    positive = jnp.sum(pay[:, :, 1].reshape(32, 128), axis=0, keepdims=True)
    total = jnp.sum(total - jnp.where(last, positive, 0.0), axis=1, keepdims=True)
    first, second = 1.0 / first, 1.0 / second
    inv = jnp.where(core == 0, first, second)
    other_all = jnp.where(core == 0, second, first)
    inv_ref[...] = inv
    here = lax.broadcasted_iota(jnp.int32, (16, 2, 128), 0) == y * 4 + k
    mine_ref[...] = jnp.sum(jnp.where(here, inv, 0.0), axis=0)
    other_ref[...] = jnp.sum(jnp.where(here, other_all, 0.0), axis=0)
    low = jnp.where(real[:4], inv[:4], total)
    high = jnp.where(real[:4], inv[12:], total)
    post_ref[...] = jnp.broadcast_to(low[None], (16, 4, 2, 128))
    post_ref[pl.ds((group + 1) % 16, 1)] = high[None]


def denom_call(ids, pay):
    f32 = jnp.float32
    return pl.pallas_call(
        denom_kernel,
        out_shape=(
            jax.ShapeDtypeStruct((16, 2, 128), f32),
            jax.ShapeDtypeStruct((2, 128), f32),
            jax.ShapeDtypeStruct((2, 128), f32),
            jax.ShapeDtypeStruct((16, 4, 2, 128), f32),
        ),
        in_specs=smem(1) + vmem(1),
        out_specs=tuple(vmem(4)),
        compiler_params=PARAMS,
        name="denoms",
    )(ids, pay)


def lanes(pair):
    return jnp.concatenate([pair[0:1, :], pair[1:2, : ROWS - 128]], axis=1)


def grad_kernel(shift, *refs):
    ids_ref, inv_ref, edge_ref, row_ref, partner_ref = refs[:5]
    expos, blocks = refs[5:12], refs[12:19]
    out_ref = refs[19]
    if not shift:
        posted = edge_ref[:, 0, 1, :]
        lane = lax.broadcasted_iota(jnp.int32, (16, 128), 1)
        total = jnp.sum(jnp.where(lane == 127, posted, 0.0), axis=0, keepdims=True)
        total = jnp.sum(total, axis=1, keepdims=True)
        refs[20][...] = total / (ROWS * 512) + 1.0 / SOFTMAX_TEMPER
    mine = lanes(row_ref[...])
    mine = jnp.transpose(jnp.broadcast_to(mine, (128, ROWS)))[:, 0:1]
    total = None
    y, k, group = ids_ref[0], ids_ref[1], ids_ref[3] // 4
    beside = jnp.where(y == 0, group + 15, group + 1) % 16
    for number in range(7):
        chip, line = k, y
        if number:
            chip = received((number - 1) % 3, k)
        if number > 3:
            line = y + jnp.where(chip < k, 1, -1)
        inside = inv_ref[pl.ds(jnp.clip(line, 0, 3) * 4 + chip, 1)]
        if number > 3:
            inside = jnp.where((line < 0) | (line > 3), edge_ref[pl.ds(beside, 1), pl.ds(chip, 1)][0], inside)
        column = lanes(inside[0])
        weight = expos[number][...] * (mine + column)
        if number == 0:
            row = lax.broadcasted_iota(jnp.int32, (ROWS, ROWS), 0) + shift
            weight = weight - jnp.where(partner_ref[...] == row, 2.0, 0.0)
        term = jnp.dot(weight.astype(jnp.bfloat16), blocks[number][...], preferred_element_type=jnp.float32)
        total = term if total is None else total + term
    out_ref[...] = total


def grad_call(shift, ids, inv, edge, row, partner, expos, blocks):
    shapes = [jax.ShapeDtypeStruct((ROWS, WIDTH), jnp.float32)]
    if not shift:
        shapes.append(jax.ShapeDtypeStruct((1, 1), jnp.float32))

    def kernel(*refs):
        grad_kernel(shift, *refs)

    return pl.pallas_call(
        kernel,
        out_shape=tuple(shapes),
        in_specs=smem(1) + vmem(18),
        out_specs=tuple(vmem(len(shapes))),
        compiler_params=PARAMS,
        cost_estimate=pl.CostEstimate(flops=2 * 7 * ROWS * ROWS * WIDTH, bytes_accessed=6 << 20, transcendentals=0),
        name="unit_gradient",
    )(ids, inv, edge, row, partner, *expos, *blocks)


def final_kernel(emb_ref, mine_ref, got_ref, out_ref):
    emb = emb_ref[...]
    norm = jnp.sqrt(jnp.sum(emb * emb, axis=1, keepdims=True) + 1e-06)
    unit32 = emb / norm
    unit_gradient = (mine_ref[...] + got_ref[...]) / SOFTMAX_TEMPER
    radial = jnp.sum(unit32 * unit_gradient, axis=1, keepdims=True)
    out_ref[...] = (unit_gradient - unit32 * radial) / norm


def final_call(emb, mine, got):
    return pl.pallas_call(
        final_kernel,
        out_shape=jax.ShapeDtypeStruct((ROWS, WIDTH), jnp.float32),
        in_specs=vmem(3),
        out_specs=pl.BlockSpec(memory_space=pltpu.VMEM),
        compiler_params=PARAMS,
        cost_estimate=pl.CostEstimate(flops=10 * ROWS * WIDTH, bytes_accessed=16 * ROWS * WIDTH, transcendentals=0),
        name="final",
    )(emb, mine, got)


def send(value, name):
    return lax.ppermute(value, AXES, ROUTES[name])


def per_device(embeddings, partner):
    norm = jnp.sqrt(jnp.sum(embeddings * embeddings, axis=1, keepdims=True) + 1e-06)
    unit = (embeddings / norm).astype(jnp.bfloat16)

    run = lax.axis_index(("zh", "x", "y"))
    ids = jnp.stack([lax.axis_index(name) for name in DEV_AXES] + [run]).astype(jnp.int32)
    partner = partner.reshape(1, ROWS)

    p1b = send(unit, "P1b")
    x1 = send(unit, "X1")
    local, e_own, sum_own, pos = own_call(ids, unit, partner)
    p1a = send(after(unit, sum_own), "P1a")
    other = lax.ppermute(after(unit, ids), ("core",), [(0, 1), (1, 0)])
    e_other, sum_other, pos = other_call(unit, other, local, pos)
    expos, blocks, sums = [(e_own, e_other)] + [None] * 6, [unit] + [None] * 6, (sum_own, sum_other)

    def add(number, cands):
        nonlocal sums
        last = number == 5
        pair, rest, block = block_call(number, ids, unit, other, sums, cands, pos if last else None)
        expos[number + 1] = pair
        blocks[number + 1] = block
        if last:
            return rest
        sums = rest

    p1b = after(p1b, other)
    r2 = send(after(unit, p1a, p1b), "P2")
    r1 = choose_call(True, ids, p1a, p1b)
    y1 = send(r1, "Y1")
    x2 = send(after(x1, r1), "X2")
    x3 = send(r1, "X3")
    add(0, [r1])
    r2 = after(r2, sums[0])
    y2 = send(after(r2, y1), "Y2")
    p3b = send(after(unit, r2), "P3b")
    p3a = send(after(r1, r2), "P3a")
    x4 = send(after(r2, x3), "X4")
    x5 = send(choose_call(False, ids, x3, after(x2, r2)), "X5")
    add(1, [r2])
    p3a = after(p3a, sums[0])
    p3b = after(p3b, sums[0])
    y3a = send(after(p3a, y2), "Y3a")
    y3b = send(after(p3b, y2), "Y3b")
    add(2, [p3a, p3b])
    add(3, [y1, x2, x4])
    add(4, [y2, x3, x5])
    pay = add(5, [y3a, y3b, x1, x5])

    pays = lax.all_to_all(pay, DEV_AXES, 0, 0)
    inv, mine_inv, other_inv, post = denom_call(ids, pays)
    posts = lax.all_to_all(post, ("zh", "x"), 0, 0)
    (for_other,) = grad_call(ROWS, ids, inv, posts, other_inv, local, [e[1] for e in expos], blocks)
    got = lax.ppermute(for_other, ("core",), [(0, 1), (1, 0)])
    mine, loss = grad_call(0, ids, after(inv, for_other), posts, mine_inv, local, [e[0] for e in expos], blocks)
    grad = final_call(embeddings, mine, got)
    loss = loss.reshape(())
    return (loss, grad)


def solution(mesh):
    split = Mesh(mesh.devices.reshape(SHAPE), AXES)
    in_specs = (P(AXES, None), P(AXES))
    out_specs = (P(), P(AXES, None))
    return jax.shard_map(per_device, mesh=split, in_specs=in_specs, out_specs=out_specs, check_vma=False)
```

```python
import jax
import jax.numpy as jnp
from jax import lax
from jax.experimental import pallas as pl
from jax.experimental.pallas import tpu as pltpu
from jax.sharding import Mesh
from jax.sharding import PartitionSpec as P

ROUNDS = 6
SOFTMAX_TEMPER = 0.1
AXES = ("zh", "x", "y", "zl", "core")
SHAPE = (4, 4, 4, 4, 2)
RUNS = 64
DEV_AXES = ("y", "zl", "core")
ROWS = 224
WIDTH = 1024

def crosses(run):
    return run % 16 == 15


def routes():
    names = ("P1a", "P1b", "P2", "P3a", "P3b", "Y1", "Y2", "Y3a", "Y3b", "X1", "X2", "X3", "X4", "X5")
    table = {name: [] for name in names}

    def chip(run, k):
        return (run % RUNS) * 4 + k

    def add(name, *pairs, cores=(0, 1)):
        for source, target in pairs:
            for core in cores:
                table[name].append((2 * source + core, 2 * target + core))

    for run in range(RUNS):
        for name, moves in (
            ("P2", ((1, 3), (2, 0), (0, 1), (3, 2))),
            ("P3a", ((2, 3), (1, 0))),
            ("P3b", ((1, 2), (2, 1))),
        ):
            add(name, *((chip(run, a), chip(run, b)) for a, b in moves))
        for name, core in (("P1a", 0), ("P1b", 1)):
            add(name, *((chip(run, a), chip(run, b)) for a, b in ((0, 2), (1, 0), (2, 3), (3, 1))), cores=(core,))
        for name, ups, downs in (
            ("Y1", (0, 1), (2, 3)),
            ("Y2", (0, 2), (1, 3)),
            ("Y3a", (0,), (3,)),
            ("Y3b", (1,), (2,)),
        ):
            if not crosses(run):
                add(name, *((chip(run, k), chip(run + 1, k)) for k in ups))
            if not crosses(run - 1):
                add(name, *((chip(run, k), chip(run - 1, k)) for k in downs))
        if crosses(run):
            low = [chip(run, k) for k in range(4)]
            high = [chip(run + 1, k) for k in range(4)]
            for name in ("X1", "X3", "X4"):
                add(name, (low[3], high[0]), (high[0], low[3]))
            for name in ("X2", "X5"):
                add(name, (high[0], high[1]), (low[3], low[2]))
            add("X5", (high[1], high[2]), (low[2], low[1]))
    return table


ROUTES = routes()


def after(value, *others):
    return lax.optimization_barrier((value,) + others)[0]


def vmem(count):
    return [pl.BlockSpec(memory_space=pltpu.VMEM)] * count


def smem(count):
    return [pl.BlockSpec(memory_space=pltpu.SMEM)] * count


PARAMS = pltpu.CompilerParams(vmem_limit_bytes=12 * 1024 * 1024)


def scores(rows, columns):
    return lax.dot_general(rows, columns, (((1,), (1,)), ((), ())), preferred_element_type=jnp.float32)


def fold(values):
    tail = jnp.concatenate([values[:, 128:], jnp.zeros((ROWS, 256 - ROWS), jnp.float32)], axis=1)
    return values[:, :128] + tail


def own_kernel(ids_ref, unit_ref, other_ref, partner_ref, local_ref, e_own_ref, e_other_ref, sum_own_ref, sum_other_ref, pos_ref):
    unit = unit_ref[...]
    row = lax.broadcasted_iota(jnp.int32, (ROWS, ROWS), 0)
    column = lax.broadcasted_iota(jnp.int32, (ROWS, ROWS), 1)
    shift = ids_ref[2] * ROWS
    partner = partner_ref[...] - (ids_ref[3] * (8 * ROWS) + ids_ref[1] * (2 * ROWS) + shift)
    partner = jnp.where(partner < 0, partner + 2 * ROWS, partner)
    local_ref[...] = partner
    logits = scores(unit, unit) / SOFTMAX_TEMPER
    expo = jnp.where(row == column, 0.0, jnp.exp(logits - 1.0 / SOFTMAX_TEMPER))
    e_own_ref[...] = expo
    sum_own_ref[...] = fold(expo)
    picked = jnp.where(partner == row, logits, 0.0)
    logits = scores(other_ref[...], unit) / SOFTMAX_TEMPER
    expo = jnp.exp(logits - 1.0 / SOFTMAX_TEMPER)
    e_other_ref[...] = expo
    sum_other_ref[...] = fold(expo)
    picked = picked + jnp.where(partner == row + ROWS, logits, 0.0)
    pos_ref[...] = jnp.sum(fold(picked), axis=0, keepdims=True)


def own_call(ids, unit, other, partner):
    f32 = jnp.float32
    return pl.pallas_call(
        own_kernel,
        out_shape=(
            jax.ShapeDtypeStruct((1, ROWS), jnp.int32),
            jax.ShapeDtypeStruct((ROWS, ROWS), f32),
            jax.ShapeDtypeStruct((ROWS, ROWS), f32),
            jax.ShapeDtypeStruct((ROWS, 128), f32),
            jax.ShapeDtypeStruct((ROWS, 128), f32),
            jax.ShapeDtypeStruct((1, 128), f32),
        ),
        in_specs=smem(1) + vmem(3),
        out_specs=tuple(vmem(6)),
        compiler_params=PARAMS,
        cost_estimate=pl.CostEstimate(flops=2 * 448 * ROWS * WIDTH, bytes_accessed=2 << 20, transcendentals=448 * ROWS),
        name="own_scores",
    )(ids, unit, other, partner)


def received(number, k):
    first = jnp.where(k == 0, 1, jnp.where(k == 1, 3, jnp.where(k == 2, 0, 2)))
    return (first, 3 - first, 3 - k)[number]


def pick(number, ids_ref):
    k, run = ids_ref[1], ids_ref[3]
    below, above = run % 16 == 15, run % 16 == 0
    end = (below & (k == 3)) | (above & (k == 0))
    mid = (below & (k == 2)) | (above & (k == 1))
    far = (below & (k == 1)) | (above & (k == 2))
    inner = jnp.where((k == 1) | (k == 2), 1, 0)
    if number == 2:
        return inner
    if number == 3:
        return jnp.where(end, 2, jnp.where(mid, 1, 0))
    if number == 4:
        return jnp.where(end, 1, jnp.where(far, 2, 0))
    return jnp.where(end, 2, jnp.where(mid, 3, inner))


def block_kernel(number_in, n_cand, last, *refs):
    ids_ref, unit_ref, other_ref, sum_own_ref, sum_other_ref = refs[:5]
    cands = refs[5 : 5 + n_cand]
    rest = refs[5 + n_cand :]
    if last:
        pos_ref, rest = rest[0], rest[1:]
    e_own_ref, e_other_ref = rest[:2]
    rest = rest[2:]
    if last:
        pay_ref, rest = rest[0], rest[1:]
    else:
        sum_own_out, sum_other_out = rest[:2]
        rest = rest[2:]
    k, core = ids_ref[1], ids_ref[2]
    steps = received(number_in % 3, k) - k
    if number_in > 2:
        steps = jnp.where(steps < 0, steps + 4, steps - 4)
    outside = steps == jnp.where(core == 0, -3, 3)
    if n_cand > 1:
        choice = pick(number_in, ids_ref)
        block_ref, rest = rest[0], rest[1:]
        block_ref[...] = cands[0][...]
        for number in range(1, n_cand):

            @pl.when(choice == number)
            def _(number=number):
                block_ref[...] = cands[number][...]
    else:
        block_ref = cands[0]
    block = block_ref[...]
    expo = jnp.exp(scores(unit_ref[...], block) / SOFTMAX_TEMPER - 1.0 / SOFTMAX_TEMPER)
    e_own_ref[...] = expo
    sum_own = sum_own_ref[...] + fold(expo)
    expo = jnp.exp(scores(other_ref[...], block) / SOFTMAX_TEMPER - 1.0 / SOFTMAX_TEMPER)
    expo = jnp.where(outside, 0.0, expo)
    e_other_ref[...] = expo
    sum_other = sum_other_ref[...] + fold(expo)
    if last:
        positive = jnp.broadcast_to(jnp.sum(pos_ref[...], axis=1, keepdims=True), (1, 256 - ROWS))
        rows = []
        for total in (sum_own, sum_other):
            across = jnp.sum(jnp.transpose(total), axis=0, keepdims=True)
            rows += [across[:, :128], jnp.concatenate([across[:, 128:], positive], axis=1)]
        pay_ref[...] = jnp.broadcast_to(jnp.concatenate(rows, axis=0)[None], (32, 4, 128))
    else:
        sum_own_out[...] = sum_own
        sum_other_out[...] = sum_other


def block_call(number_in, ids, unit, other, sums, cands, pos=None):
    f32 = jnp.float32
    last = pos is not None
    n = len(cands)
    shapes = [jax.ShapeDtypeStruct((ROWS, ROWS), f32)] * 2
    if last:
        shapes.append(jax.ShapeDtypeStruct((32, 4, 128), f32))
    else:
        shapes += [jax.ShapeDtypeStruct((ROWS, 128), f32)] * 2
    if n > 1:
        shapes.append(jax.ShapeDtypeStruct((ROWS, WIDTH), jnp.bfloat16))
    operands = [unit, other, *sums, *cands] + ([pos] if last else [])

    def kernel(*refs):
        block_kernel(number_in, n, last, *refs)

    out = pl.pallas_call(
        kernel,
        out_shape=tuple(shapes),
        in_specs=smem(1) + vmem(len(operands)),
        out_specs=tuple(vmem(len(shapes))),
        compiler_params=PARAMS,
        cost_estimate=pl.CostEstimate(flops=2 * 448 * ROWS * WIDTH, bytes_accessed=2 << 20, transcendentals=448 * ROWS),
        name="block_scores",
    )(ids, *operands)
    block = out[-1] if n > 1 else cands[0]
    if last:
        return out[:2], out[2], block
    return out[:2], out[2:4], block


def choose_call(by_core, ids, first, second):
    def kernel(ids_ref, first_ref, second_ref, out_ref):
        is_first = ids_ref[2] == 0 if by_core else (ids_ref[1] == 0) | (ids_ref[1] == 3)

        @pl.when(is_first)
        def _():
            out_ref[...] = first_ref[...]

        @pl.when(jnp.logical_not(is_first))
        def _():
            out_ref[...] = second_ref[...]

    return pl.pallas_call(
        kernel,
        out_shape=jax.ShapeDtypeStruct((ROWS, WIDTH), jnp.bfloat16),
        in_specs=smem(1) + vmem(2),
        out_specs=pl.BlockSpec(memory_space=pltpu.VMEM),
        compiler_params=PARAMS,
        name="choose",
    )(ids, first, second)


def denom_kernel(ids_ref, pay_ref, inv_ref, mine_ref, other_ref, post_ref):
    y, k, core, group = ids_ref[0], ids_ref[1], ids_ref[2], ids_ref[3] // 4
    pay = pay_ref[...].reshape(16, 2, 4, 128)
    lane = lax.broadcasted_iota(jnp.int32, (16, 2, 128), 2)
    part = lax.broadcasted_iota(jnp.int32, (16, 2, 128), 1)
    real = part * 128 + lane < ROWS
    first = jnp.where(real, pay[:, 0, 0:2] + pay[:, 1, 2:4], 1.0)
    second = jnp.where(real, pay[:, 1, 0:2] + pay[:, 0, 2:4], 1.0)
    total = jnp.log(first) + jnp.log(second)
    total = jnp.sum(total.reshape(32, 128), axis=0, keepdims=True)
    last = lax.broadcasted_iota(jnp.int32, (1, 128), 1) == 127
    positive = jnp.sum(pay[:, :, 1].reshape(32, 128), axis=0, keepdims=True)
    total = jnp.sum(total - jnp.where(last, positive, 0.0), axis=1, keepdims=True)
    first, second = 1.0 / first, 1.0 / second
    inv = jnp.where(core == 0, first, second)
    other_all = jnp.where(core == 0, second, first)
    inv_ref[...] = inv
    here = lax.broadcasted_iota(jnp.int32, (16, 2, 128), 0) == y * 4 + k
    mine_ref[...] = jnp.sum(jnp.where(here, inv, 0.0), axis=0)
    other_ref[...] = jnp.sum(jnp.where(here, other_all, 0.0), axis=0)
    low = jnp.where(real[:4], inv[:4], total)
    high = jnp.where(real[:4], inv[12:], total)
    post_ref[...] = jnp.broadcast_to(low[None], (16, 4, 2, 128))
    post_ref[pl.ds((group + 1) % 16, 1)] = high[None]


def denom_call(ids, pay):
    f32 = jnp.float32
    return pl.pallas_call(
        denom_kernel,
        out_shape=(
            jax.ShapeDtypeStruct((16, 2, 128), f32),
            jax.ShapeDtypeStruct((2, 128), f32),
            jax.ShapeDtypeStruct((2, 128), f32),
            jax.ShapeDtypeStruct((16, 4, 2, 128), f32),
        ),
        in_specs=smem(1) + vmem(1),
        out_specs=tuple(vmem(4)),
        compiler_params=PARAMS,
        name="denoms",
    )(ids, pay)


def lanes(pair):
    return jnp.concatenate([pair[0:1, :], pair[1:2, : ROWS - 128]], axis=1)


def grad_kernel(shift, *refs):
    ids_ref, inv_ref, edge_ref, row_ref, partner_ref = refs[:5]
    expos, blocks = refs[5:12], refs[12:19]
    out_ref = refs[19]
    if not shift:
        posted = edge_ref[:, 0, 1, :]
        lane = lax.broadcasted_iota(jnp.int32, (16, 128), 1)
        total = jnp.sum(jnp.where(lane == 127, posted, 0.0), axis=0, keepdims=True)
        total = jnp.sum(total, axis=1, keepdims=True)
        refs[20][...] = total / (ROWS * 512) + 1.0 / SOFTMAX_TEMPER
    mine = lanes(row_ref[...])
    mine = jnp.transpose(jnp.broadcast_to(mine, (128, ROWS)))[:, 0:1]
    total = None
    y, k, group = ids_ref[0], ids_ref[1], ids_ref[3] // 4
    beside = jnp.where(y == 0, group + 15, group + 1) % 16
    for number in range(7):
        chip, line = k, y
        if number:
            chip = received((number - 1) % 3, k)
        if number > 3:
            line = y + jnp.where(chip < k, 1, -1)
        inside = inv_ref[pl.ds(jnp.clip(line, 0, 3) * 4 + chip, 1)]
        if number > 3:
            inside = jnp.where((line < 0) | (line > 3), edge_ref[pl.ds(beside, 1), pl.ds(chip, 1)][0], inside)
        column = lanes(inside[0])
        weight = expos[number][...] * (mine + column)
        if number == 0:
            row = lax.broadcasted_iota(jnp.int32, (ROWS, ROWS), 0) + shift
            weight = weight - jnp.where(partner_ref[...] == row, 2.0, 0.0)
        term = jnp.dot(weight.astype(jnp.bfloat16), blocks[number][...], preferred_element_type=jnp.float32)
        total = term if total is None else total + term
    out_ref[...] = total


def grad_call(shift, ids, inv, edge, row, partner, expos, blocks):
    shapes = [jax.ShapeDtypeStruct((ROWS, WIDTH), jnp.float32)]
    if not shift:
        shapes.append(jax.ShapeDtypeStruct((1, 1), jnp.float32))

    def kernel(*refs):
        grad_kernel(shift, *refs)

    return pl.pallas_call(
        kernel,
        out_shape=tuple(shapes),
        in_specs=smem(1) + vmem(18),
        out_specs=tuple(vmem(len(shapes))),
        compiler_params=PARAMS,
        cost_estimate=pl.CostEstimate(flops=2 * 7 * ROWS * ROWS * WIDTH, bytes_accessed=6 << 20, transcendentals=0),
        name="unit_gradient",
    )(ids, inv, edge, row, partner, *expos, *blocks)


def final_kernel(emb_ref, mine_ref, got_ref, out_ref):
    emb = emb_ref[...]
    norm = jnp.sqrt(jnp.sum(emb * emb, axis=1, keepdims=True) + 1e-06)
    unit32 = emb / norm
    unit_gradient = (mine_ref[...] + got_ref[...]) / SOFTMAX_TEMPER
    radial = jnp.sum(unit32 * unit_gradient, axis=1, keepdims=True)
    out_ref[...] = (unit_gradient - unit32 * radial) / norm


def final_call(emb, mine, got):
    return pl.pallas_call(
        final_kernel,
        out_shape=jax.ShapeDtypeStruct((ROWS, WIDTH), jnp.float32),
        in_specs=vmem(3),
        out_specs=pl.BlockSpec(memory_space=pltpu.VMEM),
        compiler_params=PARAMS,
        cost_estimate=pl.CostEstimate(flops=10 * ROWS * WIDTH, bytes_accessed=16 * ROWS * WIDTH, transcendentals=0),
        name="final",
    )(emb, mine, got)


def unit_kernel(emb_ref, unit_ref):
    emb = emb_ref[...]
    norm = jnp.sqrt(jnp.sum(emb * emb, axis=1, keepdims=True) + 1e-06)
    unit_ref[...] = (emb / norm).astype(jnp.bfloat16)


def unit_call(emb):
    return pl.pallas_call(
        unit_kernel,
        out_shape=jax.ShapeDtypeStruct((ROWS, WIDTH), jnp.bfloat16),
        in_specs=vmem(1),
        out_specs=pl.BlockSpec(memory_space=pltpu.VMEM),
        compiler_params=PARAMS,
        name="unit_rows",
    )(emb)


def send(value, name):
    return lax.ppermute(value, AXES, ROUTES[name])


def per_device(embeddings, partner):
    unit = unit_call(embeddings)

    run = lax.axis_index(("zh", "x", "y"))
    ids = jnp.stack([lax.axis_index(name) for name in DEV_AXES] + [run]).astype(jnp.int32)
    partner = partner.reshape(1, ROWS)

    p1b = send(unit, "P1b")
    x1 = send(unit, "X1")
    other = lax.ppermute(after(unit, ids), ("core",), [(0, 1), (1, 0)])
    local, e_own, e_other, sum_own, sum_other, pos = own_call(ids, unit, other, partner)
    expos, blocks, sums = [(e_own, e_other)] + [None] * 6, [unit] + [None] * 6, (sum_own, sum_other)

    def add(number, cands):
        nonlocal sums
        last = number == 5
        pair, rest, block = block_call(number, ids, unit, other, sums, cands, pos if last else None)
        expos[number + 1] = pair
        blocks[number + 1] = block
        if last:
            return rest
        sums = rest

    p1a = send(after(unit, sums[0]), "P1a")
    r2 = send(after(unit, p1a, p1b), "P2")
    r1 = choose_call(True, ids, p1a, p1b)
    y1 = send(r1, "Y1")
    x2 = send(after(x1, r1), "X2")
    x3 = send(r1, "X3")
    add(0, [r1])
    r2 = after(r2, sums[0])
    y2 = send(after(r2, y1), "Y2")
    p3b = send(after(unit, r2), "P3b")
    p3a = send(after(r1, r2), "P3a")
    x4 = send(after(r2, x3), "X4")
    x5 = send(choose_call(False, ids, x3, after(x2, r2)), "X5")
    add(1, [r2])
    p3a = after(p3a, sums[0])
    p3b = after(p3b, sums[0])
    y3a = send(after(p3a, y2), "Y3a")
    y3b = send(after(p3b, y2), "Y3b")
    add(2, [p3a, p3b])
    add(3, [y1, x2, x4])
    add(4, [y2, x3, x5])
    pay = add(5, [y3a, y3b, x1, x5])

    pays = lax.all_to_all(pay, DEV_AXES, 0, 0)
    inv, mine_inv, other_inv, post = denom_call(ids, pays)
    posts = lax.all_to_all(post, ("zh", "x"), 0, 0)
    (for_other,) = grad_call(ROWS, ids, inv, posts, other_inv, local, [e[1] for e in expos], blocks)
    got = lax.ppermute(for_other, ("core",), [(0, 1), (1, 0)])
    mine, loss = grad_call(0, ids, after(inv, for_other), posts, mine_inv, local, [e[0] for e in expos], blocks)
    grad = final_call(embeddings, mine, got)
    loss = loss.reshape(())
    return (loss, grad)


def solution(mesh):
    split = Mesh(mesh.devices.reshape(SHAPE), AXES)
    in_specs = (P(AXES, None), P(AXES))
    out_specs = (P(), P(AXES, None))
    return jax.shard_map(per_device, mesh=split, in_specs=in_specs, out_specs=out_specs, check_vma=False)
```

```python
import jax
import jax.numpy as jnp
from jax import lax
from jax.experimental import pallas as pl
from jax.experimental.pallas import tpu as pltpu
from jax.sharding import Mesh
from jax.sharding import PartitionSpec as P

ROUNDS = 6
SOFTMAX_TEMPER = 0.1
AXES = ("zh", "x", "y", "zl", "core")
SHAPE = (4, 4, 4, 4, 2)
RUNS = 64
DEV_AXES = ("y", "zl", "core")
ROWS = 224
WIDTH = 1024

def crosses(run):
    return run % 16 == 15


def routes():
    names = ("P1a", "P1b", "P2", "P3a", "P3b", "Y1", "Y2", "Y3a", "Y3b", "X1", "X2", "X3", "X4", "X5")
    table = {name: [] for name in names}

    def chip(run, k):
        return (run % RUNS) * 4 + k

    def add(name, *pairs, cores=(0, 1)):
        for source, target in pairs:
            for core in cores:
                table[name].append((2 * source + core, 2 * target + core))

    for run in range(RUNS):
        for name, moves in (
            ("P2", ((1, 3), (2, 0), (0, 1), (3, 2))),
            ("P3a", ((2, 3), (1, 0))),
            ("P3b", ((1, 2), (2, 1))),
        ):
            add(name, *((chip(run, a), chip(run, b)) for a, b in moves))
        for name, core in (("P1a", 0), ("P1b", 1)):
            add(name, *((chip(run, a), chip(run, b)) for a, b in ((0, 2), (1, 0), (2, 3), (3, 1))), cores=(core,))
        for name, ups, downs in (
            ("Y1", (0, 1), (2, 3)),
            ("Y2", (0, 2), (1, 3)),
            ("Y3a", (0,), (3,)),
            ("Y3b", (1,), (2,)),
        ):
            if not crosses(run):
                add(name, *((chip(run, k), chip(run + 1, k)) for k in ups))
            if not crosses(run - 1):
                add(name, *((chip(run, k), chip(run - 1, k)) for k in downs))
        if crosses(run):
            low = [chip(run, k) for k in range(4)]
            high = [chip(run + 1, k) for k in range(4)]
            for name in ("X1", "X3", "X4"):
                add(name, (low[3], high[0]), (high[0], low[3]))
            for name in ("X2", "X5"):
                add(name, (high[0], high[1]), (low[3], low[2]))
            add("X5", (high[1], high[2]), (low[2], low[1]))
    return table


ROUTES = routes()


def after(value, *others):
    return lax.optimization_barrier((value,) + others)[0]


def vmem(count):
    return [pl.BlockSpec(memory_space=pltpu.VMEM)] * count


def smem(count):
    return [pl.BlockSpec(memory_space=pltpu.SMEM)] * count


PARAMS = pltpu.CompilerParams(vmem_limit_bytes=12 * 1024 * 1024)


def scores(rows, columns):
    return lax.dot_general(rows, columns, (((1,), (1,)), ((), ())), preferred_element_type=jnp.float32)


def fold(values):
    tail = jnp.concatenate([values[:, 128:], jnp.zeros((ROWS, 256 - ROWS), jnp.float32)], axis=1)
    return values[:, :128] + tail


def own_kernel(ids_ref, unit_ref, other_ref, partner_ref, local_ref, e_own_ref, e_other_ref, sum_own_ref, sum_other_ref, pos_ref):
    unit = unit_ref[...]
    row = lax.broadcasted_iota(jnp.int32, (ROWS, ROWS), 0)
    column = lax.broadcasted_iota(jnp.int32, (ROWS, ROWS), 1)
    shift = ids_ref[2] * ROWS
    partner = partner_ref[...] - (ids_ref[3] * (8 * ROWS) + ids_ref[1] * (2 * ROWS) + shift)
    partner = jnp.where(partner < 0, partner + 2 * ROWS, partner)
    local_ref[...] = partner
    logits = scores(unit, unit) / SOFTMAX_TEMPER
    expo = jnp.where(row == column, 0.0, jnp.exp(logits - 1.0 / SOFTMAX_TEMPER))
    e_own_ref[...] = expo
    sum_own_ref[...] = fold(expo)
    picked = jnp.where(partner == row, logits, 0.0)
    logits = scores(other_ref[...], unit) / SOFTMAX_TEMPER
    expo = jnp.exp(logits - 1.0 / SOFTMAX_TEMPER)
    e_other_ref[...] = expo
    sum_other_ref[...] = fold(expo)
    picked = picked + jnp.where(partner == row + ROWS, logits, 0.0)
    pos_ref[...] = jnp.sum(fold(picked), axis=0, keepdims=True)


def own_call(ids, unit, other, partner):
    f32 = jnp.float32
    return pl.pallas_call(
        own_kernel,
        out_shape=(
            jax.ShapeDtypeStruct((1, ROWS), jnp.int32),
            jax.ShapeDtypeStruct((ROWS, ROWS), f32),
            jax.ShapeDtypeStruct((ROWS, ROWS), f32),
            jax.ShapeDtypeStruct((ROWS, 128), f32),
            jax.ShapeDtypeStruct((ROWS, 128), f32),
            jax.ShapeDtypeStruct((1, 128), f32),
        ),
        in_specs=smem(1) + vmem(3),
        out_specs=tuple(vmem(6)),
        compiler_params=PARAMS,
        cost_estimate=pl.CostEstimate(flops=2 * 448 * ROWS * WIDTH, bytes_accessed=2 << 20, transcendentals=448 * ROWS),
        name="own_scores",
    )(ids, unit, other, partner)


def received(number, k):
    first = jnp.where(k == 0, 1, jnp.where(k == 1, 3, jnp.where(k == 2, 0, 2)))
    return (first, 3 - first, 3 - k)[number]


def pick(number, ids_ref):
    k, run = ids_ref[1], ids_ref[3]
    below, above = run % 16 == 15, run % 16 == 0
    end = (below & (k == 3)) | (above & (k == 0))
    mid = (below & (k == 2)) | (above & (k == 1))
    far = (below & (k == 1)) | (above & (k == 2))
    inner = jnp.where((k == 1) | (k == 2), 1, 0)
    if number == 2:
        return inner
    if number == 3:
        return jnp.where(end, 2, jnp.where(mid, 1, 0))
    if number == 4:
        return jnp.where(end, 1, jnp.where(far, 2, 0))
    return jnp.where(end, 2, jnp.where(mid, 3, inner))


def block_kernel(number_in, n_cand, last, *refs):
    ids_ref, unit_ref, other_ref, sum_own_ref, sum_other_ref = refs[:5]
    cands = refs[5 : 5 + n_cand]
    rest = refs[5 + n_cand :]
    if last:
        pos_ref, rest = rest[0], rest[1:]
    e_own_ref, e_other_ref = rest[:2]
    rest = rest[2:]
    if last:
        pay_ref, rest = rest[0], rest[1:]
    else:
        sum_own_out, sum_other_out = rest[:2]
        rest = rest[2:]
    k, core = ids_ref[1], ids_ref[2]
    steps = received(number_in % 3, k) - k
    if number_in > 2:
        steps = jnp.where(steps < 0, steps + 4, steps - 4)
    outside = steps == jnp.where(core == 0, -3, 3)
    if n_cand > 1:
        choice = pick(number_in, ids_ref)
        block_ref, rest = rest[0], rest[1:]
        block_ref[...] = cands[0][...]
        for number in range(1, n_cand):

            @pl.when(choice == number)
            def _(number=number):
                block_ref[...] = cands[number][...]
    else:
        block_ref = cands[0]
    block = block_ref[...]
    expo = jnp.exp(scores(unit_ref[...], block) / SOFTMAX_TEMPER - 1.0 / SOFTMAX_TEMPER)
    e_own_ref[...] = expo
    sum_own = sum_own_ref[...] + fold(expo)
    expo = jnp.exp(scores(other_ref[...], block) / SOFTMAX_TEMPER - 1.0 / SOFTMAX_TEMPER)
    expo = jnp.where(outside, 0.0, expo)
    e_other_ref[...] = expo
    sum_other = sum_other_ref[...] + fold(expo)
    if last:
        positive = jnp.broadcast_to(jnp.sum(pos_ref[...], axis=1, keepdims=True), (1, 256 - ROWS))
        rows = []
        for total in (sum_own, sum_other):
            across = jnp.sum(jnp.transpose(total), axis=0, keepdims=True)
            rows += [across[:, :128], jnp.concatenate([across[:, 128:], positive], axis=1)]
        pay_ref[...] = jnp.broadcast_to(jnp.concatenate(rows, axis=0)[None], (32, 4, 128))
    else:
        sum_own_out[...] = sum_own
        sum_other_out[...] = sum_other


def block_call(number_in, ids, unit, other, sums, cands, pos=None):
    f32 = jnp.float32
    last = pos is not None
    n = len(cands)
    shapes = [jax.ShapeDtypeStruct((ROWS, ROWS), f32)] * 2
    if last:
        shapes.append(jax.ShapeDtypeStruct((32, 4, 128), f32))
    else:
        shapes += [jax.ShapeDtypeStruct((ROWS, 128), f32)] * 2
    if n > 1:
        shapes.append(jax.ShapeDtypeStruct((ROWS, WIDTH), jnp.bfloat16))
    operands = [unit, other, *sums, *cands] + ([pos] if last else [])

    def kernel(*refs):
        block_kernel(number_in, n, last, *refs)

    out = pl.pallas_call(
        kernel,
        out_shape=tuple(shapes),
        in_specs=smem(1) + vmem(len(operands)),
        out_specs=tuple(vmem(len(shapes))),
        compiler_params=PARAMS,
        cost_estimate=pl.CostEstimate(flops=2 * 448 * ROWS * WIDTH, bytes_accessed=2 << 20, transcendentals=448 * ROWS),
        name="block_scores",
    )(ids, *operands)
    block = out[-1] if n > 1 else cands[0]
    if last:
        return out[:2], out[2], block
    return out[:2], out[2:4], block


def choose_call(by_core, ids, first, second):
    def kernel(ids_ref, first_ref, second_ref, out_ref):
        is_first = ids_ref[2] == 0 if by_core else (ids_ref[1] == 0) | (ids_ref[1] == 3)

        @pl.when(is_first)
        def _():
            out_ref[...] = first_ref[...]

        @pl.when(jnp.logical_not(is_first))
        def _():
            out_ref[...] = second_ref[...]

    return pl.pallas_call(
        kernel,
        out_shape=jax.ShapeDtypeStruct((ROWS, WIDTH), jnp.bfloat16),
        in_specs=smem(1) + vmem(2),
        out_specs=pl.BlockSpec(memory_space=pltpu.VMEM),
        compiler_params=PARAMS,
        name="choose",
    )(ids, first, second)


def denom_kernel(ids_ref, pay_ref, inv_ref, mine_ref, other_ref, post_ref):
    y, k, core, group = ids_ref[0], ids_ref[1], ids_ref[2], ids_ref[3] // 4
    pay = pay_ref[...].reshape(16, 2, 4, 128)
    lane = lax.broadcasted_iota(jnp.int32, (16, 2, 128), 2)
    part = lax.broadcasted_iota(jnp.int32, (16, 2, 128), 1)
    real = part * 128 + lane < ROWS
    first = jnp.where(real, pay[:, 0, 0:2] + pay[:, 1, 2:4], 1.0)
    second = jnp.where(real, pay[:, 1, 0:2] + pay[:, 0, 2:4], 1.0)
    total = jnp.log(first) + jnp.log(second)
    total = jnp.sum(total.reshape(32, 128), axis=0, keepdims=True)
    last = lax.broadcasted_iota(jnp.int32, (1, 128), 1) == 127
    positive = jnp.sum(pay[:, :, 1].reshape(32, 128), axis=0, keepdims=True)
    total = jnp.sum(total - jnp.where(last, positive, 0.0), axis=1, keepdims=True)
    first, second = 1.0 / first, 1.0 / second
    inv = jnp.where(core == 0, first, second)
    other_all = jnp.where(core == 0, second, first)
    inv_ref[...] = inv
    here = lax.broadcasted_iota(jnp.int32, (16, 2, 128), 0) == y * 4 + k
    mine_ref[...] = jnp.sum(jnp.where(here, inv, 0.0), axis=0)
    other_ref[...] = jnp.sum(jnp.where(here, other_all, 0.0), axis=0)
    low = jnp.where(real[:4], inv[:4], total)
    high = jnp.where(real[:4], inv[12:], total)
    post_ref[...] = jnp.broadcast_to(low[None], (16, 4, 2, 128))
    post_ref[pl.ds((group + 1) % 16, 1)] = high[None]


def denom_call(ids, pay):
    f32 = jnp.float32
    return pl.pallas_call(
        denom_kernel,
        out_shape=(
            jax.ShapeDtypeStruct((16, 2, 128), f32),
            jax.ShapeDtypeStruct((2, 128), f32),
            jax.ShapeDtypeStruct((2, 128), f32),
            jax.ShapeDtypeStruct((16, 4, 2, 128), f32),
        ),
        in_specs=smem(1) + vmem(1),
        out_specs=tuple(vmem(4)),
        compiler_params=PARAMS,
        name="denoms",
    )(ids, pay)


def lanes(pair):
    return jnp.concatenate([pair[0:1, :], pair[1:2, : ROWS - 128]], axis=1)


def grad_kernel(shift, *refs):
    ids_ref, inv_ref, edge_ref, row_ref, partner_ref = refs[:5]
    expos, blocks = refs[5:12], refs[12:19]
    out_ref = refs[19]
    if not shift:
        posted = edge_ref[:, 0, 1, :]
        lane = lax.broadcasted_iota(jnp.int32, (16, 128), 1)
        total = jnp.sum(jnp.where(lane == 127, posted, 0.0), axis=0, keepdims=True)
        total = jnp.sum(total, axis=1, keepdims=True)
        refs[20][...] = total / (ROWS * 512) + 1.0 / SOFTMAX_TEMPER
    mine = lanes(row_ref[...])
    mine = jnp.transpose(jnp.broadcast_to(mine, (128, ROWS)))[:, 0:1]
    total = None
    y, k, group = ids_ref[0], ids_ref[1], ids_ref[3] // 4
    beside = jnp.where(y == 0, group + 15, group + 1) % 16
    for number in range(7):
        chip, line = k, y
        if number:
            chip = received((number - 1) % 3, k)
        if number > 3:
            line = y + jnp.where(chip < k, 1, -1)
        inside = inv_ref[pl.ds(jnp.clip(line, 0, 3) * 4 + chip, 1)]
        if number > 3:
            inside = jnp.where((line < 0) | (line > 3), edge_ref[pl.ds(beside, 1), pl.ds(chip, 1)][0], inside)
        column = lanes(inside[0])
        weight = expos[number][...] * (mine + column)
        if number == 0:
            row = lax.broadcasted_iota(jnp.int32, (ROWS, ROWS), 0) + shift
            weight = weight - jnp.where(partner_ref[...] == row, 2.0, 0.0)
        term = jnp.dot(weight.astype(jnp.bfloat16), blocks[number][...], preferred_element_type=jnp.float32)
        total = term if total is None else total + term
    out_ref[...] = total


def grad_call(shift, ids, inv, edge, row, partner, expos, blocks):
    shapes = [jax.ShapeDtypeStruct((ROWS, WIDTH), jnp.float32)]
    if not shift:
        shapes.append(jax.ShapeDtypeStruct((1, 1), jnp.float32))

    def kernel(*refs):
        grad_kernel(shift, *refs)

    return pl.pallas_call(
        kernel,
        out_shape=tuple(shapes),
        in_specs=smem(1) + vmem(18),
        out_specs=tuple(vmem(len(shapes))),
        compiler_params=PARAMS,
        cost_estimate=pl.CostEstimate(flops=2 * 7 * ROWS * ROWS * WIDTH, bytes_accessed=6 << 20, transcendentals=0),
        name="unit_gradient",
    )(ids, inv, edge, row, partner, *expos, *blocks)


def final_kernel(emb_ref, mine_ref, got_ref, out_ref):
    emb = emb_ref[...]
    norm = jnp.sqrt(jnp.sum(emb * emb, axis=1, keepdims=True) + 1e-06)
    unit32 = emb / norm
    unit_gradient = (mine_ref[...] + got_ref[...]) / SOFTMAX_TEMPER
    radial = jnp.sum(unit32 * unit_gradient, axis=1, keepdims=True)
    out_ref[...] = (unit_gradient - unit32 * radial) / norm


def final_call(emb, mine, got):
    return pl.pallas_call(
        final_kernel,
        out_shape=jax.ShapeDtypeStruct((ROWS, WIDTH), jnp.float32),
        in_specs=vmem(3),
        out_specs=pl.BlockSpec(memory_space=pltpu.VMEM),
        compiler_params=PARAMS,
        cost_estimate=pl.CostEstimate(flops=10 * ROWS * WIDTH, bytes_accessed=16 * ROWS * WIDTH, transcendentals=0),
        name="final",
    )(emb, mine, got)


def unit_kernel(emb_any, unit_ref, emb_ref, sems):
    copies = []
    for part in range(7):
        rows = pl.ds(part * 32, 32)
        copies.append(pltpu.make_async_copy(emb_any.at[rows], emb_ref.at[rows], sems.at[part]))
    for copy in copies:
        copy.start()
    for part, copy in enumerate(copies):
        rows = pl.ds(part * 32, 32)
        copy.wait()
        emb = emb_ref[rows, :]
        norm = jnp.sqrt(jnp.sum(emb * emb, axis=1, keepdims=True) + 1e-06)
        unit_ref[rows, :] = (emb / norm).astype(jnp.bfloat16)


def unit_call(emb):
    return pl.pallas_call(
        unit_kernel,
        out_shape=jax.ShapeDtypeStruct((ROWS, WIDTH), jnp.bfloat16),
        in_specs=[pl.BlockSpec(memory_space=pl.ANY)],
        out_specs=pl.BlockSpec(memory_space=pltpu.VMEM),
        scratch_shapes=[pltpu.VMEM((ROWS, WIDTH), jnp.float32), pltpu.SemaphoreType.DMA((7,))],
        compiler_params=pltpu.CompilerParams(vmem_limit_bytes=60 * 1024 * 1024),
        name="unit_rows",
    )(emb)


def send(value, name):
    return lax.ppermute(value, AXES, ROUTES[name])


def per_device(embeddings, partner):
    unit = unit_call(embeddings)

    run = lax.axis_index(("zh", "x", "y"))
    ids = jnp.stack([lax.axis_index(name) for name in DEV_AXES] + [run]).astype(jnp.int32)
    partner = partner.reshape(1, ROWS)

    p1b = send(unit, "P1b")
    x1 = send(unit, "X1")
    other = lax.ppermute(after(unit, ids), ("core",), [(0, 1), (1, 0)])
    local, e_own, e_other, sum_own, sum_other, pos = own_call(ids, unit, other, partner)
    expos, blocks, sums = [(e_own, e_other)] + [None] * 6, [unit] + [None] * 6, (sum_own, sum_other)

    def add(number, cands):
        nonlocal sums
        last = number == 5
        pair, rest, block = block_call(number, ids, unit, other, sums, cands, pos if last else None)
        expos[number + 1] = pair
        blocks[number + 1] = block
        if last:
            return rest
        sums = rest

    p1a = send(after(unit, sums[0]), "P1a")
    r2 = send(after(unit, p1a, p1b), "P2")
    r1 = choose_call(True, ids, p1a, p1b)
    y1 = send(r1, "Y1")
    x2 = send(after(x1, r1), "X2")
    x3 = send(r1, "X3")
    add(0, [r1])
    r2 = after(r2, sums[0])
    y2 = send(after(r2, y1), "Y2")
    p3b = send(after(unit, r2), "P3b")
    p3a = send(after(r1, r2), "P3a")
    x4 = send(after(r2, x3), "X4")
    x5 = send(choose_call(False, ids, x3, after(x2, r2)), "X5")
    add(1, [r2])
    p3a = after(p3a, sums[0])
    p3b = after(p3b, sums[0])
    y3a = send(after(p3a, y2), "Y3a")
    y3b = send(after(p3b, y2), "Y3b")
    add(2, [p3a, p3b])
    add(3, [y1, x2, x4])
    add(4, [y2, x3, x5])
    pay = add(5, [y3a, y3b, x1, x5])

    pays = lax.all_to_all(pay, DEV_AXES, 0, 0)
    inv, mine_inv, other_inv, post = denom_call(ids, pays)
    posts = lax.all_to_all(post, ("zh", "x"), 0, 0)
    (for_other,) = grad_call(ROWS, ids, inv, posts, other_inv, local, [e[1] for e in expos], blocks)
    got = lax.ppermute(for_other, ("core",), [(0, 1), (1, 0)])
    mine, loss = grad_call(0, ids, after(inv, for_other), posts, mine_inv, local, [e[0] for e in expos], blocks)
    grad = final_call(embeddings, mine, got)
    loss = loss.reshape(())
    return (loss, grad)


def solution(mesh):
    split = Mesh(mesh.devices.reshape(SHAPE), AXES)
    in_specs = (P(AXES, None), P(AXES))
    out_specs = (P(), P(AXES, None))
    return jax.shard_map(per_device, mesh=split, in_specs=in_specs, out_specs=out_specs, check_vma=False)
```
